32 devices in a mesh: tm: 4 (over y, x), gx: 8 (over z, core).
Axes of the slice: x: 2, y: 2, z: 4, core: 2. Of those that a mesh axis runs over, the one named last changes fastest.
Arguments:
- start_states: float32 [4, 128, 128, 128], P('tm', 'gx'), may hold values from -1.2 to 1.2
- mobility: float32 [128, 128, 128], P('gx'), may hold values from 0.25 to 1
Outputs:
- end_state: float32 [4, 128, 128, 128], P('tm', 'gx')
- next_start: float32 [4, 128, 128, 128], P('tm', 'gx')
The draws below stay inside these ranges and needn't reach their ends.
All inputs are finite; a program needn't handle non-finite values.
Results may differ from the reference program's by a relative error of at most 0.0001.
Values sent between devices are 32-bit elements; how exact they have to be, the bound alone decides.
No kernel may reach another device: no remote copies, remote signals or barrier semaphores. Data moves between devices by JAX's collectives and lax.ppermute only.
A program may use at most 128 MiB of HBM per device.

```python
import math
import jax
import jax.numpy as jnp
from jax import lax

NY = 128
NZ = 128
KY = 64
KZ = 64
ITERS = 2
NX = 128
SLICES = 4


def block_levels(stream_key, extent, shards, low, high):
    level = 1.0
    for dim, parts in shards:
        heights = jax.random.uniform(jax.random.fold_in(jax.random.fold_in(stream_key, 6), dim), (parts,), jnp.float32, low / len(shards), high / len(shards))
        level = level * jnp.repeat(jnp.exp(heights), extent[dim] // parts).reshape((-1,) + (1,) * (len(extent) - 1 - dim))
    return level


def setup_inputs(seed: int = 0) -> dict:
    arg_keys = jax.random.split(jax.random.key(seed), 3)
    start_states = jnp.clip(jax.random.uniform(arg_keys[0], (SLICES, NX, NY, NZ), jnp.float32, -1.2, 1.2) * block_levels(arg_keys[0], (SLICES, NX, NY, NZ), ((0, 4), (1, 8)), -0.4, 0.0), -1.2, 1.2)
    mobility = jnp.clip(jnp.exp(math.log(1.0) - 1.3862944 * jax.random.uniform(arg_keys[1], (NX, NY, NZ), jnp.float32) ** block_levels(arg_keys[1], (NX, NY, NZ), ((0, 8),), -0.2, 0.2)), 0.25, 1.0)
    return {"start_states": start_states, "mobility": mobility}


time_step = 0.05

def basis_value(node_times, source, point):
    total = 1.0
    for other in range(5):
        if other != source:
            total = total * (point - node_times[other]) / (node_times[source] - node_times[other])
    return total

def picard_table():
    root = math.sqrt(3.0 / 7.0)
    node_times = [0.0, (1.0 - root) / 2.0, 0.5, (1.0 + root) / 2.0, 1.0]
    gauss_points = [-math.sqrt(0.6), 0.0, math.sqrt(0.6)]
    gauss_weights = [5.0 / 9.0, 8.0 / 9.0, 5.0 / 9.0]
    picard_rows = []
    for target in range(1, 5):
        upper = node_times[target]
        row_values = []
        for source in range(5):
            integral = 0.0
            for point, weight in zip(gauss_points, gauss_weights):
                integral = integral + 0.5 * upper * weight * basis_value(node_times, source, 0.5 * upper * (1.0 + point))
            row_values.append(integral)
        picard_rows.append(row_values)
    return picard_rows

def dct_rows(count, kept):
    freq = jnp.arange(kept, dtype=jnp.float32)[:, None]
    place = jnp.arange(count, dtype=jnp.float32)[None, :]
    matrix = jnp.cos(jnp.pi * (place + 0.5) * freq / count) * jnp.sqrt(2.0 / count)
    return jnp.where(freq == 0, matrix * jnp.sqrt(0.5), matrix)

def project(values):
    low_y = dct_rows(NY, KY)
    low_z = dct_rows(NZ, KZ)
    hp = lax.Precision.HIGHEST
    coeffs = jnp.einsum('ky,...yz->...kz', low_y, values, precision=hp)
    coeffs = jnp.einsum('...kz,lz->...kl', coeffs, low_z, precision=hp)
    back = jnp.einsum('...kl,lz->...kz', coeffs, low_z, precision=hp)
    return jnp.einsum('ky,...kz->...yz', low_y, back, precision=hp)

def evaluate(fields, mobility):
    padded = jnp.pad(fields, ((0, 0), (1, 1), (1, 1), (1, 1)))
    values = padded[:, 1:-1, 1:-1, 1:-1]
    laplace = padded[:, 2:, 1:-1, 1:-1] + padded[:, :-2, 1:-1, 1:-1]
    laplace = laplace + padded[:, 1:-1, 2:, 1:-1] + padded[:, 1:-1, :-2, 1:-1]
    laplace = laplace + padded[:, 1:-1, 1:-1, 2:] + padded[:, 1:-1, 1:-1, :-2] - 6.0 * values
    return mobility * (laplace + values - values * values * values)

def reference(start_states, mobility):
    picard_rows = picard_table()

    def sweep(pair):
        start_value, nodes = pair
        fields = jnp.concatenate([start_value[None], nodes], axis=0)
        node_rates = evaluate(fields, mobility)
        updated = []
        for target in range(4):
            total = picard_rows[target][0] * node_rates[0]
            for source in range(1, 5):
                total = total + picard_rows[target][source] * node_rates[source]
            updated.append(start_value + time_step * total)
        return jnp.stack(updated, axis=0)
    start_value = start_states
    nodes = jnp.broadcast_to(start_states[:, None], (start_states.shape[0], 4) + start_states.shape[1:])
    end_value = start_states
    for iteration in range(ITERS):
        nodes = lax.map(sweep, (start_value, nodes))
        end_value = nodes[:, 3]
        arrived = jnp.concatenate([jnp.zeros_like(end_value[:1]), end_value[:-1]], axis=0)
        receive_mask = (jnp.arange(start_value.shape[0]) > 0).astype(jnp.float32)[:, None, None, None]
        start_value = start_value + receive_mask * lax.map(project, arrived - start_value)
    return (end_value, start_value)
```

```python
import functools
import math

import jax
import jax.numpy as jnp
import numpy as np
from jax import lax
from jax.experimental import pallas as pl
from jax.experimental.pallas import tpu as pltpu
from jax.sharding import PartitionSpec as P

KY = 64
KZ = 64
time_step = 0.05
F32 = jnp.float32
BF16 = jnp.bfloat16
VMEM_LIMIT = 24 * 2**20


def basis_value(node_times, source, point):
    total = 1.0
    for other in range(5):
        if other != source:
            total = total * (point - node_times[other]) / (node_times[source] - node_times[other])
    return total


def lobatto():
    root = math.sqrt(3.0 / 7.0)
    node_times = [0.0, (1.0 - root) / 2.0, 0.5, (1.0 + root) / 2.0, 1.0]
    gauss_points = [-math.sqrt(0.6), 0.0, math.sqrt(0.6)]
    gauss_weights = [5.0 / 9.0, 8.0 / 9.0, 5.0 / 9.0]
    last_row = []
    for source in range(5):
        integral = 0.0
        for point, weight in zip(gauss_points, gauss_weights):
            integral += 0.5 * weight * basis_value(node_times, source, 0.5 * (1.0 + point))
        last_row.append(integral)
    return node_times, last_row


NODE_TIMES, LAST_ROW = lobatto()
W = [sum(LAST_ROW[j] * NODE_TIMES[j] ** k for j in range(1, 5)) for k in range(4)]


def dct_rows(count, kept):
    freq = np.arange(kept, dtype=np.float64)[:, None]
    place = np.arange(count, dtype=np.float64)[None, :]
    matrix = np.cos(np.pi * (place + 0.5) * freq / count) * np.sqrt(2.0 / count)
    return np.where(freq == 0, matrix * np.sqrt(0.5), matrix)


def halves(matrix):
    high = matrix.astype(jnp.bfloat16)
    low = (matrix - high.astype(np.float64)).astype(jnp.bfloat16)
    return high, low


def tables(ny, nz):
    cy = dct_rows(ny, KY)
    cz = dct_rows(nz, KZ)
    twice = np.zeros((2 * nz, 2 * KZ))
    twice[:nz, :KZ] = cz.T
    twice[nz:, KZ:] = cz.T
    zh, zl = halves(twice)
    fz = np.concatenate([zh, zh, zl], axis=0)
    yh, yl = halves(cy)
    fy = np.concatenate([yh, yh, yl], axis=1)
    by = np.concatenate([yh.T, yh.T, yl.T], axis=1)
    bz = np.concatenate([zh.T, zh.T, zl.T], axis=0)
    return fz, fy, by, bz


def split(x):
    high = x.astype(BF16)
    return high, (x - high.astype(F32)).astype(BF16)


def dot(a, b):
    return jnp.dot(a, b, preferred_element_type=F32)


def neighbours(v):
    ny, nz = v.shape
    rows = lax.broadcasted_iota(jnp.int32, v.shape, 0)
    lanes = lax.broadcasted_iota(jnp.int32, v.shape, 1)
    total = jnp.where(rows == 0, 0.0, pltpu.roll(v, 1, 0))
    total = total + jnp.where(rows == ny - 1, 0.0, pltpu.roll(v, ny - 1, 0))
    total = total + jnp.where(lanes == 0, 0.0, pltpu.roll(v, 1, 1))
    return total + jnp.where(lanes == nz - 1, 0.0, pltpu.roll(v, nz - 1, 1))


def rate(below, v, above, mobility):
    return mobility * (neighbours(v) + (below + above) - v * (5.0 + v * v))


def analyse(pairs, fz_ref, fy_ref):
    rows = []
    for first, second in pairs:
        first_high, first_low = split(first)
        second_high, second_low = split(second)
        rows.append(
            jnp.concatenate([first_high, second_high, first_low, second_low, first_high, second_high], axis=1)
        )
    half = dot(jnp.concatenate(rows, axis=0), fz_ref[...])
    ny = pairs[0][0].shape[0]
    columns = []
    for i in range(len(pairs)):
        high, low = split(half[i * ny : (i + 1) * ny])
        columns.append(jnp.concatenate([high, low, high], axis=0))
    return dot(fy_ref[...], jnp.concatenate(columns, axis=1))


def synthesise(coeffs, by_ref, bz_ref):
    high, low = split(coeffs)
    half = dot(by_ref[...], jnp.concatenate([high, low, high], axis=0))
    width = 2 * KZ
    count = coeffs.shape[1] // width
    rows = []
    for i in range(count):
        high, low = split(half[:, i * width : (i + 1) * width])
        rows.append(jnp.concatenate([high, low, high], axis=1))
    planes = dot(jnp.concatenate(rows, axis=0), bz_ref[...])
    ny = half.shape[0]
    return [planes[i * ny : (i + 1) * ny] for i in range(count)]


def call(kernel, outs, name, flops=10**7, nbytes=10**6, scratch=(), specs=None, out_specs=None, aliases={}):
    def run(*args):
        return pl.pallas_call(
            kernel,
            out_shape=outs,
            in_specs=specs or [pl.BlockSpec(memory_space=pltpu.VMEM)] * len(args),
            out_specs=out_specs or jax.tree.map(lambda _: pl.BlockSpec(memory_space=pltpu.VMEM), outs),
            scratch_shapes=scratch,
            input_output_aliases=aliases,
            compiler_params=pltpu.CompilerParams(vmem_limit_bytes=VMEM_LIMIT),
            cost_estimate=pl.CostEstimate(flops=flops, bytes_accessed=nbytes, transcendentals=0),
            name=name,
        )(*args)

    return run


ANY = pl.BlockSpec(memory_space=pl.ANY)


def is_even():
    return lax.rem(lax.axis_index("gx"), 2) == 0


def pack_kernel(a_ref, mu_ref, even_ref, odd_ref, sems):
    nx = a_ref.shape[0]
    even = is_even()
    tail_a, tail_m = nx - 2, nx - 1
    copies = []
    for i, (out, is_tail) in enumerate([(even_ref, even), (odd_ref, jnp.logical_not(even))]):
        start = jnp.where(is_tail, tail_a, 0)
        plane = jnp.where(is_tail, tail_m, 0)
        copies.append(pltpu.make_async_copy(a_ref.at[pl.ds(start, 2)], out.at[pl.ds(0, 2)], sems.at[2 * i]))
        copies.append(pltpu.make_async_copy(mu_ref.at[pl.ds(plane, 1)], out.at[pl.ds(2, 1)], sems.at[2 * i + 1]))
    for copy in copies:
        copy.start()
    for copy in copies:
        copy.wait()


def inner_kernel(a_ref, mu_ref, fz_ref, fy_ref, g_ref, c_ref):
    nx = a_ref.shape[0]
    pairs = []
    for p in range(1, nx - 1, 2):
        pair = []
        for q in (p, p + 1):
            g = rate(a_ref[q - 1], a_ref[q], a_ref[q + 1], mu_ref[q])
            g_ref[q - 1] = g
            pair.append(a_ref[q] + time_step * g)
        pairs.append(pair)
    c_ref[...] = analyse(pairs, fz_ref, fy_ref)


def own_kernel(a_ref, fz_ref, fy_ref, c_ref):
    nx = a_ref.shape[0]
    c_ref[...] = analyse([(a_ref[p], a_ref[p + 1]) for p in range(1, nx - 1, 2)], fz_ref, fy_ref)


def outer_kernel(a_ref, mu_ref, even_ref, odd_ref, fz_ref, fy_ref, a_out, g_out, c_ref):
    nx = a_ref.shape[0]
    even = is_even()
    place = lax.axis_index("gx")
    count = lax.axis_size("gx")
    keep_low = (place > 0).astype(F32)
    keep_high = (place < count - 1).astype(F32)
    low = [jnp.where(even, odd_ref[i], even_ref[i]) * keep_low for i in range(3)]
    high = [jnp.where(even, even_ref[i], odd_ref[i]) * keep_high for i in range(3)]
    values = [low[0], low[1], a_ref[0], a_ref[1]]
    g_low = [
        rate(values[0], values[1], values[2], low[2]),
        rate(values[1], values[2], values[3], mu_ref[0]),
    ]
    ends = [a_ref[nx - 2], a_ref[nx - 1], high[0], high[1]]
    g_high = [
        rate(ends[0], ends[1], ends[2], mu_ref[nx - 1]),
        rate(ends[1], ends[2], ends[3], high[2]),
    ]
    for i, (v, g) in enumerate(zip(values[1:3] + ends[1:3], g_low + g_high)):
        a_out[i] = v
        g_out[i] = g
    pairs = [
        [v + time_step * g for v, g in zip(values[1:3], g_low)],
        [v + time_step * g for v, g in zip(ends[1:3], g_high)],
    ]
    c_ref[...] = analyse(pairs, fz_ref, fy_ref)


def later_kernel(a_ref, mu_ref, g_ref, ab_ref, gb_ref, fz_ref, fy_ref, acc_ref, c_ref):
    nx = a_ref.shape[0]
    h = time_step

    def plane(p):
        if p in (-1, 0):
            return gb_ref[p + 1]
        if p in (nx - 1, nx):
            return gb_ref[p - nx + 3]
        return g_ref[p - 1]

    c_ref[...] = analyse([(ab_ref[0], ab_ref[1]), (ab_ref[2], ab_ref[3])], fz_ref, fy_ref)
    for p in range(nx):
        g = plane(p)
        a = a_ref[p]
        laplace = neighbours(g) + (plane(p - 1) + plane(p + 1)) - 5.0 * g
        hg = h * g
        cube = hg * (3.0 * W[1] * a * a + hg * (3.0 * W[2] * a + W[3] * hg))
        acc_ref[p] = h * (W[0] * g + mu_ref[p] * (h * W[1] * laplace - cube))


def received(c, own):
    return jnp.where(lax.axis_index("tm") > 0, c - own, 0.0)


def second_inner_kernel(a_ref, mu_ref, acc_ref, c1_ref, own_ref, fz_ref, fy_ref, by_ref, bz_ref, a1_ref, e_ref, c2_ref):
    nx = a_ref.shape[0]
    nz = a_ref.shape[2]
    change = synthesise(received(c1_ref[...], own_ref[...]), by_ref, bz_ref)
    for p in range(1, nx - 1):
        i, k = (p - 1) // 2, (p - 1) % 2
        a1_ref[p - 1] = a_ref[p] + change[i][:, k * nz : (k + 1) * nz]
    pairs = []
    for p in range(2, nx - 2, 2):
        pair = []
        for q in (p, p + 1):
            v = a1_ref[q - 1]
            f = rate(a1_ref[q - 2], v, a1_ref[q], mu_ref[q])
            e = v + time_step * LAST_ROW[0] * f + acc_ref[q]
            e_ref[q - 2] = e
            pair.append(e)
        pairs.append(pair)
    c2_ref[...] = analyse(pairs, fz_ref, fy_ref)


def second_outer_kernel(
    ab_ref, mu_ref, acc_ref, a1_ref, c1_ref, own_ref, fz_ref, fy_ref, by_ref, bz_ref, a1b_ref, e_ref, c2_ref
):
    nx = mu_ref.shape[0]
    nz = mu_ref.shape[2]
    change = synthesise(received(c1_ref[...], own_ref[...]), by_ref, bz_ref)
    outer = [ab_ref[i] + change[i // 2][:, (i % 2) * nz : (i % 2 + 1) * nz] for i in range(4)]
    a1b_ref[0] = outer[1]
    a1b_ref[1] = outer[2]
    pairs = []
    for start, planes in (
        (0, [outer[0], outer[1], a1_ref[0], a1_ref[1]]),
        (nx - 2, [a1_ref[nx - 4], a1_ref[nx - 3], outer[2], outer[3]]),
    ):
        pair = []
        for k in range(2):
            q = start + k
            f = rate(planes[k], planes[k + 1], planes[k + 2], mu_ref[q])
            e = planes[k + 1] + time_step * LAST_ROW[0] * f + acc_ref[q]
            e_ref[2 * (start > 0) + k] = e
            pair.append(e)
        pairs.append(pair)
    c2_ref[...] = analyse(pairs, fz_ref, fy_ref)


def last_kernel(a1_ref, a1b_ref, c1_ref, c1b_ref, c2_ref, c2b_ref, by_ref, bz_ref, out_ref):
    nx = a1_ref.shape[0] + 2
    nz = a1_ref.shape[2]
    k = KZ
    c1 = c1_ref[...]
    c1b = c1b_ref[...]
    inner = received(c2_ref[...], c1[:, k : c1.shape[1] - k])
    ends = jnp.concatenate([c1b[:, k : 2 * k], c1[:, :k], c1[:, c1.shape[1] - k :], c1b[:, 2 * k : 3 * k]], axis=1)
    outer = received(c2b_ref[...], ends)
    change = synthesise(jnp.concatenate([inner, outer], axis=1), by_ref, bz_ref)
    for p in range(2, nx - 2):
        i, j = (p - 2) // 2, p % 2
        out_ref[0, p] = a1_ref[p - 1] + change[i][:, j * nz : (j + 1) * nz]
    last = (nx - 4) // 2
    out_ref[0, 0] = a1b_ref[0] + change[last][:, :nz]
    out_ref[0, 1] = a1_ref[0] + change[last][:, nz:]
    out_ref[0, nx - 2] = a1_ref[nx - 3] + change[last + 1][:, :nz]
    out_ref[0, nx - 1] = a1b_ref[1] + change[last + 1][:, nz:]


def join_kernel(inner_ref, outer_ref, out_ref, sems):
    nx = out_ref.shape[1]
    copies = [
        pltpu.make_async_copy(outer_ref.at[pl.ds(0, 2)], out_ref.at[0, pl.ds(0, 2)], sems.at[0]),
        pltpu.make_async_copy(outer_ref.at[pl.ds(2, 2)], out_ref.at[0, pl.ds(nx - 2, 2)], sems.at[1]),
    ]
    for i in range(2, nx - 2, 4):
        copies.append(
            pltpu.make_async_copy(inner_ref.at[pl.ds(i - 2, 4)], out_ref.at[0, pl.ds(i, 4)], sems.at[1 + i // 4 + 1])
        )
    for copy in copies:
        copy.start()
    for copy in copies:
        copy.wait()


def body(start_states, mobility):
    a = start_states[0]
    nx, ny, nz = a.shape
    slices, slabs = lax.axis_size("tm"), lax.axis_size("gx")
    fz, fy, by, bz = [jnp.asarray(t) for t in tables(ny, nz)]
    plane = functools.partial(jax.ShapeDtypeStruct, dtype=F32)
    inner = (nx - 2) // 2

    even_pairs = [(s * slabs + g, s * slabs + (g ^ 1)) for s in range(slices) for g in range(slabs)]
    odd_pairs = []
    for s in range(slices):
        for g in range(slabs):
            other = g + 1 if g % 2 else g - 1
            if 0 <= other < slabs:
                odd_pairs.append((s * slabs + g, s * slabs + other))
            else:
                odd_pairs.append((s * slabs + g, (s ^ 1) * slabs + g))
    ring = [(s, (s + 1) % slices) for s in range(slices)]

    to_even, to_odd = call(
        pack_kernel,
        [plane((3, ny, nz)), plane((3, ny, nz))],
        "pack",
        scratch=[pltpu.SemaphoreType.DMA((4,))],
        specs=[ANY, ANY],
        out_specs=[ANY, ANY],
    )(a, mobility)
    from_even = lax.ppermute(to_even, ("tm", "gx"), even_pairs)
    from_odd = lax.ppermute(to_odd, ("tm", "gx"), odd_pairs)
    g, c1 = call(inner_kernel, [plane((nx - 2, ny, nz)), plane((KY, inner * 2 * KZ))], "inner")(a, mobility, fz, fy)
    c1_in = lax.ppermute(c1, "tm", ring)
    own = call(own_kernel, plane((KY, inner * 2 * KZ)), "own")(a, fz, fy)
    ab, gb, c1b = call(
        outer_kernel, [plane((4, ny, nz)), plane((4, ny, nz)), plane((KY, 4 * KZ))], "outer"
    )(a, mobility, from_even, from_odd, fz, fy)
    c1b_in = lax.ppermute(c1b, "tm", ring)
    acc, own_b = call(later_kernel, [plane((nx, ny, nz)), plane((KY, 4 * KZ))], "later")(
        a, mobility, g, ab, gb, fz, fy
    )
    a1, e2, c2 = call(
        second_inner_kernel,
        [plane((nx - 2, ny, nz)), plane((nx - 4, ny, nz)), plane((KY, (inner - 1) * 2 * KZ))],
        "second_inner",
    )(a, mobility, acc, c1_in, own, fz, fy, by, bz)
    c2_in = lax.ppermute(c2, "tm", ring)
    a1b, e2b, c2b = call(
        second_outer_kernel,
        [plane((2, ny, nz)), plane((4, ny, nz)), plane((KY, 4 * KZ))],
        "second_outer",
    )(ab, mobility, acc, a1, c1b_in, own_b, fz, fy, by, bz)
    c2b_in = lax.ppermute(c2b, "tm", ring)
    end_state = call(
        join_kernel,
        plane((1, nx, ny, nz)),
        "join",
        scratch=[pltpu.SemaphoreType.DMA((2 + (nx - 4) // 4,))],
        specs=[ANY, ANY],
        out_specs=ANY,
    )(e2, e2b)
    next_start = call(last_kernel, plane((1, nx, ny, nz)), "last")(a1, a1b, c1_in, c1b_in, c2_in, c2b_in, by, bz)
    return end_state, next_start


def solution(mesh):
    placed = (P("tm", "gx", None, None), P("gx", None, None))
    return jax.shard_map(
        body,
        mesh=mesh,
        in_specs=placed,
        out_specs=(P("tm", "gx", None, None), P("tm", "gx", None, None)),
        check_vma=False,
    )
```

```python
import functools
import math

import jax
import jax.numpy as jnp
import numpy as np
from jax import lax
from jax.experimental import pallas as pl
from jax.experimental.pallas import tpu as pltpu
from jax.sharding import PartitionSpec as P

KY = 64
KZ = 64
time_step = 0.05
F32 = jnp.float32
BF16 = jnp.bfloat16
VMEM_LIMIT = 24 * 2**20


def basis_value(node_times, source, point):
    total = 1.0
    for other in range(5):
        if other != source:
            total = total * (point - node_times[other]) / (node_times[source] - node_times[other])
    return total


def lobatto():
    root = math.sqrt(3.0 / 7.0)
    node_times = [0.0, (1.0 - root) / 2.0, 0.5, (1.0 + root) / 2.0, 1.0]
    gauss_points = [-math.sqrt(0.6), 0.0, math.sqrt(0.6)]
    gauss_weights = [5.0 / 9.0, 8.0 / 9.0, 5.0 / 9.0]
    last_row = []
    for source in range(5):
        integral = 0.0
        for point, weight in zip(gauss_points, gauss_weights):
            integral += 0.5 * weight * basis_value(node_times, source, 0.5 * (1.0 + point))
        last_row.append(integral)
    return node_times, last_row


NODE_TIMES, LAST_ROW = lobatto()
W = [sum(LAST_ROW[j] * NODE_TIMES[j] ** k for j in range(1, 5)) for k in range(4)]


def dct_rows(count, kept):
    freq = np.arange(kept, dtype=np.float64)[:, None]
    place = np.arange(count, dtype=np.float64)[None, :]
    matrix = np.cos(np.pi * (place + 0.5) * freq / count) * np.sqrt(2.0 / count)
    return np.where(freq == 0, matrix * np.sqrt(0.5), matrix)


def halves(matrix):
    high = matrix.astype(jnp.bfloat16)
    low = (matrix - high.astype(np.float64)).astype(jnp.bfloat16)
    return high, low


def tables(ny, nz):
    cy = dct_rows(ny, KY)
    cz = dct_rows(nz, KZ)
    twice = np.zeros((2 * nz, 2 * KZ))
    twice[:nz, :KZ] = cz.T
    twice[nz:, KZ:] = cz.T
    zh, zl = halves(twice)
    fz = np.concatenate([zh, zh, zl], axis=0)
    yh, yl = halves(cy)
    fy = np.concatenate([yh, yh, yl], axis=1)
    by = np.concatenate([yh.T, yh.T, yl.T], axis=1)
    bz = np.concatenate([zh.T, zh.T, zl.T], axis=0)
    return fz, fy, by, bz


def split(x):
    high = x.astype(BF16)
    return high, (x - high.astype(F32)).astype(BF16)


def dot(a, b):
    return jnp.dot(a, b, preferred_element_type=F32)


def neighbours(v):
    ny, nz = v.shape
    rows = lax.broadcasted_iota(jnp.int32, v.shape, 0)
    lanes = lax.broadcasted_iota(jnp.int32, v.shape, 1)
    total = jnp.where(rows == 0, 0.0, pltpu.roll(v, 1, 0))
    total = total + jnp.where(rows == ny - 1, 0.0, pltpu.roll(v, ny - 1, 0))
    total = total + jnp.where(lanes == 0, 0.0, pltpu.roll(v, 1, 1))
    return total + jnp.where(lanes == nz - 1, 0.0, pltpu.roll(v, nz - 1, 1))


def rate(below, v, above, mobility):
    return mobility * (neighbours(v) + (below + above) - v * (5.0 + v * v))


def analyse(pairs, fz_ref, fy_ref):
    rows = []
    for first, second in pairs:
        first_high, first_low = split(first)
        second_high, second_low = split(second)
        rows.append(
            jnp.concatenate([first_high, second_high, first_low, second_low, first_high, second_high], axis=1)
        )
    half = dot(jnp.concatenate(rows, axis=0), fz_ref[...])
    ny = pairs[0][0].shape[0]
    columns = []
    for i in range(len(pairs)):
        high, low = split(half[i * ny : (i + 1) * ny])
        columns.append(jnp.concatenate([high, low, high], axis=0))
    return dot(fy_ref[...], jnp.concatenate(columns, axis=1))


def synthesise(coeffs, by_ref, bz_ref):
    high, low = split(coeffs)
    half = dot(by_ref[...], jnp.concatenate([high, low, high], axis=0))
    width = 2 * KZ
    count = coeffs.shape[1] // width
    rows = []
    for i in range(count):
        high, low = split(half[:, i * width : (i + 1) * width])
        rows.append(jnp.concatenate([high, low, high], axis=1))
    planes = dot(jnp.concatenate(rows, axis=0), bz_ref[...])
    ny = half.shape[0]
    return [planes[i * ny : (i + 1) * ny] for i in range(count)]


def call(kernel, outs, name, flops=10**7, nbytes=10**6, scratch=(), specs=None, out_specs=None, aliases={}):
    def run(*args):
        return pl.pallas_call(
            kernel,
            out_shape=outs,
            in_specs=specs or [pl.BlockSpec(memory_space=pltpu.VMEM)] * len(args),
            out_specs=out_specs or jax.tree.map(lambda _: pl.BlockSpec(memory_space=pltpu.VMEM), outs),
            scratch_shapes=scratch,
            input_output_aliases=aliases,
            compiler_params=pltpu.CompilerParams(vmem_limit_bytes=VMEM_LIMIT),
            cost_estimate=pl.CostEstimate(flops=flops, bytes_accessed=nbytes, transcendentals=0),
            name=name,
        )(*args)

    return run


ANY = pl.BlockSpec(memory_space=pl.ANY)


def is_even():
    return lax.rem(lax.axis_index("gx"), 2) == 0


def pack_kernel(a_ref, mu_ref, even_ref, odd_ref, sems):
    nx = a_ref.shape[0]
    even = is_even()
    tail_a, tail_m = nx - 2, nx - 1
    copies = []
    for i, (out, is_tail) in enumerate([(even_ref, even), (odd_ref, jnp.logical_not(even))]):
        start = jnp.where(is_tail, tail_a, 0)
        plane = jnp.where(is_tail, tail_m, 0)
        copies.append(pltpu.make_async_copy(a_ref.at[pl.ds(start, 2)], out.at[pl.ds(0, 2)], sems.at[2 * i]))
        copies.append(pltpu.make_async_copy(mu_ref.at[pl.ds(plane, 1)], out.at[pl.ds(2, 1)], sems.at[2 * i + 1]))
    for copy in copies:
        copy.start()
    for copy in copies:
        copy.wait()


def chunks(nx):
    last = nx // 2
    middle = (last + 1) // 2
    first = [list(range(1, middle + 1)), list(range(middle + 1, last)), [0, last]]
    second = [list(range(1, middle)), list(range(middle, last - 1)), [0, last - 1]]
    return first, second


def planes_of(pairs, shift):
    return [2 * t + shift + k for t in pairs for k in (0, 1)]


def fetch_kernel(a_in, mu_in, fz_in, fy_in, by_in, bz_in, after, a_ref, mu_ref, fz_ref, fy_ref, by_ref, bz_ref, g_ref, c_ref, sems):
    nx = a_ref.shape[0]
    pairs = chunks(nx)[0][0]
    planes = planes_of(pairs, -1)
    cut = (planes[-1] + 2 + 3) // 4 * 4
    early, late = [], []
    for start in range(0, nx, 4):
        for source, target in ((a_in, a_ref), (mu_in, mu_ref)):
            (early if start < cut else late).append((source.at[pl.ds(start, 4)], target.at[pl.ds(start, 4)]))
    early += [(fz_in, fz_ref), (fy_in, fy_ref)]
    late += [(by_in, by_ref), (bz_in, bz_ref)]
    copies = [pltpu.make_async_copy(s, t, sems.at[i]) for i, (s, t) in enumerate(early + late)]
    for copy in copies:
        copy.start()
    for copy in copies[: len(early)]:
        copy.wait()
    inner_chunk(a_ref, mu_ref, fz_ref, fy_ref, g_ref, c_ref, pairs)
    for copy in copies[len(early) :]:
        copy.wait()


def inner_chunk(a_ref, mu_ref, fz_ref, fy_ref, g_ref, c_ref, pairs):
    ends = []
    for i, p in enumerate(planes_of(pairs, -1)):
        g = rate(a_ref[p - 1], a_ref[p], a_ref[p + 1], mu_ref[p])
        g_ref[i] = g
        ends.append(a_ref[p] + time_step * g)
    c_ref[...] = analyse(list(zip(ends[::2], ends[1::2])), fz_ref, fy_ref)


def inner_kernel(a_ref, mu_ref, fz_ref, fy_ref, g_ref, c_ref):
    inner_chunk(a_ref, mu_ref, fz_ref, fy_ref, g_ref, c_ref, chunks(a_ref.shape[0])[0][1])


def own_kernel(a_ref, fz_ref, fy_ref, after, first_ref, second_ref):
    first, second, _ = chunks(a_ref.shape[0])[0]
    coeffs = analyse([(a_ref[p - 1], a_ref[p]) for p in planes_of(first + second, -1)[1::2]], fz_ref, fy_ref)
    first_ref[...] = coeffs[:, : first_ref.shape[1]]
    second_ref[...] = coeffs[:, first_ref.shape[1] :]


def outer_kernel(a_ref, mu_ref, even_ref, odd_ref, fz_ref, fy_ref, after, a_out, g_out, c_ref):
    nx = a_ref.shape[0]
    even = is_even()
    place = lax.axis_index("gx")
    count = lax.axis_size("gx")
    keep_low = (place > 0).astype(F32)
    keep_high = (place < count - 1).astype(F32)
    low = [jnp.where(even, odd_ref[i], even_ref[i]) * keep_low for i in range(3)]
    high = [jnp.where(even, even_ref[i], odd_ref[i]) * keep_high for i in range(3)]
    values = [low[0], low[1], a_ref[0], a_ref[1]]
    g_low = [
        rate(values[0], values[1], values[2], low[2]),
        rate(values[1], values[2], values[3], mu_ref[0]),
    ]
    ends = [a_ref[nx - 2], a_ref[nx - 1], high[0], high[1]]
    g_high = [
        rate(ends[0], ends[1], ends[2], mu_ref[nx - 1]),
        rate(ends[1], ends[2], ends[3], high[2]),
    ]
    for i, (v, g) in enumerate(zip(values[1:3] + ends[1:3], g_low + g_high)):
        a_out[i] = v
        g_out[i] = g
    pairs = [
        [v + time_step * g for v, g in zip(values[1:3], g_low)],
        [v + time_step * g for v, g in zip(ends[1:3], g_high)],
    ]
    c_ref[...] = analyse(pairs, fz_ref, fy_ref)


def plane_reader(refs, nx):
    where = {}
    for ref, pairs in zip(refs, chunks(nx)[0]):
        for i, p in enumerate(planes_of(pairs, -1)):
            where[p] = (ref, i)

    def read(p):
        ref, i = where[p]
        return ref[i]

    return read


def later_kernel(a_ref, mu_ref, g0_ref, g1_ref, g2_ref, ab_ref, fz_ref, fy_ref, acc_ref, c_ref):
    nx = a_ref.shape[0]
    h = time_step
    rates = plane_reader((g0_ref, g1_ref, g2_ref), nx)
    c_ref[...] = analyse([(ab_ref[0], ab_ref[1]), (ab_ref[2], ab_ref[3])], fz_ref, fy_ref)
    for p in range(nx):
        g = rates(p)
        a = a_ref[p]
        laplace = neighbours(g) + (rates(p - 1) + rates(p + 1)) - 5.0 * g
        hg = h * g
        cube = hg * (3.0 * W[1] * a * a + hg * (3.0 * W[2] * a + W[3] * hg))
        acc_ref[p] = h * (W[0] * g + mu_ref[p] * (h * W[1] * laplace - cube))


def received(c, own):
    return jnp.where(lax.axis_index("tm") > 0, c - own, 0.0)


def second_kernel(stage, *refs):
    a_ref, mu_ref, acc_ref, c1_ref, own_ref, fz_ref, fy_ref, by_ref, bz_ref = refs[:9]
    earlier, (a1_ref, e_ref, c2_ref) = refs[9:-3], refs[-3:]
    nx, ny, nz = mu_ref.shape
    first, second = chunks(nx)
    change = synthesise(received(c1_ref[...], own_ref[...]), by_ref, bz_ref)
    for i, p in enumerate(planes_of(first[stage], -1)):
        a = a_ref[i] if stage == 2 else a_ref[p]
        a1_ref[i] = a + change[i // 2][:, (i % 2) * nz : (i % 2 + 1) * nz]
    values = plane_reader((*earlier, a1_ref), nx)
    ends = []
    for i, p in enumerate(planes_of(second[stage], 0)):
        v = values(p)
        e = v + time_step * LAST_ROW[0] * rate(values(p - 1), v, values(p + 1), mu_ref[p]) + acc_ref[p]
        e_ref[i] = e
        ends.append(e)
    c2_ref[...] = analyse(list(zip(ends[::2], ends[1::2])), fz_ref, fy_ref)


def last_kernel(stages, *refs):
    count = len(stages)
    c2_refs, c1_refs, a1_refs = refs[:count], refs[count : count + 3], refs[count + 3 : count + 6]
    by_ref, bz_ref = refs[count + 6 : count + 8]
    out_ref, buffer, sems = refs[-3:]
    nx, ny, nz = out_ref.shape[1:]
    first, second = chunks(nx)
    where = {}
    for ref, pairs in zip(c1_refs, first):
        for i, p in enumerate(planes_of(pairs, -1)):
            where[p] = (ref, i)

    def column(p):
        ref, i = where[p]
        return ref[:, i * KZ : (i + 1) * KZ]

    values = plane_reader(a1_refs, nx)
    planes = [p for stage in stages for p in planes_of(second[stage], 0)]
    before = jnp.concatenate([column(p) for p in planes], axis=1)
    arrived = jnp.concatenate([ref[...] for ref in c2_refs], axis=1)
    change = synthesise(received(arrived, before), by_ref, bz_ref)
    copies = []
    for i in range(0, len(planes), 2):
        for k in (0, 1):
            buffer[i + k] = values(planes[i + k]) + change[i // 2][:, k * nz : (k + 1) * nz]
        copy = pltpu.make_async_copy(buffer.at[pl.ds(i, 2)], out_ref.at[0, pl.ds(planes[i], 2)], sems.at[i // 2])
        copy.start()
        copies.append(copy)
    for copy in copies:
        copy.wait()


def join_kernel(first_ref, second_ref, third_ref, out_ref, sems):
    nx = out_ref.shape[1]
    copies = []
    for ref, pairs in zip((first_ref, second_ref, third_ref), chunks(nx)[1]):
        for i, p in enumerate(planes_of(pairs, 0)[::2]):
            copies.append(
                pltpu.make_async_copy(ref.at[pl.ds(2 * i, 2)], out_ref.at[0, pl.ds(p, 2)], sems.at[len(copies)])
            )
    for copy in copies:
        copy.start()
    for copy in copies:
        copy.wait()


def body(start_states, mobility):
    a_in = start_states[0]
    nx, ny, nz = a_in.shape
    slices, slabs = lax.axis_size("tm"), lax.axis_size("gx")
    fz, fy, by, bz = [jnp.asarray(t) for t in tables(ny, nz)]
    like = functools.partial(jax.ShapeDtypeStruct, dtype=F32)
    first, second = chunks(nx)

    def grid(count):
        return like((count, ny, nz))

    def modes(pairs):
        return like((KY, len(pairs) * 2 * KZ))

    even_pairs = [(s * slabs + g, s * slabs + (g ^ 1)) for s in range(slices) for g in range(slabs)]
    odd_pairs = []
    for s in range(slices):
        for g in range(slabs):
            other = g + 1 if g % 2 else g - 1
            if 0 <= other < slabs:
                odd_pairs.append((s * slabs + g, s * slabs + other))
            else:
                odd_pairs.append((s * slabs + g, (s ^ 1) * slabs + g))
    ring = [(s, (s + 1) % slices) for s in range(slices)]

    def onward(c):
        return lax.ppermute(c, "tm", ring)

    to_even, to_odd = call(
        pack_kernel,
        [grid(3), grid(3)],
        "pack",
        scratch=[pltpu.SemaphoreType.DMA((4,))],
        specs=[ANY, ANY],
        out_specs=[ANY, ANY],
    )(a_in, mobility)
    from_odd = lax.ppermute(to_odd, ("tm", "gx"), odd_pairs)
    from_even = lax.ppermute(to_even, ("tm", "gx"), even_pairs)
    tables_like = [jax.ShapeDtypeStruct(t.shape, t.dtype) for t in (fz, fy, by, bz)]
    a, mu, fz, fy, by, bz, g0, c10 = call(
        fetch_kernel,
        [grid(nx), grid(nx), *tables_like, grid(2 * len(first[0])), modes(first[0])],
        "fetch",
        scratch=[pltpu.SemaphoreType.DMA((nx // 2 + 4,))],
        specs=[ANY] * 7,
    )(a_in, mobility, fz, fy, by, bz, to_odd)
    c10_in = onward(c10)
    g1, c11 = call(inner_kernel, [grid(2 * len(first[1])), modes(first[1])], "inner")(a, mu, fz, fy)
    c11_in = onward(c11)
    vmem = pl.BlockSpec(memory_space=pltpu.VMEM)
    own0, own1 = call(own_kernel, [modes(first[0]), modes(first[1])], "own", specs=[vmem] * 3 + [ANY])(a, fz, fy, g1)
    ab, g2, c12 = call(outer_kernel, [grid(4), grid(4), modes(first[2])], "outer", specs=[vmem] * 6 + [ANY])(
        a, mu, from_even, from_odd, fz, fy, own1
    )
    c12_in = onward(c12)
    acc, own2 = call(later_kernel, [grid(nx), modes(first[2])], "later")(a, mu, g0, g1, g2, ab, fz, fy)
    a1, e, c2_in = [], [], []
    for stage, (own, c1_in) in enumerate(zip((own0, own1, own2), (c10_in, c11_in, c12_in))):
        values, end, c2 = call(
            functools.partial(second_kernel, stage),
            [grid(2 * len(first[stage])), grid(2 * len(second[stage])), modes(second[stage])],
            "second",
        )(ab if stage == 2 else a, mu, acc, c1_in, own, fz, fy, by, bz, *a1)
        a1.append(values)
        e.append(end)
        c2_in.append(onward(c2))
    end_state = call(
        join_kernel,
        like((1, nx, ny, nz)),
        "join",
        scratch=[pltpu.SemaphoreType.DMA((nx // 2,))],
        specs=[ANY] * 3,
        out_specs=ANY,
    )(*e)
    c1_all = (c10_in, c11_in, c12_in)
    inner_planes = 2 * (len(second[0]) + len(second[1]))
    result = call(
        functools.partial(last_kernel, (0, 1)),
        like((1, nx, ny, nz)),
        "last_inner",
        scratch=[pltpu.VMEM((inner_planes, ny, nz), F32), pltpu.SemaphoreType.DMA((inner_planes // 2,))],
        out_specs=ANY,
    )(c2_in[0], c2_in[1], *c1_all, *a1, by, bz)
    next_start = call(
        functools.partial(last_kernel, (2,)),
        like((1, nx, ny, nz)),
        "last_outer",
        scratch=[pltpu.VMEM((4, ny, nz), F32), pltpu.SemaphoreType.DMA((2,))],
        specs=[vmem] * 9 + [ANY],
        out_specs=ANY,
        aliases={9: 0},
    )(c2_in[2], *c1_all, *a1, by, bz, result)
    return end_state, next_start


def solution(mesh):
    placed = (P("tm", "gx", None, None), P("gx", None, None))
    return jax.shard_map(
        body,
        mesh=mesh,
        in_specs=placed,
        out_specs=(P("tm", "gx", None, None), P("tm", "gx", None, None)),
        check_vma=False,
    )
```

```python
import functools
import math

import jax
import jax.numpy as jnp
import numpy as np
from jax import lax
from jax.experimental import pallas as pl
from jax.experimental.pallas import tpu as pltpu
from jax.sharding import PartitionSpec as P

KY = 64
KZ = 64
time_step = 0.05
F32 = jnp.float32
BF16 = jnp.bfloat16
VMEM_LIMIT = 24 * 2**20


def basis_value(node_times, source, point):
    total = 1.0
    for other in range(5):
        if other != source:
            total = total * (point - node_times[other]) / (node_times[source] - node_times[other])
    return total


def lobatto():
    root = math.sqrt(3.0 / 7.0)
    node_times = [0.0, (1.0 - root) / 2.0, 0.5, (1.0 + root) / 2.0, 1.0]
    gauss_points = [-math.sqrt(0.6), 0.0, math.sqrt(0.6)]
    gauss_weights = [5.0 / 9.0, 8.0 / 9.0, 5.0 / 9.0]
    last_row = []
    for source in range(5):
        integral = 0.0
        for point, weight in zip(gauss_points, gauss_weights):
            integral += 0.5 * weight * basis_value(node_times, source, 0.5 * (1.0 + point))
        last_row.append(integral)
    return node_times, last_row


NODE_TIMES, LAST_ROW = lobatto()
W = [sum(LAST_ROW[j] * NODE_TIMES[j] ** k for j in range(1, 5)) for k in range(4)]


def dct_rows(count, kept):
    freq = np.arange(kept, dtype=np.float64)[:, None]
    place = np.arange(count, dtype=np.float64)[None, :]
    matrix = np.cos(np.pi * (place + 0.5) * freq / count) * np.sqrt(2.0 / count)
    return np.where(freq == 0, matrix * np.sqrt(0.5), matrix)


def halves(matrix):
    high = matrix.astype(jnp.bfloat16)
    low = (matrix - high.astype(np.float64)).astype(jnp.bfloat16)
    return high, low


def tables(ny, nz):
    cy = dct_rows(ny, KY)
    cz = dct_rows(nz, KZ)
    twice = np.zeros((2 * nz, 2 * KZ))
    twice[:nz, :KZ] = cz.T
    twice[nz:, KZ:] = cz.T
    zh, zl = halves(twice)
    fz = np.concatenate([zh, zh, zl], axis=0)
    yh, yl = halves(cy)
    fy = np.concatenate([yh, yh, yl], axis=1)
    by = np.concatenate([yh.T, yh.T, yl.T], axis=1)
    bz = np.concatenate([zh.T, zh.T, zl.T], axis=0)
    return fz, fy, by, bz


def split(x):
    high = x.astype(BF16)
    return high, (x - high.astype(F32)).astype(BF16)


def dot(a, b):
    return jnp.dot(a, b, preferred_element_type=F32)


def neighbours(v):
    ny, nz = v.shape
    rows = lax.broadcasted_iota(jnp.int32, v.shape, 0)
    lanes = lax.broadcasted_iota(jnp.int32, v.shape, 1)
    total = jnp.where(rows == 0, 0.0, pltpu.roll(v, 1, 0))
    total = total + jnp.where(rows == ny - 1, 0.0, pltpu.roll(v, ny - 1, 0))
    total = total + jnp.where(lanes == 0, 0.0, pltpu.roll(v, 1, 1))
    return total + jnp.where(lanes == nz - 1, 0.0, pltpu.roll(v, nz - 1, 1))


def rate(below, v, above, mobility):
    return mobility * (neighbours(v) + (below + above) - v * (5.0 + v * v))


def analyse(pairs, fz_ref, fy_ref):
    rows = []
    for first, second in pairs:
        first_high, first_low = split(first)
        second_high, second_low = split(second)
        rows.append(
            jnp.concatenate([first_high, second_high, first_low, second_low, first_high, second_high], axis=1)
        )
    half = dot(jnp.concatenate(rows, axis=0), fz_ref[...])
    ny = pairs[0][0].shape[0]
    columns = []
    for i in range(len(pairs)):
        high, low = split(half[i * ny : (i + 1) * ny])
        columns.append(jnp.concatenate([high, low, high], axis=0))
    return dot(fy_ref[...], jnp.concatenate(columns, axis=1))


def synthesise(coeffs, by_ref, bz_ref):
    high, low = split(coeffs)
    half = dot(by_ref[...], jnp.concatenate([high, low, high], axis=0))
    width = 2 * KZ
    count = coeffs.shape[1] // width
    rows = []
    for i in range(count):
        high, low = split(half[:, i * width : (i + 1) * width])
        rows.append(jnp.concatenate([high, low, high], axis=1))
    planes = dot(jnp.concatenate(rows, axis=0), bz_ref[...])
    ny = half.shape[0]
    return [planes[i * ny : (i + 1) * ny] for i in range(count)]


def call(kernel, outs, name, flops=10**7, nbytes=10**6, scratch=(), specs=None, out_specs=None, aliases={}):
    def run(*args):
        return pl.pallas_call(
            kernel,
            out_shape=outs,
            in_specs=specs or [pl.BlockSpec(memory_space=pltpu.VMEM)] * len(args),
            out_specs=out_specs or jax.tree.map(lambda _: pl.BlockSpec(memory_space=pltpu.VMEM), outs),
            scratch_shapes=scratch,
            input_output_aliases=aliases,
            compiler_params=pltpu.CompilerParams(vmem_limit_bytes=VMEM_LIMIT),
            cost_estimate=pl.CostEstimate(flops=flops, bytes_accessed=nbytes, transcendentals=0),
            name=name,
        )(*args)

    return run


ANY = pl.BlockSpec(memory_space=pl.ANY)


def is_even():
    return lax.rem(lax.axis_index("gx"), 2) == 0


def pack_kernel(a_ref, mu_ref, even_ref, odd_ref, sems):
    nx = a_ref.shape[0]
    even = is_even()
    tail_a, tail_m = nx - 2, nx - 1
    copies = []
    for i, (out, is_tail) in enumerate([(even_ref, even), (odd_ref, jnp.logical_not(even))]):
        start = jnp.where(is_tail, tail_a, 0)
        plane = jnp.where(is_tail, tail_m, 0)
        copies.append(pltpu.make_async_copy(a_ref.at[pl.ds(start, 2)], out.at[pl.ds(0, 2)], sems.at[2 * i]))
        copies.append(pltpu.make_async_copy(mu_ref.at[pl.ds(plane, 1)], out.at[pl.ds(2, 1)], sems.at[2 * i + 1]))
    for copy in copies:
        copy.start()
    for copy in copies:
        copy.wait()


def chunks(nx):
    last = nx // 2
    middle = (last + 1) // 2
    first = [list(range(1, middle + 1)), list(range(middle + 1, last)), [0, last]]
    second = [list(range(1, middle)), list(range(middle, last - 1)), [0, last - 1]]
    return first, second


def planes_of(pairs, shift):
    return [2 * t + shift + k for t in pairs for k in (0, 1)]


def fetch_kernel(a_in, mu_in, fz_in, fy_in, by_in, bz_in, after, a_ref, mu_ref, fz_ref, fy_ref, by_ref, bz_ref, g_ref, c_ref, sems):
    nx = a_ref.shape[0]
    pairs = chunks(nx)[0][0]
    planes = planes_of(pairs, -1)
    cut = (planes[-1] + 2 + 3) // 4 * 4
    early, late = [], []
    for start in range(0, nx, 4):
        for source, target in ((a_in, a_ref), (mu_in, mu_ref)):
            (early if start < cut else late).append((source.at[pl.ds(start, 4)], target.at[pl.ds(start, 4)]))
    early += [(fz_in, fz_ref), (fy_in, fy_ref)]
    late += [(by_in, by_ref), (bz_in, bz_ref)]
    copies = [pltpu.make_async_copy(s, t, sems.at[i]) for i, (s, t) in enumerate(early + late)]
    for copy in copies:
        copy.start()
    for copy in copies[: len(early)]:
        copy.wait()
    inner_chunk(a_ref, mu_ref, fz_ref, fy_ref, g_ref, c_ref, pairs)
    for copy in copies[len(early) :]:
        copy.wait()


def inner_chunk(a_ref, mu_ref, fz_ref, fy_ref, g_ref, c_ref, pairs):
    ends = []
    for i, p in enumerate(planes_of(pairs, -1)):
        g = rate(a_ref[p - 1], a_ref[p], a_ref[p + 1], mu_ref[p])
        g_ref[i] = g
        ends.append(a_ref[p] + time_step * g)
    c_ref[...] = analyse(list(zip(ends[::2], ends[1::2])), fz_ref, fy_ref)


def inner_kernel(a_ref, mu_ref, fz_ref, fy_ref, g_ref, c_ref):
    inner_chunk(a_ref, mu_ref, fz_ref, fy_ref, g_ref, c_ref, chunks(a_ref.shape[0])[0][1])


def own_kernel(a_ref, fz_ref, fy_ref, after, first_ref, second_ref):
    first, second, _ = chunks(a_ref.shape[0])[0]
    coeffs = analyse([(a_ref[p - 1], a_ref[p]) for p in planes_of(first + second, -1)[1::2]], fz_ref, fy_ref)
    first_ref[...] = coeffs[:, : first_ref.shape[1]]
    second_ref[...] = coeffs[:, first_ref.shape[1] :]


def outer_kernel(a_ref, mu_ref, even_ref, odd_ref, fz_ref, fy_ref, after, a_out, g_out, c_ref):
    nx = a_ref.shape[0]
    even = is_even()
    place = lax.axis_index("gx")
    count = lax.axis_size("gx")
    keep_low = (place > 0).astype(F32)
    keep_high = (place < count - 1).astype(F32)
    low = [jnp.where(even, odd_ref[i], even_ref[i]) * keep_low for i in range(3)]
    high = [jnp.where(even, even_ref[i], odd_ref[i]) * keep_high for i in range(3)]
    values = [low[0], low[1], a_ref[0], a_ref[1]]
    g_low = [
        rate(values[0], values[1], values[2], low[2]),
        rate(values[1], values[2], values[3], mu_ref[0]),
    ]
    ends = [a_ref[nx - 2], a_ref[nx - 1], high[0], high[1]]
    g_high = [
        rate(ends[0], ends[1], ends[2], mu_ref[nx - 1]),
        rate(ends[1], ends[2], ends[3], high[2]),
    ]
    for i, (v, g) in enumerate(zip(values[1:3] + ends[1:3], g_low + g_high)):
        a_out[i] = v
        g_out[i] = g
    pairs = [
        [v + time_step * g for v, g in zip(values[1:3], g_low)],
        [v + time_step * g for v, g in zip(ends[1:3], g_high)],
    ]
    c_ref[...] = analyse(pairs, fz_ref, fy_ref)


def plane_reader(refs, nx):
    where = {}
    for ref, pairs in zip(refs, chunks(nx)[0]):
        for i, p in enumerate(planes_of(pairs, -1)):
            where[p] = (ref, i)

    def read(p):
        ref, i = where[p]
        return ref[i]

    return read


def later_kernel(a_ref, mu_ref, g0_ref, g1_ref, g2_ref, ab_ref, fz_ref, fy_ref, acc_ref, c_ref):
    nx = a_ref.shape[0]
    h = time_step
    rates = plane_reader((g0_ref, g1_ref, g2_ref), nx)
    c_ref[...] = analyse([(ab_ref[0], ab_ref[1]), (ab_ref[2], ab_ref[3])], fz_ref, fy_ref)
    for p in range(nx):
        g = rates(p)
        a = a_ref[p]
        laplace = neighbours(g) + (rates(p - 1) + rates(p + 1)) - 5.0 * g
        hg = h * g
        cube = hg * (3.0 * W[1] * a * a + hg * (3.0 * W[2] * a + W[3] * hg))
        acc_ref[p] = h * (W[0] * g + mu_ref[p] * (h * W[1] * laplace - cube))


def received(c, own):
    return jnp.where(lax.axis_index("tm") > 0, c - own, 0.0)


def second_kernel(stage, *refs):
    a_ref, mu_ref, acc_ref, c1_ref, own_ref, fz_ref, fy_ref, by_ref, bz_ref = refs[:9]
    earlier, (a1_ref, e_ref, c2_ref) = refs[9:-3], refs[-3:]
    nx, ny, nz = mu_ref.shape
    first, second = chunks(nx)
    change = synthesise(received(c1_ref[...], own_ref[...]), by_ref, bz_ref)
    for i, p in enumerate(planes_of(first[stage], -1)):
        a = a_ref[i] if stage == 2 else a_ref[p]
        a1_ref[i] = a + change[i // 2][:, (i % 2) * nz : (i % 2 + 1) * nz]
    values = plane_reader((*earlier, a1_ref), nx)
    ends = []
    for i, p in enumerate(planes_of(second[stage], 0)):
        v = values(p)
        e = v + time_step * LAST_ROW[0] * rate(values(p - 1), v, values(p + 1), mu_ref[p]) + acc_ref[p]
        e_ref[i] = e
        ends.append(e)
    c2_ref[...] = analyse(list(zip(ends[::2], ends[1::2])), fz_ref, fy_ref)


def last_kernel(stages, *refs):
    count = len(stages)
    c2_refs, c1_refs, a1_refs = refs[:count], refs[count : count + 3], refs[count + 3 : count + 6]
    by_ref, bz_ref = refs[count + 6 : count + 8]
    out_ref, buffer, sems = refs[-3:]
    nx, ny, nz = out_ref.shape[1:]
    first, second = chunks(nx)
    where = {}
    for ref, pairs in zip(c1_refs, first):
        for i, p in enumerate(planes_of(pairs, -1)):
            where[p] = (ref, i)

    def column(p):
        ref, i = where[p]
        return ref[:, i * KZ : (i + 1) * KZ]

    values = plane_reader(a1_refs, nx)
    planes = [p for stage in stages for p in planes_of(second[stage], 0)]
    before = jnp.concatenate([column(p) for p in planes], axis=1)
    arrived = jnp.concatenate([ref[...] for ref in c2_refs], axis=1)
    change = synthesise(received(arrived, before), by_ref, bz_ref)
    copies = []
    for i in range(0, len(planes), 2):
        for k in (0, 1):
            buffer[i + k] = values(planes[i + k]) + change[i // 2][:, k * nz : (k + 1) * nz]
        copy = pltpu.make_async_copy(buffer.at[pl.ds(i, 2)], out_ref.at[0, pl.ds(planes[i], 2)], sems.at[i // 2])
        copy.start()
        copies.append(copy)
    for copy in copies:
        copy.wait()


def join_kernel(first_ref, second_ref, third_ref, out_ref, sems):
    nx = out_ref.shape[1]
    copies = []
    for ref, pairs in zip((first_ref, second_ref, third_ref), chunks(nx)[1]):
        for i, p in enumerate(planes_of(pairs, 0)[::2]):
            copies.append(
                pltpu.make_async_copy(ref.at[pl.ds(2 * i, 2)], out_ref.at[0, pl.ds(p, 2)], sems.at[len(copies)])
            )
    for copy in copies:
        copy.start()
    for copy in copies:
        copy.wait()


def body(start_states, mobility):
    nx, ny, nz = mobility.shape
    a_in = pltpu.with_memory_space_constraint(start_states[0], pltpu.HBM)
    mobility = pltpu.with_memory_space_constraint(mobility, pltpu.HBM)
    slices, slabs = lax.axis_size("tm"), lax.axis_size("gx")
    fz, fy, by, bz = [pltpu.with_memory_space_constraint(jnp.asarray(t), pltpu.HBM) for t in tables(ny, nz)]
    like = functools.partial(jax.ShapeDtypeStruct, dtype=F32)
    first, second = chunks(nx)

    def grid(count):
        return like((count, ny, nz))

    def modes(pairs):
        return like((KY, len(pairs) * 2 * KZ))

    even_pairs = [(s * slabs + g, s * slabs + (g ^ 1)) for s in range(slices) for g in range(slabs)]
    odd_pairs = []
    for s in range(slices):
        for g in range(slabs):
            other = g + 1 if g % 2 else g - 1
            if 0 <= other < slabs:
                odd_pairs.append((s * slabs + g, s * slabs + other))
            else:
                odd_pairs.append((s * slabs + g, (s ^ 1) * slabs + g))
    ring = [(s, (s + 1) % slices) for s in range(slices)]

    def onward(c):
        return lax.ppermute(c, "tm", ring)

    to_even, to_odd = call(
        pack_kernel,
        [grid(3), grid(3)],
        "pack",
        scratch=[pltpu.SemaphoreType.DMA((4,))],
        specs=[ANY, ANY],
        out_specs=[ANY, ANY],
    )(a_in, mobility)
    from_odd = lax.ppermute(to_odd, ("tm", "gx"), odd_pairs)
    from_even = lax.ppermute(to_even, ("tm", "gx"), even_pairs)
    tables_like = [jax.ShapeDtypeStruct(t.shape, t.dtype) for t in (fz, fy, by, bz)]
    a, mu, fz, fy, by, bz, g0, c10 = call(
        fetch_kernel,
        [grid(nx), grid(nx), *tables_like, grid(2 * len(first[0])), modes(first[0])],
        "fetch",
        scratch=[pltpu.SemaphoreType.DMA((nx // 2 + 4,))],
        specs=[ANY] * 7,
    )(a_in, mobility, fz, fy, by, bz, to_odd)
    c10_in = onward(c10)
    g1, c11 = call(inner_kernel, [grid(2 * len(first[1])), modes(first[1])], "inner")(a, mu, fz, fy)
    c11_in = onward(c11)
    vmem = pl.BlockSpec(memory_space=pltpu.VMEM)
    own0, own1 = call(own_kernel, [modes(first[0]), modes(first[1])], "own", specs=[vmem] * 3 + [ANY])(a, fz, fy, g1)
    ab, g2, c12 = call(outer_kernel, [grid(4), grid(4), modes(first[2])], "outer", specs=[vmem] * 6 + [ANY])(
        a, mu, from_even, from_odd, fz, fy, own1
    )
    c12_in = onward(c12)
    acc, own2 = call(later_kernel, [grid(nx), modes(first[2])], "later")(a, mu, g0, g1, g2, ab, fz, fy)
    a1, e, c2_in = [], [], []
    for stage, (own, c1_in) in enumerate(zip((own0, own1, own2), (c10_in, c11_in, c12_in))):
        values, end, c2 = call(
            functools.partial(second_kernel, stage),
            [grid(2 * len(first[stage])), grid(2 * len(second[stage])), modes(second[stage])],
            "second",
        )(ab if stage == 2 else a, mu, acc, c1_in, own, fz, fy, by, bz, *a1)
        a1.append(values)
        e.append(end)
        c2_in.append(onward(c2))
    end_state = call(
        join_kernel,
        like((1, nx, ny, nz)),
        "join",
        scratch=[pltpu.SemaphoreType.DMA((nx // 2,))],
        specs=[ANY] * 3,
        out_specs=ANY,
    )(*e)
    c1_all = (c10_in, c11_in, c12_in)
    inner_planes = 2 * (len(second[0]) + len(second[1]))
    result = call(
        functools.partial(last_kernel, (0, 1)),
        like((1, nx, ny, nz)),
        "last_inner",
        scratch=[pltpu.VMEM((inner_planes, ny, nz), F32), pltpu.SemaphoreType.DMA((inner_planes // 2,))],
        out_specs=ANY,
    )(c2_in[0], c2_in[1], *c1_all, *a1, by, bz)
    next_start = call(
        functools.partial(last_kernel, (2,)),
        like((1, nx, ny, nz)),
        "last_outer",
        scratch=[pltpu.VMEM((4, ny, nz), F32), pltpu.SemaphoreType.DMA((2,))],
        specs=[vmem] * 9 + [ANY],
        out_specs=ANY,
        aliases={9: 0},
    )(c2_in[2], *c1_all, *a1, by, bz, result)
    return end_state, next_start


def solution(mesh):
    placed = (P("tm", "gx", None, None), P("gx", None, None))
    return jax.shard_map(
        body,
        mesh=mesh,
        in_specs=placed,
        out_specs=(P("tm", "gx", None, None), P("tm", "gx", None, None)),
        check_vma=False,
    )
```

```python
import functools
import math

import jax
import jax.numpy as jnp
import numpy as np
from jax import lax
from jax.experimental import pallas as pl
from jax.experimental.pallas import tpu as pltpu
from jax.sharding import PartitionSpec as P

KY = 64
KZ = 64
time_step = 0.05
F32 = jnp.float32
BF16 = jnp.bfloat16
VMEM_LIMIT = 24 * 2**20
COST = 10**8
ANY = pl.BlockSpec(memory_space=pl.ANY)
VMEM = pl.BlockSpec(memory_space=pltpu.VMEM)


def CUTS(last):
    return [last - 2]


def basis_value(node_times, source, point):
    total = 1.0
    for other in range(5):
        if other != source:
            total = total * (point - node_times[other]) / (node_times[source] - node_times[other])
    return total


def lobatto():
    root = math.sqrt(3.0 / 7.0)
    node_times = [0.0, (1.0 - root) / 2.0, 0.5, (1.0 + root) / 2.0, 1.0]
    gauss_points = [-math.sqrt(0.6), 0.0, math.sqrt(0.6)]
    gauss_weights = [5.0 / 9.0, 8.0 / 9.0, 5.0 / 9.0]
    last_row = []
    for source in range(5):
        integral = 0.0
        for point, weight in zip(gauss_points, gauss_weights):
            integral += 0.5 * weight * basis_value(node_times, source, 0.5 * (1.0 + point))
        last_row.append(integral)
    return node_times, last_row


NODE_TIMES, LAST_ROW = lobatto()
W = [sum(LAST_ROW[j] * NODE_TIMES[j] ** k for j in range(1, 5)) for k in range(4)]


def dct_rows(count, kept):
    freq = np.arange(kept, dtype=np.float64)[:, None]
    place = np.arange(count, dtype=np.float64)[None, :]
    matrix = np.cos(np.pi * (place + 0.5) * freq / count) * np.sqrt(2.0 / count)
    return np.where(freq == 0, matrix * np.sqrt(0.5), matrix)


def halves(matrix):
    high = matrix.astype(jnp.bfloat16)
    low = (matrix - high.astype(np.float64)).astype(jnp.bfloat16)
    return high, low


def tables(ny, nz):
    cy = dct_rows(ny, KY)
    cz = dct_rows(nz, KZ)
    twice = np.zeros((2 * nz, 2 * KZ))
    twice[:nz, :KZ] = cz.T
    twice[nz:, KZ:] = cz.T
    zh, zl = halves(twice)
    fz = np.concatenate([zh, zh, zl], axis=0)
    yh, yl = halves(cy)
    fy = np.concatenate([yh, yh, yl], axis=1)
    by = np.concatenate([yh.T, yh.T, yl.T], axis=1)
    bz = np.concatenate([zh.T, zh.T, zl.T], axis=0)
    return fz, fy, by, bz


def split(x):
    high = x.astype(BF16)
    return high, (x - high.astype(F32)).astype(BF16)


def dot(a, b):
    return jnp.dot(a, b, preferred_element_type=F32)


def neighbours(v):
    ny, nz = v.shape
    rows = lax.broadcasted_iota(jnp.int32, v.shape, 0)
    lanes = lax.broadcasted_iota(jnp.int32, v.shape, 1)
    total = jnp.where(rows == 0, 0.0, pltpu.roll(v, 1, 0))
    total = total + jnp.where(rows == ny - 1, 0.0, pltpu.roll(v, ny - 1, 0))
    total = total + jnp.where(lanes == 0, 0.0, pltpu.roll(v, 1, 1))
    return total + jnp.where(lanes == nz - 1, 0.0, pltpu.roll(v, nz - 1, 1))


def rate(below, v, above, mobility):
    return mobility * (neighbours(v) + (below + above) - v * (5.0 + v * v))


def analyse(pairs, fz_ref, fy_ref):
    rows = []
    for first, second in pairs:
        first_high, first_low = split(first)
        second_high, second_low = split(second)
        rows.append(
            jnp.concatenate([first_high, second_high, first_low, second_low, first_high, second_high], axis=1)
        )
    half = dot(jnp.concatenate(rows, axis=0), fz_ref[...])
    ny = pairs[0][0].shape[0]
    columns = []
    for i in range(len(pairs)):
        high, low = split(half[i * ny : (i + 1) * ny])
        columns.append(jnp.concatenate([high, low, high], axis=0))
    return dot(fy_ref[...], jnp.concatenate(columns, axis=1))


def synthesise(coeffs, by_ref, bz_ref):
    high, low = split(coeffs)
    half = dot(by_ref[...], jnp.concatenate([high, low, high], axis=0))
    width = 2 * KZ
    count = coeffs.shape[1] // width
    rows = []
    for i in range(count):
        high, low = split(half[:, i * width : (i + 1) * width])
        rows.append(jnp.concatenate([high, low, high], axis=1))
    planes = dot(jnp.concatenate(rows, axis=0), bz_ref[...])
    ny = half.shape[0]
    return [planes[i * ny : (i + 1) * ny] for i in range(count)]


def call(kernel, outs, name, scratch=(), specs=None, out_specs=None, aliases={}, cost=COST):
    def run(*args):
        return pl.pallas_call(
            kernel,
            out_shape=outs,
            in_specs=specs or [VMEM] * len(args),
            out_specs=out_specs or jax.tree.map(lambda _: VMEM, outs),
            scratch_shapes=scratch,
            input_output_aliases=aliases,
            compiler_params=pltpu.CompilerParams(vmem_limit_bytes=VMEM_LIMIT),
            cost_estimate=pl.CostEstimate(flops=100 * cost, bytes_accessed=10 * cost, transcendentals=0),
            name=name,
        )(*args)

    return run


def chunks(nx):
    last = nx // 2
    cuts = [1, *CUTS(last)]
    first = [list(range(cuts[i], cuts[i + 1])) for i in range(len(cuts) - 1)]
    second = [list(range(cuts[i] - (i > 0), cuts[i + 1] - 1)) for i in range(len(cuts) - 1)]
    first.append([0, *range(cuts[-1], last), last])
    second.append([0, *range(cuts[-1] - 1, last - 1), last - 1])
    return first, second


def planes_of(pairs, shift):
    return [2 * t + shift + k for t in pairs for k in (0, 1)]


def outer_planes(nx):
    return [-1, 0, nx - 1, nx]


def reader(*parts):
    where = {}
    for ref, planes in parts:
        for i, p in enumerate(planes):
            where[p] = (ref, i)

    def read(p):
        ref, i = where[p]
        return ref[i]

    return read


def by_pairs(planes):
    return list(zip(planes[::2], planes[1::2]))


def is_even():
    return lax.rem(lax.axis_index("gx"), 2) == 0


def fetch_kernel(a_in, mu_in, *refs):
    table_ins, (even_ref, odd_ref, a_ref, mu_ref), table_refs, sems = refs[:4], refs[4:8], refs[8:12], refs[12]
    nx = a_ref.shape[0]
    even = is_even()
    moves = []
    for out, is_tail in ((odd_ref, jnp.logical_not(even)), (even_ref, even)):
        moves.append((a_in.at[pl.ds(jnp.where(is_tail, nx - 2, 0), 2)], out.at[pl.ds(0, 2)]))
        moves.append((mu_in.at[pl.ds(jnp.where(is_tail, nx - 1, 0), 1)], out.at[pl.ds(2, 1)]))
    for start in range(0, nx, 4):
        moves.append((a_in.at[pl.ds(start, 4)], a_ref.at[pl.ds(start, 4)]))
        moves.append((mu_in.at[pl.ds(start, 4)], mu_ref.at[pl.ds(start, 4)]))
    moves += zip(table_ins, table_refs)
    copies = [pltpu.make_async_copy(s, t, sems.at[i]) for i, (s, t) in enumerate(moves)]
    for copy in copies:
        copy.start()
    for copy in copies:
        copy.wait()


def inner_kernel(stage, a_ref, mu_ref, fz_ref, fy_ref, g_ref, c_ref):
    ends = []
    for i, p in enumerate(planes_of(chunks(a_ref.shape[0])[0][stage], -1)):
        g = rate(a_ref[p - 1], a_ref[p], a_ref[p + 1], mu_ref[p])
        g_ref[i] = g
        ends.append(a_ref[p] + time_step * g)
    c_ref[...] = analyse(by_pairs(ends), fz_ref, fy_ref)


def later_part(below, g, above, a, mobility):
    h = time_step
    laplace = neighbours(g) + (below + above) - 5.0 * g
    hg = h * g
    cube = hg * (3.0 * W[1] * a * a + hg * (3.0 * W[2] * a + W[3] * hg))
    return h * (W[0] * g + mobility * (h * W[1] * laplace - cube))


def middle_kernel(a_ref, mu_ref, fz_ref, fy_ref, *refs):
    nx = a_ref.shape[0]
    first = chunks(nx)[0]
    early = [planes_of(part, -1) for part in first[:-1]]
    g_refs, (g_ref, acc_ref), own_refs = refs[: len(early)], refs[len(early) : len(early) + 2], refs[len(early) + 2 :]
    rest = planes_of(first[-1][1:-1], -1)
    for i, p in enumerate(rest):
        g_ref[i] = rate(a_ref[p - 1], a_ref[p], a_ref[p + 1], mu_ref[p])
    rates = reader(*zip(g_refs, early), (g_ref, rest))
    inner = sum(first[:-1], []) + first[-1][1:-1]
    coeffs = analyse([(a_ref[p - 1], a_ref[p]) for p in planes_of(inner, -1)[1::2]], fz_ref, fy_ref)
    start = 0
    for ref in own_refs:
        ref[...] = coeffs[:, start : start + ref.shape[1]]
        start += ref.shape[1]
    for p in range(2, nx - 2):
        acc_ref[p - 2] = later_part(rates(p - 1), rates(p), rates(p + 1), a_ref[p], mu_ref[p])


def outer_kernel(a_ref, mu_ref, even_ref, odd_ref, g_ref, fz_ref, fy_ref, after, a_out, g_out, c_ref):
    nx = a_ref.shape[0]
    even = is_even()
    place = lax.axis_index("gx")
    count = lax.axis_size("gx")
    keep_low = (place > 0).astype(F32)
    keep_high = (place < count - 1).astype(F32)
    low = [jnp.where(even, odd_ref[i], even_ref[i]) * keep_low for i in range(3)]
    high = [jnp.where(even, even_ref[i], odd_ref[i]) * keep_high for i in range(3)]
    starts = [low[0], low[1], a_ref[0], a_ref[1]]
    ends = [a_ref[nx - 2], a_ref[nx - 1], high[0], high[1]]
    values = starts[1:3] + ends[1:3]
    rates = [
        rate(starts[0], starts[1], starts[2], low[2]),
        rate(starts[1], starts[2], starts[3], mu_ref[0]),
        rate(ends[0], ends[1], ends[2], mu_ref[nx - 1]),
        rate(ends[1], ends[2], ends[3], high[2]),
    ]
    for i in range(4):
        a_out[i] = values[i]
        g_out[i] = rates[i]
    outer = [v + time_step * g for v, g in zip(values, rates)]
    rest = planes_of(chunks(nx)[0][-1][1:-1], -1)
    inner = [a_ref[p] + time_step * g_ref[i] for i, p in enumerate(rest)]
    c_ref[...] = analyse(by_pairs(outer[:2] + inner + outer[2:]), fz_ref, fy_ref)


def later_kernel(a_ref, mu_ref, ab_ref, gb_ref, low_ref, high_ref, rest_ref, fz_ref, fy_ref, acc_ref, c_ref):
    nx = a_ref.shape[0]
    first = chunks(nx)[0]
    rates = reader(
        (gb_ref, outer_planes(nx)), (low_ref, planes_of(first[0], -1)), (high_ref, planes_of(first[-1][1:-1], -1))
    )
    own = analyse([(ab_ref[0], ab_ref[1]), (ab_ref[2], ab_ref[3])], fz_ref, fy_ref)
    width = 2 * KZ
    c_ref[:, :width] = own[:, :width]
    c_ref[:, width : c_ref.shape[1] - width] = rest_ref[...]
    c_ref[:, c_ref.shape[1] - width :] = own[:, width:]
    for i, p in enumerate((0, 1, nx - 2, nx - 1)):
        acc_ref[i] = later_part(rates(p - 1), rates(p), rates(p + 1), a_ref[p], mu_ref[p])


def received(c, own):
    return jnp.where(lax.axis_index("tm") > 0, c - own, 0.0)


def second_kernel(stage, *refs):
    a_ref, ab_ref, mu_ref, acc_ref, accb_ref, c1_ref, own_ref, fz_ref, fy_ref, by_ref, bz_ref = refs[:11]
    earlier, (a1_ref, e_ref, c2_ref) = refs[11:-3], refs[-3:]
    nx, ny, nz = mu_ref.shape
    first, second = chunks(nx)
    change = synthesise(received(c1_ref[...], own_ref[...]), by_ref, bz_ref)
    before = reader((a_ref, range(nx)), (ab_ref, outer_planes(nx)))
    for i, p in enumerate(planes_of(first[stage], -1)):
        a1_ref[i] = before(p) + change[i // 2][:, (i % 2) * nz : (i % 2 + 1) * nz]
    values = reader(*[(ref, planes_of(part, -1)) for ref, part in zip((*earlier, a1_ref), first)])
    parts = reader((acc_ref, range(2, nx - 2)), (accb_ref, (0, 1, nx - 2, nx - 1)))
    ends = []
    for i, p in enumerate(planes_of(second[stage], 0)):
        v = values(p)
        e = v + time_step * LAST_ROW[0] * rate(values(p - 1), v, values(p + 1), mu_ref[p]) + parts(p)
        e_ref[i] = e
        ends.append(e)
    c2_ref[...] = analyse(by_pairs(ends), fz_ref, fy_ref)


def last_kernel(stage, count, *refs):
    c2_ref, by_ref, bz_ref = refs[:3]
    c1_refs, a1_refs = refs[3 : 3 + count], refs[3 + count : 3 + 2 * count]
    out_ref, buffer, sems = refs[-3:]
    nx, ny, nz = out_ref.shape[1:]
    first, second = chunks(nx)
    where = {}
    for ref, part in zip(c1_refs, first):
        for i, p in enumerate(planes_of(part, -1)):
            where[p] = (ref, i)

    def column(p):
        ref, i = where[p]
        return ref[:, i * KZ : (i + 1) * KZ]

    values = reader(*[(ref, planes_of(part, -1)) for ref, part in zip(a1_refs, first)])
    planes = planes_of(second[stage], 0)
    before = jnp.concatenate([column(p) for p in planes], axis=1)
    change = synthesise(received(c2_ref[...], before), by_ref, bz_ref)
    copies = []
    for i in range(0, len(planes), 2):
        for k in (0, 1):
            buffer[i + k] = values(planes[i + k]) + change[i // 2][:, k * nz : (k + 1) * nz]
        copy = pltpu.make_async_copy(buffer.at[pl.ds(i, 2)], out_ref.at[0, pl.ds(planes[i], 2)], sems.at[i // 2])
        copy.start()
        copies.append(copy)
    for copy in copies:
        copy.wait()


def join_kernel(*refs):
    parts, out_ref, sems = refs[:-2], refs[-2], refs[-1]
    copies = []
    for ref, part in zip(parts, chunks(out_ref.shape[1])[1]):
        for i, p in enumerate(planes_of(part, 0)[::2]):
            copies.append(
                pltpu.make_async_copy(ref.at[pl.ds(2 * i, 2)], out_ref.at[0, pl.ds(p, 2)], sems.at[len(copies)])
            )
    for copy in copies:
        copy.start()
    for copy in copies:
        copy.wait()


def body(start_states, mobility):
    nx, ny, nz = mobility.shape
    slices, slabs = lax.axis_size("tm"), lax.axis_size("gx")
    inputs = [start_states[0], mobility, *map(jnp.asarray, tables(ny, nz))]
    inputs = [pltpu.with_memory_space_constraint(x, pltpu.HBM) for x in inputs]
    first, second = chunks(nx)
    count = len(first)

    def grid(planes):
        return jax.ShapeDtypeStruct((planes, ny, nz), F32)

    def modes(pairs):
        return jax.ShapeDtypeStruct((KY, len(pairs) * 2 * KZ), F32)

    even_pairs = [(s * slabs + g, s * slabs + (g ^ 1)) for s in range(slices) for g in range(slabs)]
    odd_pairs = []
    for s in range(slices):
        for g in range(slabs):
            other = g + 1 if g % 2 else g - 1
            if 0 <= other < slabs:
                odd_pairs.append((s * slabs + g, s * slabs + other))
            else:
                odd_pairs.append((s * slabs + g, (s ^ 1) * slabs + g))
    ring = [(s, (s + 1) % slices) for s in range(slices)]

    def onward(c):
        return lax.ppermute(c, "tm", ring)

    to_even, to_odd, a, mu, fz, fy, by, bz = call(
        fetch_kernel,
        [grid(3), grid(3), grid(nx), grid(nx), *[jax.ShapeDtypeStruct(t.shape, t.dtype) for t in inputs[2:]]],
        "fetch",
        scratch=[pltpu.SemaphoreType.DMA((8 + nx // 2,))],
        specs=[ANY] * 6,
    )(*inputs)
    from_odd = lax.ppermute(to_odd, ("tm", "gx"), odd_pairs)
    from_even = lax.ppermute(to_even, ("tm", "gx"), even_pairs)
    g, c1 = [], []
    for stage, part in enumerate(first[:-1]):
        rates, c = call(functools.partial(inner_kernel, stage), [grid(2 * len(part)), modes(part)], "inner")(
            a, mu, fz, fy
        )
        g.append(rates)
        c1.append(onward(c))
    rest = first[-1][1:-1]
    g_rest, acc, *own, own_rest = call(
        middle_kernel,
        [grid(2 * len(rest)), grid(nx - 4), *[modes(part) for part in first[:-1]], modes(rest)],
        "middle",
        cost=0,
    )(a, mu, fz, fy, *g)
    ab, gb, c = call(outer_kernel, [grid(4), grid(4), modes(first[-1])], "outer", specs=[VMEM] * 7 + [ANY])(
        a, mu, from_even, from_odd, g_rest, fz, fy, acc
    )
    c1.append(onward(c))
    accb, own_last = call(later_kernel, [grid(4), modes(first[-1])], "later")(
        a, mu, ab, gb, g[0], g_rest, own_rest, fz, fy
    )
    own.append(own_last)
    a1, e, c2 = [], [], []
    for stage in range(count):
        values, end, c = call(
            functools.partial(second_kernel, stage),
            [grid(2 * len(first[stage])), grid(2 * len(second[stage])), modes(second[stage])],
            "second",
        )(a, ab, mu, acc, accb, c1[stage], own[stage], fz, fy, by, bz, *a1)
        a1.append(values)
        e.append(end)
        c2.append(onward(c))
    whole = jax.ShapeDtypeStruct((1, nx, ny, nz), F32)
    end_state = call(
        join_kernel,
        whole,
        "join",
        scratch=[pltpu.SemaphoreType.DMA((nx // 2,))],
        specs=[ANY] * count,
        out_specs=ANY,
    )(*e)
    result = []
    for stage, part in enumerate(second):
        result = [
            call(
                functools.partial(last_kernel, stage, count),
                whole,
                "last",
                scratch=[pltpu.VMEM((2 * len(part), ny, nz), F32), pltpu.SemaphoreType.DMA((len(part),))],
                specs=[VMEM] * (3 + 2 * count) + [ANY] * len(result),
                out_specs=ANY,
                aliases={3 + 2 * count: 0} if result else {},
            )(c2[stage], by, bz, *c1, *a1, *result)
        ]
    return end_state, result[0]


def solution(mesh):
    placed = (P("tm", "gx", None, None), P("gx", None, None))
    return jax.shard_map(
        body,
        mesh=mesh,
        in_specs=placed,
        out_specs=(P("tm", "gx", None, None), P("tm", "gx", None, None)),
        check_vma=False,
    )
```

```python
import functools
import math

import jax
import jax.numpy as jnp
import numpy as np
from jax import lax
from jax.experimental import pallas as pl
from jax.experimental.pallas import tpu as pltpu
from jax.sharding import PartitionSpec as P

KY = 64
KZ = 64
time_step = 0.05
F32 = jnp.float32
BF16 = jnp.bfloat16
VMEM_LIMIT = 24 * 2**20
COST = 10**8
ANY = pl.BlockSpec(memory_space=pl.ANY)
VMEM = pl.BlockSpec(memory_space=pltpu.VMEM)


def CUTS(last):
    return [last - 2]


def basis_value(node_times, source, point):
    total = 1.0
    for other in range(5):
        if other != source:
            total = total * (point - node_times[other]) / (node_times[source] - node_times[other])
    return total


def lobatto():
    root = math.sqrt(3.0 / 7.0)
    node_times = [0.0, (1.0 - root) / 2.0, 0.5, (1.0 + root) / 2.0, 1.0]
    gauss_points = [-math.sqrt(0.6), 0.0, math.sqrt(0.6)]
    gauss_weights = [5.0 / 9.0, 8.0 / 9.0, 5.0 / 9.0]
    last_row = []
    for source in range(5):
        integral = 0.0
        for point, weight in zip(gauss_points, gauss_weights):
            integral += 0.5 * weight * basis_value(node_times, source, 0.5 * (1.0 + point))
        last_row.append(integral)
    return node_times, last_row


NODE_TIMES, LAST_ROW = lobatto()
W = [sum(LAST_ROW[j] * NODE_TIMES[j] ** k for j in range(1, 5)) for k in range(4)]


def dct_rows(count, kept):
    freq = np.arange(kept, dtype=np.float64)[:, None]
    place = np.arange(count, dtype=np.float64)[None, :]
    matrix = np.cos(np.pi * (place + 0.5) * freq / count) * np.sqrt(2.0 / count)
    return np.where(freq == 0, matrix * np.sqrt(0.5), matrix)


def halves(matrix):
    high = matrix.astype(jnp.bfloat16)
    low = (matrix - high.astype(np.float64)).astype(jnp.bfloat16)
    return high, low


def tables(ny, nz):
    cy = dct_rows(ny, KY)
    cz = dct_rows(nz, KZ)
    twice = np.zeros((2 * nz, 2 * KZ))
    twice[:nz, :KZ] = cz.T
    twice[nz:, KZ:] = cz.T
    zh, zl = halves(twice)
    fz = np.concatenate([zh, zh, zl], axis=0)
    yh, yl = halves(cy)
    fy = np.concatenate([yh, yh, yl], axis=1)
    by = np.concatenate([yh.T, yh.T, yl.T], axis=1)
    bz = np.concatenate([zh.T, zh.T, zl.T], axis=0)
    return fz, fy, by, bz


def split(x):
    high = x.astype(BF16)
    return high, (x - high.astype(F32)).astype(BF16)


def dot(a, b):
    return jnp.dot(a, b, preferred_element_type=F32)


def neighbours(v):
    ny, nz = v.shape
    rows = lax.broadcasted_iota(jnp.int32, v.shape, 0)
    lanes = lax.broadcasted_iota(jnp.int32, v.shape, 1)
    total = jnp.where(rows == 0, 0.0, pltpu.roll(v, 1, 0))
    total = total + jnp.where(rows == ny - 1, 0.0, pltpu.roll(v, ny - 1, 0))
    total = total + jnp.where(lanes == 0, 0.0, pltpu.roll(v, 1, 1))
    return total + jnp.where(lanes == nz - 1, 0.0, pltpu.roll(v, nz - 1, 1))


def rate(below, v, above, mobility):
    return mobility * (neighbours(v) + (below + above) - v * (5.0 + v * v))


def analyse(pairs, fz_ref, fy_ref):
    rows = []
    for first, second in pairs:
        first_high, first_low = split(first)
        second_high, second_low = split(second)
        rows.append(
            jnp.concatenate([first_high, second_high, first_low, second_low, first_high, second_high], axis=1)
        )
    half = dot(jnp.concatenate(rows, axis=0), fz_ref[...])
    ny = pairs[0][0].shape[0]
    columns = []
    for i in range(len(pairs)):
        high, low = split(half[i * ny : (i + 1) * ny])
        columns.append(jnp.concatenate([high, low, high], axis=0))
    return dot(fy_ref[...], jnp.concatenate(columns, axis=1))


def synthesise(coeffs, by_ref, bz_ref):
    high, low = split(coeffs)
    half = dot(by_ref[...], jnp.concatenate([high, low, high], axis=0))
    width = 2 * KZ
    count = coeffs.shape[1] // width
    rows = []
    for i in range(count):
        high, low = split(half[:, i * width : (i + 1) * width])
        rows.append(jnp.concatenate([high, low, high], axis=1))
    planes = dot(jnp.concatenate(rows, axis=0), bz_ref[...])
    ny = half.shape[0]
    return [planes[i * ny : (i + 1) * ny] for i in range(count)]


def call(kernel, outs, name, scratch=(), specs=None, out_specs=None, aliases={}, cost=COST):
    def run(*args):
        return pl.pallas_call(
            kernel,
            out_shape=outs,
            in_specs=specs or [VMEM] * len(args),
            out_specs=out_specs or jax.tree.map(lambda _: VMEM, outs),
            scratch_shapes=scratch,
            input_output_aliases=aliases,
            compiler_params=pltpu.CompilerParams(vmem_limit_bytes=VMEM_LIMIT),
            cost_estimate=pl.CostEstimate(flops=100 * cost, bytes_accessed=10 * cost, transcendentals=0),
            name=name,
        )(*args)

    return run


def chunks(nx):
    last = nx // 2
    cuts = [1, *CUTS(last)]
    first = [list(range(cuts[i], cuts[i + 1])) for i in range(len(cuts) - 1)]
    second = [list(range(cuts[i] - (i > 0), cuts[i + 1] - 1)) for i in range(len(cuts) - 1)]
    first.append([0, *range(cuts[-1], last), last])
    second.append([0, *range(cuts[-1] - 1, last - 1), last - 1])
    return first, second


def planes_of(pairs, shift):
    return [2 * t + shift + k for t in pairs for k in (0, 1)]


def outer_planes(nx):
    return [-1, 0, nx - 1, nx]


def reader(*parts):
    where = {}
    for ref, planes in parts:
        for i, p in enumerate(planes):
            where[p] = (ref, i)

    def read(p):
        ref, i = where[p]
        return ref[i]

    return read


def by_pairs(planes):
    return list(zip(planes[::2], planes[1::2]))


def is_even():
    return lax.rem(lax.axis_index("gx"), 2) == 0


def pack_kernel(a_ref, mu_ref, odd_ref, sems):
    nx = a_ref.shape[0]
    even = is_even()
    copies = [
        pltpu.make_async_copy(a_ref.at[pl.ds(jnp.where(even, 0, nx - 2), 2)], odd_ref.at[pl.ds(0, 2)], sems.at[0]),
        pltpu.make_async_copy(mu_ref.at[pl.ds(jnp.where(even, 0, nx - 1), 1)], odd_ref.at[pl.ds(2, 1)], sems.at[1]),
    ]
    for copy in copies:
        copy.start()
    for copy in copies:
        copy.wait()


def inner_kernel(stage, a_ref, mu_ref, fz_ref, fy_ref, after, g_ref, c_ref, *even_ref):
    ends = []
    for i, p in enumerate(planes_of(chunks(a_ref.shape[0])[0][stage], -1)):
        g = rate(a_ref[p - 1], a_ref[p], a_ref[p + 1], mu_ref[p])
        g_ref[i] = g
        ends.append(a_ref[p] + time_step * g)
    c_ref[...] = analyse(by_pairs(ends), fz_ref, fy_ref)
    if stage == 0:
        nx = a_ref.shape[0]
        even = is_even()
        even_ref[0][0] = jnp.where(even, a_ref[nx - 2], a_ref[0])
        even_ref[0][1] = jnp.where(even, a_ref[nx - 1], a_ref[1])
        even_ref[0][2] = jnp.where(even, mu_ref[nx - 1], mu_ref[0])


def later_part(below, g, above, a, mobility):
    h = time_step
    laplace = neighbours(g) + (below + above) - 5.0 * g
    hg = h * g
    cube = hg * (3.0 * W[1] * a * a + hg * (3.0 * W[2] * a + W[3] * hg))
    return h * (W[0] * g + mobility * (h * W[1] * laplace - cube))


def middle_kernel(a_ref, mu_ref, fz_ref, fy_ref, *refs):
    nx = a_ref.shape[0]
    first = chunks(nx)[0]
    early = [planes_of(part, -1) for part in first[:-1]]
    g_refs, (g_ref, acc_ref), own_refs = refs[: len(early)], refs[len(early) : len(early) + 2], refs[len(early) + 2 :]
    rest = planes_of(first[-1][1:-1], -1)
    for i, p in enumerate(rest):
        g_ref[i] = rate(a_ref[p - 1], a_ref[p], a_ref[p + 1], mu_ref[p])
    rates = reader(*zip(g_refs, early), (g_ref, rest))
    inner = sum(first[:-1], []) + first[-1][1:-1]
    coeffs = analyse([(a_ref[p - 1], a_ref[p]) for p in planes_of(inner, -1)[1::2]], fz_ref, fy_ref)
    start = 0
    for ref in own_refs:
        ref[...] = coeffs[:, start : start + ref.shape[1]]
        start += ref.shape[1]
    for p in range(2, nx - 2):
        acc_ref[p - 2] = later_part(rates(p - 1), rates(p), rates(p + 1), a_ref[p], mu_ref[p])


def outer_kernel(a_ref, mu_ref, even_ref, odd_ref, g_ref, fz_ref, fy_ref, after, a_out, g_out, c_ref):
    nx = a_ref.shape[0]
    even = is_even()
    place = lax.axis_index("gx")
    count = lax.axis_size("gx")
    keep_low = (place > 0).astype(F32)
    keep_high = (place < count - 1).astype(F32)
    low = [jnp.where(even, odd_ref[i], even_ref[i]) * keep_low for i in range(3)]
    high = [jnp.where(even, even_ref[i], odd_ref[i]) * keep_high for i in range(3)]
    starts = [low[0], low[1], a_ref[0], a_ref[1]]
    ends = [a_ref[nx - 2], a_ref[nx - 1], high[0], high[1]]
    values = starts[1:3] + ends[1:3]
    rates = [
        rate(starts[0], starts[1], starts[2], low[2]),
        rate(starts[1], starts[2], starts[3], mu_ref[0]),
        rate(ends[0], ends[1], ends[2], mu_ref[nx - 1]),
        rate(ends[1], ends[2], ends[3], high[2]),
    ]
    for i in range(4):
        a_out[i] = values[i]
        g_out[i] = rates[i]
    outer = [v + time_step * g for v, g in zip(values, rates)]
    rest = planes_of(chunks(nx)[0][-1][1:-1], -1)
    inner = [a_ref[p] + time_step * g_ref[i] for i, p in enumerate(rest)]
    c_ref[...] = analyse(by_pairs(outer[:2] + inner + outer[2:]), fz_ref, fy_ref)


def later_kernel(a_ref, mu_ref, ab_ref, gb_ref, low_ref, high_ref, rest_ref, fz_ref, fy_ref, acc_ref, c_ref):
    nx = a_ref.shape[0]
    first = chunks(nx)[0]
    rates = reader(
        (gb_ref, outer_planes(nx)), (low_ref, planes_of(first[0], -1)), (high_ref, planes_of(first[-1][1:-1], -1))
    )
    own = analyse([(ab_ref[0], ab_ref[1]), (ab_ref[2], ab_ref[3])], fz_ref, fy_ref)
    width = 2 * KZ
    c_ref[:, :width] = own[:, :width]
    c_ref[:, width : c_ref.shape[1] - width] = rest_ref[...]
    c_ref[:, c_ref.shape[1] - width :] = own[:, width:]
    for i, p in enumerate((0, 1, nx - 2, nx - 1)):
        acc_ref[i] = later_part(rates(p - 1), rates(p), rates(p + 1), a_ref[p], mu_ref[p])


def received(c, own):
    return jnp.where(lax.axis_index("tm") > 0, c - own, 0.0)


def second_kernel(stage, *refs):
    a_ref, ab_ref, mu_ref, acc_ref, accb_ref, c1_ref, own_ref, fz_ref, fy_ref, by_ref, bz_ref = refs[:11]
    earlier, (a1_ref, e_ref, c2_ref) = refs[11:-3], refs[-3:]
    nx, ny, nz = mu_ref.shape
    first, second = chunks(nx)
    change = synthesise(received(c1_ref[...], own_ref[...]), by_ref, bz_ref)
    before = reader((a_ref, range(nx)), (ab_ref, outer_planes(nx)))
    for i, p in enumerate(planes_of(first[stage], -1)):
        a1_ref[i] = before(p) + change[i // 2][:, (i % 2) * nz : (i % 2 + 1) * nz]
    values = reader(*[(ref, planes_of(part, -1)) for ref, part in zip((*earlier, a1_ref), first)])
    parts = reader((acc_ref, range(2, nx - 2)), (accb_ref, (0, 1, nx - 2, nx - 1)))
    ends = []
    for i, p in enumerate(planes_of(second[stage], 0)):
        v = values(p)
        e = v + time_step * LAST_ROW[0] * rate(values(p - 1), v, values(p + 1), mu_ref[p]) + parts(p)
        e_ref[i] = e
        ends.append(e)
    c2_ref[...] = analyse(by_pairs(ends), fz_ref, fy_ref)


def last_kernel(stage, count, *refs):
    c2_ref, by_ref, bz_ref, a_ref = refs[:4]
    c1_refs, a1_refs = refs[4 : 4 + count], refs[4 + count : 4 + 2 * count]
    out_ref, buffer, sems = refs[-3:]
    nx, ny, nz = out_ref.shape[1:]
    first, second = chunks(nx)
    where = {}
    for ref, part in zip(c1_refs, first):
        for i, p in enumerate(planes_of(part, -1)):
            where[p] = (ref, i)

    def column(p):
        ref, i = where[p]
        return ref[:, i * KZ : (i + 1) * KZ]

    receives = lax.axis_index("tm") > 0

    @pl.when(receives)
    def _():
        values = reader(*[(ref, planes_of(part, -1)) for ref, part in zip(a1_refs, first)])
        planes = planes_of(second[stage], 0)
        before = jnp.concatenate([column(p) for p in planes], axis=1)
        change = synthesise(c2_ref[...] - before, by_ref, bz_ref)
        copies = []
        for i in range(0, len(planes), 2):
            for k in (0, 1):
                buffer[i + k] = values(planes[i + k]) + change[i // 2][:, k * nz : (k + 1) * nz]
            copy = pltpu.make_async_copy(
                buffer.at[pl.ds(i, 2)], out_ref.at[0, pl.ds(planes[i], 2)], sems.at[i // 2]
            )
            copy.start()
            copies.append(copy)
        for copy in copies:
            copy.wait()

    if stage == 0:

        @pl.when(jnp.logical_not(receives))
        def _():
            half = nx // 2
            copies = [
                pltpu.make_async_copy(a_ref.at[pl.ds(i * half, half)], out_ref.at[0, pl.ds(i * half, half)], sems.at[i])
                for i in range(2)
            ]
            for copy in copies:
                copy.start()
            for copy in copies:
                copy.wait()


def join_kernel(*refs):
    parts, out_ref, sems = refs[:-2], refs[-2], refs[-1]
    copies = []
    for ref, part in zip(parts, chunks(out_ref.shape[1])[1]):
        for i, p in enumerate(planes_of(part, 0)[::2]):
            copies.append(
                pltpu.make_async_copy(ref.at[pl.ds(2 * i, 2)], out_ref.at[0, pl.ds(p, 2)], sems.at[len(copies)])
            )
    for copy in copies:
        copy.start()
    for copy in copies:
        copy.wait()


def body(start_states, mobility):
    nx, ny, nz = mobility.shape
    slices, slabs = lax.axis_size("tm"), lax.axis_size("gx")
    a, mu = start_states[0], mobility
    fz, fy, by, bz = map(jnp.asarray, tables(ny, nz))
    first, second = chunks(nx)
    count = len(first)

    def grid(planes):
        return jax.ShapeDtypeStruct((planes, ny, nz), F32)

    def modes(pairs):
        return jax.ShapeDtypeStruct((KY, len(pairs) * 2 * KZ), F32)

    even_pairs = [(s * slabs + g, s * slabs + (g ^ 1)) for s in range(slices) for g in range(slabs)]
    odd_pairs = []
    for s in range(slices):
        for g in range(slabs):
            other = g + 1 if g % 2 else g - 1
            if 0 <= other < slabs:
                odd_pairs.append((s * slabs + g, s * slabs + other))
            else:
                odd_pairs.append((s * slabs + g, (s ^ 2) * slabs + g))
    ring = [(s, (s + 1) % slices) for s in range(slices)]

    def onward(c):
        return lax.ppermute(c, "tm", ring)

    to_odd = call(pack_kernel, grid(3), "pack", scratch=[pltpu.SemaphoreType.DMA((2,))], specs=[ANY] * 2)(
        *[pltpu.with_memory_space_constraint(x, pltpu.HBM) for x in (a, mu)]
    )
    from_odd = lax.ppermute(to_odd, ("tm", "gx"), odd_pairs)
    g, c1 = [], []
    for stage, part in enumerate(first[:-1]):
        rates, c, *to_even = call(
            functools.partial(inner_kernel, stage),
            [grid(2 * len(part)), modes(part)] + [grid(3)] * (stage == 0),
            "inner",
            specs=[VMEM] * 4 + [ANY],
        )(a, mu, fz, fy, to_odd)
        g.append(rates)
        c1.append(onward(c))
        if stage == 0:
            from_even = lax.ppermute(to_even[0], ("tm", "gx"), even_pairs)
    rest = first[-1][1:-1]
    g_rest, acc, *own, own_rest = call(
        middle_kernel,
        [grid(2 * len(rest)), grid(nx - 4), *[modes(part) for part in first[:-1]], modes(rest)],
        "middle",
        cost=0,
    )(a, mu, fz, fy, *g)
    ab, gb, c = call(outer_kernel, [grid(4), grid(4), modes(first[-1])], "outer", specs=[VMEM] * 7 + [ANY])(
        a, mu, from_even, from_odd, g_rest, fz, fy, acc
    )
    c1.append(onward(c))
    accb, own_last = call(later_kernel, [grid(4), modes(first[-1])], "later")(
        a, mu, ab, gb, g[0], g_rest, own_rest, fz, fy
    )
    own.append(own_last)
    a1, e, c2 = [], [], []
    for stage in range(count):
        values, end, c = call(
            functools.partial(second_kernel, stage),
            [grid(2 * len(first[stage])), grid(2 * len(second[stage])), modes(second[stage])],
            "second",
        )(a, ab, mu, acc, accb, c1[stage], own[stage], fz, fy, by, bz, *a1)
        a1.append(values)
        e.append(end)
        c2.append(onward(c))
    whole = jax.ShapeDtypeStruct((1, nx, ny, nz), F32)
    end_state = call(
        join_kernel,
        whole,
        "join",
        scratch=[pltpu.SemaphoreType.DMA((nx // 2,))],
        specs=[ANY] * count,
        out_specs=ANY,
    )(*e)
    result = []
    for stage, part in enumerate(second):
        result = [
            call(
                functools.partial(last_kernel, stage, count),
                whole,
                "last",
                scratch=[pltpu.VMEM((2 * len(part), ny, nz), F32), pltpu.SemaphoreType.DMA((len(part),))],
                specs=[VMEM] * (4 + 2 * count) + [ANY] * len(result),
                out_specs=ANY,
                aliases={4 + 2 * count: 0} if result else {},
            )(c2[stage], by, bz, a, *c1, *a1, *result)
        ]
    return end_state, result[0]


def solution(mesh):
    placed = (P("tm", "gx", None, None), P("gx", None, None))
    return jax.shard_map(
        body,
        mesh=mesh,
        in_specs=placed,
        out_specs=(P("tm", "gx", None, None), P("tm", "gx", None, None)),
        check_vma=False,
    )
```

```python
import functools
import math

import jax
import jax.numpy as jnp
import numpy as np
from jax import lax
from jax.experimental import pallas as pl
from jax.experimental.pallas import tpu as pltpu
from jax.sharding import PartitionSpec as P

KY = 64
KZ = 64
time_step = 0.05
F32 = jnp.float32
BF16 = jnp.bfloat16
VMEM_LIMIT = 24 * 2**20
COST = 10**8
ANY = pl.BlockSpec(memory_space=pl.ANY)
VMEM = pl.BlockSpec(memory_space=pltpu.VMEM)


def basis_value(node_times, source, point):
    total = 1.0
    for other in range(5):
        if other != source:
            total = total * (point - node_times[other]) / (node_times[source] - node_times[other])
    return total


def lobatto():
    root = math.sqrt(3.0 / 7.0)
    node_times = [0.0, (1.0 - root) / 2.0, 0.5, (1.0 + root) / 2.0, 1.0]
    gauss_points = [-math.sqrt(0.6), 0.0, math.sqrt(0.6)]
    gauss_weights = [5.0 / 9.0, 8.0 / 9.0, 5.0 / 9.0]
    last_row = []
    for source in range(5):
        integral = 0.0
        for point, weight in zip(gauss_points, gauss_weights):
            integral += 0.5 * weight * basis_value(node_times, source, 0.5 * (1.0 + point))
        last_row.append(integral)
    return node_times, last_row


NODE_TIMES, LAST_ROW = lobatto()
W = [sum(LAST_ROW[j] * NODE_TIMES[j] ** k for j in range(1, 5)) for k in range(4)]


def dct_rows(count, kept):
    freq = np.arange(kept, dtype=np.float64)[:, None]
    place = np.arange(count, dtype=np.float64)[None, :]
    matrix = np.cos(np.pi * (place + 0.5) * freq / count) * np.sqrt(2.0 / count)
    return np.where(freq == 0, matrix * np.sqrt(0.5), matrix)


def halves(matrix):
    high = matrix.astype(jnp.bfloat16)
    low = (matrix - high.astype(np.float64)).astype(jnp.bfloat16)
    return high, low


def tables(ny, nz):
    cy = dct_rows(ny, KY)
    cz = dct_rows(nz, KZ)
    twice = np.zeros((2 * nz, 2 * KZ))
    twice[:nz, :KZ] = cz.T
    twice[nz:, KZ:] = cz.T
    zh, zl = halves(twice)
    fz = np.concatenate([zh, zl], axis=1)
    yh, yl = halves(cy)
    fy = np.block([[yh, yh], [yl, np.zeros_like(yl)]])
    by = np.concatenate([yh.T, yh.T, yl.T], axis=1)
    bz = np.concatenate([zh.T, zh.T, zl.T], axis=0)
    return fz, fy, by, bz


def split(x):
    high = x.astype(BF16)
    return high, (x - high.astype(F32)).astype(BF16)


def dot(a, b):
    return jnp.dot(a, b, preferred_element_type=F32)


def neighbours(v):
    ny, nz = v.shape
    rows = lax.broadcasted_iota(jnp.int32, (8, nz), 0)
    lanes = lax.broadcasted_iota(jnp.int32, v.shape, 1)
    low = pltpu.roll(v, 1, 0)
    high = pltpu.roll(v, ny - 1, 0)
    low = jnp.concatenate([jnp.where(rows == 0, 0.0, low[:8]), low[8:]], axis=0)
    high = jnp.concatenate([high[: ny - 8], jnp.where(rows == 7, 0.0, high[ny - 8 :])], axis=0)
    left = jnp.where(lanes == 0, 0.0, pltpu.roll(v, 1, 1))
    right = jnp.where(lanes == nz - 1, 0.0, pltpu.roll(v, nz - 1, 1))
    return (low + high) + (left + right)


def rate(below, v, above, mobility):
    return mobility * (neighbours(v) + (below + above) - v * (5.0 + v * v))


def analyse(pairs, fz_ref, fy_ref):
    rows = []
    for first, second in pairs:
        first_high, first_low = split(first)
        second_high, second_low = split(second)
        rows.append(jnp.concatenate([first_high, second_high, first_low, second_low], axis=1))
    rows = jnp.concatenate(rows, axis=0)
    width, nz = 2 * KZ, pairs[0][0].shape[1]
    half = dot(rows[:, : 2 * nz], fz_ref[...])
    half = half[:, :width] + half[:, width:] + dot(rows[:, 2 * nz :], fz_ref[:, :width])
    ny = pairs[0][0].shape[0]
    columns = []
    for i in range(len(pairs)):
        columns.append(jnp.concatenate(split(half[i * ny : (i + 1) * ny]), axis=0))
    coeffs = dot(fy_ref[...], jnp.concatenate(columns, axis=1))
    return coeffs[:KY] + coeffs[KY:]


def synthesise(coeffs, by_ref, bz_ref):
    high, low = split(coeffs)
    half = dot(by_ref[...], jnp.concatenate([high, low, high], axis=0))
    width = 2 * KZ
    count = coeffs.shape[1] // width
    rows = []
    for i in range(count):
        high, low = split(half[:, i * width : (i + 1) * width])
        rows.append(jnp.concatenate([high, low, high], axis=1))
    planes = dot(jnp.concatenate(rows, axis=0), bz_ref[...])
    ny = half.shape[0]
    return [planes[i * ny : (i + 1) * ny] for i in range(count)]


def call(kernel, outs, name, scratch=(), specs=None, out_specs=None, aliases={}, cost=COST):
    def run(*args):
        return pl.pallas_call(
            kernel,
            out_shape=outs,
            in_specs=specs or [VMEM] * len(args),
            out_specs=out_specs or jax.tree.map(lambda _: VMEM, outs),
            scratch_shapes=scratch,
            input_output_aliases=aliases,
            compiler_params=pltpu.CompilerParams(vmem_limit_bytes=VMEM_LIMIT),
            cost_estimate=pl.CostEstimate(flops=100 * cost, bytes_accessed=10 * cost, transcendentals=0),
            name=name,
        )(*args)

    return run


def chunks(nx):
    last = nx // 2
    early, soon = last - 3, last - 4
    first = [list(range(1, early + 1)), [0, *range(early + 1, last + 1)]]
    second = [list(range(1, soon + 1)), [0, *range(soon + 1, last)]]
    return first, second


def planes_of(pairs, shift):
    return [2 * t + shift + k for t in pairs for k in (0, 1)]


def outer_planes(nx):
    return [-1, 0, nx - 1, nx]


def reader(*parts):
    where = {}
    for ref, planes in parts:
        for i, p in enumerate(planes):
            where[p] = (ref, i)

    def read(p):
        ref, i = where[p]
        return ref[i]

    return read


def by_pairs(planes):
    return list(zip(planes[::2], planes[1::2]))


def is_even():
    return lax.rem(lax.axis_index("gx"), 2) == 0


def pack_kernel(a_ref, mu_ref, odd_ref, sems):
    nx = a_ref.shape[0]
    even = is_even()
    copies = [
        pltpu.make_async_copy(a_ref.at[pl.ds(jnp.where(even, 0, nx - 2), 2)], odd_ref.at[pl.ds(0, 2)], sems.at[0]),
        pltpu.make_async_copy(mu_ref.at[pl.ds(jnp.where(even, 0, nx - 1), 1)], odd_ref.at[pl.ds(2, 1)], sems.at[1]),
    ]
    for copy in copies:
        copy.start()
    for copy in copies:
        copy.wait()


def inner_kernel(stage, a_ref, mu_ref, fz_ref, fy_ref, after, g_ref, c_ref, *even_ref):
    ends = []
    for i, p in enumerate(planes_of(chunks(a_ref.shape[0])[0][stage], -1)):
        g = rate(a_ref[p - 1], a_ref[p], a_ref[p + 1], mu_ref[p])
        g_ref[i] = g
        ends.append(a_ref[p] + time_step * g)
    c_ref[...] = analyse(by_pairs(ends), fz_ref, fy_ref)
    if stage == 0:
        nx = a_ref.shape[0]
        even = is_even()
        even_ref[0][0] = jnp.where(even, a_ref[nx - 2], a_ref[0])
        even_ref[0][1] = jnp.where(even, a_ref[nx - 1], a_ref[1])
        even_ref[0][2] = jnp.where(even, mu_ref[nx - 1], mu_ref[0])


def later_part(below, g, above, a, mobility):
    h = time_step
    laplace = neighbours(g) + (below + above) - 5.0 * g
    hg = h * g
    cube = hg * (3.0 * W[1] * a * a + hg * (3.0 * W[2] * a + W[3] * hg))
    return h * (W[0] * g + mobility * (h * W[1] * laplace - cube))


def middle_kernel(a_ref, mu_ref, fz_ref, fy_ref, *refs):
    nx = a_ref.shape[0]
    first = chunks(nx)[0]
    early = [planes_of(part, -1) for part in first[:-1]]
    g_refs, (g_ref, acc_ref), own_refs = refs[: len(early)], refs[len(early) : len(early) + 2], refs[len(early) + 2 :]
    rest = planes_of(first[-1][1:-1], -1)
    for i, p in enumerate(rest):
        g_ref[i] = rate(a_ref[p - 1], a_ref[p], a_ref[p + 1], mu_ref[p])
    rates = reader(*zip(g_refs, early), (g_ref, rest))
    inner = sum(first[:-1], []) + first[-1][1:-1]
    coeffs = analyse([(a_ref[p - 1], a_ref[p]) for p in planes_of(inner, -1)[1::2]], fz_ref, fy_ref)
    start = 0
    for ref in own_refs:
        ref[...] = coeffs[:, start : start + ref.shape[1]]
        start += ref.shape[1]
    for p in range(2, nx - 2):
        acc_ref[p - 2] = later_part(rates(p - 1), rates(p), rates(p + 1), a_ref[p], mu_ref[p])


def outer_kernel(a_ref, mu_ref, even_ref, odd_ref, g_ref, fz_ref, fy_ref, after, a_out, g_out, c_ref):
    nx = a_ref.shape[0]
    even = is_even()
    place = lax.axis_index("gx")
    count = lax.axis_size("gx")
    keep_low = (place > 0).astype(F32)
    keep_high = (place < count - 1).astype(F32)
    low = [jnp.where(even, odd_ref[i], even_ref[i]) * keep_low for i in range(3)]
    high = [jnp.where(even, even_ref[i], odd_ref[i]) * keep_high for i in range(3)]
    starts = [low[0], low[1], a_ref[0], a_ref[1]]
    ends = [a_ref[nx - 2], a_ref[nx - 1], high[0], high[1]]
    values = starts[1:3] + ends[1:3]
    rates = [
        rate(starts[0], starts[1], starts[2], low[2]),
        rate(starts[1], starts[2], starts[3], mu_ref[0]),
        rate(ends[0], ends[1], ends[2], mu_ref[nx - 1]),
        rate(ends[1], ends[2], ends[3], high[2]),
    ]
    for i in range(4):
        a_out[i] = values[i]
        g_out[i] = rates[i]
    outer = [v + time_step * g for v, g in zip(values, rates)]
    rest = planes_of(chunks(nx)[0][-1][1:-1], -1)
    inner = [a_ref[p] + time_step * g_ref[i] for i, p in enumerate(rest)]
    c_ref[...] = analyse(by_pairs(outer[:2] + inner + outer[2:]), fz_ref, fy_ref)


def later_kernel(a_ref, mu_ref, ab_ref, gb_ref, low_ref, high_ref, rest_ref, fz_ref, fy_ref, acc_ref, c_ref):
    nx = a_ref.shape[0]
    first = chunks(nx)[0]
    rates = reader(
        (gb_ref, outer_planes(nx)), (low_ref, planes_of(first[0], -1)), (high_ref, planes_of(first[-1][1:-1], -1))
    )
    own = analyse([(ab_ref[0], ab_ref[1]), (ab_ref[2], ab_ref[3])], fz_ref, fy_ref)
    width = 2 * KZ
    c_ref[:, :width] = own[:, :width]
    c_ref[:, width : c_ref.shape[1] - width] = rest_ref[...]
    c_ref[:, c_ref.shape[1] - width :] = own[:, width:]
    for i, p in enumerate((0, 1, nx - 2, nx - 1)):
        acc_ref[i] = later_part(rates(p - 1), rates(p), rates(p + 1), a_ref[p], mu_ref[p])


def received(c, own):
    return jnp.where(lax.axis_index("tm") > 0, c - own, 0.0)


def second_kernel(stage, *refs):
    a_ref, ab_ref, mu_ref, acc_ref, accb_ref, c1_ref, own_ref, fz_ref, fy_ref, by_ref, bz_ref = refs[:11]
    earlier, (a1_ref, e_ref, c2_ref) = refs[11:-3], refs[-3:]
    nx, ny, nz = mu_ref.shape
    first, second = chunks(nx)
    before = reader((a_ref, range(nx)), (ab_ref, outer_planes(nx)))
    receives = lax.axis_index("tm") > 0

    @pl.when(receives)
    def _():
        change = synthesise(c1_ref[...] - own_ref[...], by_ref, bz_ref)
        for i, p in enumerate(planes_of(first[stage], -1)):
            a1_ref[i] = before(p) + change[i // 2][:, (i % 2) * nz : (i % 2 + 1) * nz]

    @pl.when(jnp.logical_not(receives))
    def _():
        for i, p in enumerate(planes_of(first[stage], -1)):
            a1_ref[i] = before(p)

    values = reader(*[(ref, planes_of(part, -1)) for ref, part in zip((*earlier, a1_ref), first)])
    parts = reader((acc_ref, range(2, nx - 2)), (accb_ref, (0, 1, nx - 2, nx - 1)))
    ends = []
    for i, p in enumerate(planes_of(second[stage], 0)):
        v = values(p)
        e = v + time_step * LAST_ROW[0] * rate(values(p - 1), v, values(p + 1), mu_ref[p]) + parts(p)
        e_ref[i] = e
        ends.append(e)
    c2_ref[...] = analyse(by_pairs(ends), fz_ref, fy_ref)


def last_kernel(stage, count, *refs):
    c2_ref, by_ref, bz_ref, a_ref = refs[:4]
    c1_refs, a1_refs = refs[4 : 4 + count], refs[4 + count : 4 + 2 * count]
    out_ref, buffer, sems = refs[-3:]
    nx, ny, nz = out_ref.shape[1:]
    first, second = chunks(nx)
    where = {}
    for ref, part in zip(c1_refs, first):
        for i, p in enumerate(planes_of(part, -1)):
            where[p] = (ref, i)

    def column(p):
        ref, i = where[p]
        return ref[:, i * KZ : (i + 1) * KZ]

    receives = lax.axis_index("tm") > 0

    @pl.when(receives)
    def _():
        values = reader(*[(ref, planes_of(part, -1)) for ref, part in zip(a1_refs, first)])
        planes = planes_of(second[stage], 0)
        before = jnp.concatenate([column(p) for p in planes], axis=1)
        change = synthesise(c2_ref[...] - before, by_ref, bz_ref)
        copies = []
        for i in range(0, len(planes), 2):
            for k in (0, 1):
                buffer[i + k] = values(planes[i + k]) + change[i // 2][:, k * nz : (k + 1) * nz]
            copy = pltpu.make_async_copy(
                buffer.at[pl.ds(i, 2)], out_ref.at[0, pl.ds(planes[i], 2)], sems.at[i // 2]
            )
            copy.start()
            copies.append(copy)
        for copy in copies:
            copy.wait()

    if stage == 0:

        @pl.when(jnp.logical_not(receives))
        def _():
            half = nx // 2
            copies = [
                pltpu.make_async_copy(a_ref.at[pl.ds(i * half, half)], out_ref.at[0, pl.ds(i * half, half)], sems.at[i])
                for i in range(2)
            ]
            for copy in copies:
                copy.start()
            for copy in copies:
                copy.wait()


def join_kernel(*refs):
    parts, out_ref, sems = refs[:-2], refs[-2], refs[-1]
    copies = []
    for ref, part in zip(parts, chunks(out_ref.shape[1])[1]):
        for i, p in enumerate(planes_of(part, 0)[::2]):
            copies.append(
                pltpu.make_async_copy(ref.at[pl.ds(2 * i, 2)], out_ref.at[0, pl.ds(p, 2)], sems.at[len(copies)])
            )
    for copy in copies:
        copy.start()
    for copy in copies:
        copy.wait()


def body(start_states, mobility):
    nx, ny, nz = mobility.shape
    slices, slabs = lax.axis_size("tm"), lax.axis_size("gx")
    a, mu = start_states[0], mobility
    fz, fy, by, bz = map(jnp.asarray, tables(ny, nz))
    first, second = chunks(nx)
    count = len(first)

    def grid(planes):
        return jax.ShapeDtypeStruct((planes, ny, nz), F32)

    def modes(pairs):
        return jax.ShapeDtypeStruct((KY, len(pairs) * 2 * KZ), F32)

    even_pairs = [(s * slabs + g, s * slabs + (g ^ 1)) for s in range(slices) for g in range(slabs)]
    odd_pairs = []
    for s in range(slices):
        for g in range(slabs):
            other = g + 1 if g % 2 else g - 1
            if 0 <= other < slabs:
                odd_pairs.append((s * slabs + g, s * slabs + other))
            else:
                odd_pairs.append((s * slabs + g, (s ^ 2) * slabs + g))
    ring = [(s, (s + 1) % slices) for s in range(slices)]

    def onward(c):
        return lax.ppermute(c, "tm", ring)

    to_odd = call(pack_kernel, grid(3), "pack", scratch=[pltpu.SemaphoreType.DMA((2,))], specs=[ANY] * 2)(
        *[pltpu.with_memory_space_constraint(x, pltpu.HBM) for x in (a, mu)]
    )
    from_odd = lax.ppermute(to_odd, ("tm", "gx"), odd_pairs)
    g, c1 = [], []
    for stage, part in enumerate(first[:-1]):
        rates, c, *to_even = call(
            functools.partial(inner_kernel, stage),
            [grid(2 * len(part)), modes(part)] + [grid(3)] * (stage == 0),
            "inner",
            specs=[VMEM] * 4 + [ANY],
        )(a, mu, fz, fy, to_odd)
        g.append(rates)
        c1.append(onward(c))
        if stage == 0:
            from_even = lax.ppermute(to_even[0], ("tm", "gx"), even_pairs)
    rest = first[-1][1:-1]
    g_rest, acc, *own, own_rest = call(
        middle_kernel,
        [grid(2 * len(rest)), grid(nx - 4), *[modes(part) for part in first[:-1]], modes(rest)],
        "middle",
        cost=0,
    )(a, mu, fz, fy, *g)
    ab, gb, c = call(outer_kernel, [grid(4), grid(4), modes(first[-1])], "outer", specs=[VMEM] * 7 + [ANY])(
        a, mu, from_even, from_odd, g_rest, fz, fy, acc
    )
    c1.append(onward(c))
    accb, own_last = call(later_kernel, [grid(4), modes(first[-1])], "later")(
        a, mu, ab, gb, g[0], g_rest, own_rest, fz, fy
    )
    own.append(own_last)
    a1, e, c2 = [], [], []
    for stage in range(count):
        values, end, c = call(
            functools.partial(second_kernel, stage),
            [grid(2 * len(first[stage])), grid(2 * len(second[stage])), modes(second[stage])],
            "second",
        )(a, ab, mu, acc, accb, c1[stage], own[stage], fz, fy, by, bz, *a1)
        a1.append(values)
        e.append(end)
        c2.append(onward(c))
    whole = jax.ShapeDtypeStruct((1, nx, ny, nz), F32)
    end_state = call(
        join_kernel,
        whole,
        "join",
        scratch=[pltpu.SemaphoreType.DMA((nx // 2,))],
        specs=[ANY] * count,
        out_specs=ANY,
    )(*e)
    result = []
    for stage, part in enumerate(second):
        result = [
            call(
                functools.partial(last_kernel, stage, count),
                whole,
                "last",
                scratch=[pltpu.VMEM((2 * len(part), ny, nz), F32), pltpu.SemaphoreType.DMA((len(part),))],
                specs=[VMEM] * (4 + 2 * count) + [ANY] * len(result),
                out_specs=ANY,
                aliases={4 + 2 * count: 0} if result else {},
            )(c2[stage], by, bz, a, *c1, *a1, *result)
        ]
    return end_state, result[0]


def solution(mesh):
    placed = (P("tm", "gx", None, None), P("gx", None, None))
    return jax.shard_map(
        body,
        mesh=mesh,
        in_specs=placed,
        out_specs=(P("tm", "gx", None, None), P("tm", "gx", None, None)),
        check_vma=False,
    )
```

```python
import functools
import math

import jax
import jax.numpy as jnp
import numpy as np
from jax import lax
from jax.experimental import pallas as pl
from jax.experimental.pallas import tpu as pltpu
from jax.sharding import PartitionSpec as P

KY = 64
KZ = 64
time_step = 0.05
F32 = jnp.float32
BF16 = jnp.bfloat16
VMEM_LIMIT = 24 * 2**20
COST = 10**8
ANY = pl.BlockSpec(memory_space=pl.ANY)
VMEM = pl.BlockSpec(memory_space=pltpu.VMEM)


def basis_value(node_times, source, point):
    total = 1.0
    for other in range(5):
        if other != source:
            total = total * (point - node_times[other]) / (node_times[source] - node_times[other])
    return total


def lobatto():
    root = math.sqrt(3.0 / 7.0)
    node_times = [0.0, (1.0 - root) / 2.0, 0.5, (1.0 + root) / 2.0, 1.0]
    gauss_points = [-math.sqrt(0.6), 0.0, math.sqrt(0.6)]
    gauss_weights = [5.0 / 9.0, 8.0 / 9.0, 5.0 / 9.0]
    last_row = []
    for source in range(5):
        integral = 0.0
        for point, weight in zip(gauss_points, gauss_weights):
            integral += 0.5 * weight * basis_value(node_times, source, 0.5 * (1.0 + point))
        last_row.append(integral)
    return node_times, last_row


NODE_TIMES, LAST_ROW = lobatto()
W = [sum(LAST_ROW[j] * NODE_TIMES[j] ** k for j in range(1, 5)) for k in range(4)]


def dct_rows(count, kept):
    freq = np.arange(kept, dtype=np.float64)[:, None]
    place = np.arange(count, dtype=np.float64)[None, :]
    matrix = np.cos(np.pi * (place + 0.5) * freq / count) * np.sqrt(2.0 / count)
    return np.where(freq == 0, matrix * np.sqrt(0.5), matrix)


def halves(matrix):
    high = matrix.astype(jnp.bfloat16)
    low = (matrix - high.astype(np.float64)).astype(jnp.bfloat16)
    return high, low


def tables(ny, nz):
    cy = dct_rows(ny, KY)
    cz = dct_rows(nz, KZ)
    twice = np.zeros((2 * nz, 2 * KZ))
    twice[:nz, :KZ] = cz.T
    twice[nz:, KZ:] = cz.T
    zh, zl = halves(twice)
    fz = np.concatenate([zh, zl], axis=1)
    yh, yl = halves(cy)
    fy = np.block([[yh, yh], [yl, np.zeros_like(yl)]])
    by = np.concatenate([yh.T, yh.T, yl.T], axis=1)
    bz = np.concatenate([zh.T, zh.T, zl.T], axis=0)
    return fz, fy, by, bz


def split(x):
    high = x.astype(BF16)
    return high, (x - high.astype(F32)).astype(BF16)


def dot(a, b):
    return jnp.dot(a, b, preferred_element_type=F32)


def neighbours(v):
    ny, nz = v.shape
    rows = lax.broadcasted_iota(jnp.int32, (8, nz), 0)
    lanes = lax.broadcasted_iota(jnp.int32, v.shape, 1)
    low = pltpu.roll(v, 1, 0)
    high = pltpu.roll(v, ny - 1, 0)
    low = jnp.concatenate([jnp.where(rows == 0, 0.0, low[:8]), low[8:]], axis=0)
    high = jnp.concatenate([high[: ny - 8], jnp.where(rows == 7, 0.0, high[ny - 8 :])], axis=0)
    left = jnp.where(lanes == 0, 0.0, pltpu.roll(v, 1, 1))
    right = jnp.where(lanes == nz - 1, 0.0, pltpu.roll(v, nz - 1, 1))
    return (low + high) + (left + right)


def rate(below, v, above, mobility):
    return mobility * (neighbours(v) + (below + above) - v * (5.0 + v * v))


def analyse(pairs, fz_ref, fy_ref):
    rows = []
    for first, second in pairs:
        first_high, first_low = split(first)
        second_high, second_low = split(second)
        rows.append(jnp.concatenate([first_high, second_high, first_low, second_low], axis=1))
    rows = jnp.concatenate(rows, axis=0)
    width, nz = 2 * KZ, pairs[0][0].shape[1]
    half = dot(rows[:, : 2 * nz], fz_ref[...])
    half = half[:, :width] + half[:, width:] + dot(rows[:, 2 * nz :], fz_ref[:, :width])
    ny = pairs[0][0].shape[0]
    columns = []
    for i in range(len(pairs)):
        columns.append(jnp.concatenate(split(half[i * ny : (i + 1) * ny]), axis=0))
    coeffs = dot(fy_ref[...], jnp.concatenate(columns, axis=1))
    return coeffs[:KY] + coeffs[KY:]


def synthesise(coeffs, by_ref, bz_ref):
    high, low = split(coeffs)
    half = dot(by_ref[...], jnp.concatenate([high, low, high], axis=0))
    width = 2 * KZ
    count = coeffs.shape[1] // width
    rows = []
    for i in range(count):
        high, low = split(half[:, i * width : (i + 1) * width])
        rows.append(jnp.concatenate([high, low, high], axis=1))
    planes = dot(jnp.concatenate(rows, axis=0), bz_ref[...])
    ny = half.shape[0]
    return [planes[i * ny : (i + 1) * ny] for i in range(count)]


def call(kernel, outs, name, scratch=(), specs=None, out_specs=None, aliases={}, cost=COST):
    def run(*args):
        return pl.pallas_call(
            kernel,
            out_shape=outs,
            in_specs=specs or [VMEM] * len(args),
            out_specs=out_specs or jax.tree.map(lambda _: VMEM, outs),
            scratch_shapes=scratch,
            input_output_aliases=aliases,
            compiler_params=pltpu.CompilerParams(vmem_limit_bytes=VMEM_LIMIT),
            cost_estimate=pl.CostEstimate(flops=100 * cost, bytes_accessed=10 * cost, transcendentals=0),
            name=name,
        )(*args)

    return run


def chunks(nx):
    last = nx // 2
    early, soon = last - 3, last - 4
    first = [list(range(1, early + 1)), [0, *range(early + 1, last + 1)]]
    second = [list(range(1, soon + 1)), [0, *range(soon + 1, last)]]
    return first, second


def planes_of(pairs, shift):
    return [2 * t + shift + k for t in pairs for k in (0, 1)]


def outer_planes(nx):
    return [-1, 0, nx - 1, nx]


def reader(*parts):
    where = {}
    for ref, planes in parts:
        for i, p in enumerate(planes):
            where[p] = (ref, i)

    def read(p):
        ref, i = where[p]
        return ref[i]

    return read


def by_pairs(planes):
    return list(zip(planes[::2], planes[1::2]))


def is_even():
    return lax.rem(lax.axis_index("gx"), 2) == 0


def pack_kernel(a_ref, mu_ref, odd_ref, sems):
    nx = a_ref.shape[0]
    even = is_even()
    copies = [
        pltpu.make_async_copy(a_ref.at[pl.ds(jnp.where(even, 0, nx - 2), 2)], odd_ref.at[pl.ds(0, 2)], sems.at[0]),
        pltpu.make_async_copy(mu_ref.at[pl.ds(jnp.where(even, 0, nx - 1), 1)], odd_ref.at[pl.ds(2, 1)], sems.at[1]),
    ]
    for copy in copies:
        copy.start()
    for copy in copies:
        copy.wait()


def inner_kernel(stage, a_ref, mu_ref, fz_ref, fy_ref, after, g_ref, c_ref, *even_ref):
    ends = []
    for i, p in enumerate(planes_of(chunks(a_ref.shape[0])[0][stage], -1)):
        g = rate(a_ref[p - 1], a_ref[p], a_ref[p + 1], mu_ref[p])
        g_ref[i] = g
        ends.append(a_ref[p] + time_step * g)
    c_ref[...] = analyse(by_pairs(ends), fz_ref, fy_ref)
    if stage == 0:
        nx = a_ref.shape[0]
        even = is_even()
        even_ref[0][0] = jnp.where(even, a_ref[nx - 2], a_ref[0])
        even_ref[0][1] = jnp.where(even, a_ref[nx - 1], a_ref[1])
        even_ref[0][2] = jnp.where(even, mu_ref[nx - 1], mu_ref[0])


def later_part(below, g, above, a, mobility):
    h = time_step
    laplace = neighbours(g) + (below + above) - 5.0 * g
    hg = h * g
    cube = hg * (3.0 * W[1] * a * a + hg * (3.0 * W[2] * a + W[3] * hg))
    return h * (W[0] * g + mobility * (h * W[1] * laplace - cube))


def middle_kernel(a_ref, mu_ref, fz_ref, fy_ref, *refs):
    nx = a_ref.shape[0]
    first = chunks(nx)[0]
    early = [planes_of(part, -1) for part in first[:-1]]
    g_refs, (g_ref, acc_ref), own_refs = refs[: len(early)], refs[len(early) : len(early) + 2], refs[len(early) + 2 :]
    rest = planes_of(first[-1][1:-1], -1)
    for i, p in enumerate(rest):
        g_ref[i] = rate(a_ref[p - 1], a_ref[p], a_ref[p + 1], mu_ref[p])
    rates = reader(*zip(g_refs, early), (g_ref, rest))
    inner = sum(first[:-1], []) + first[-1][1:-1]
    coeffs = analyse([(a_ref[p - 1], a_ref[p]) for p in planes_of(inner, -1)[1::2]], fz_ref, fy_ref)
    start = 0
    for ref in own_refs:
        ref[...] = coeffs[:, start : start + ref.shape[1]]
        start += ref.shape[1]
    for p in range(2, nx - 2):
        acc_ref[p - 2] = later_part(rates(p - 1), rates(p), rates(p + 1), a_ref[p], mu_ref[p])


def mark_kernel(from_odd, after, out_ref):
    out_ref[...] = jnp.zeros_like(out_ref)


def outer_kernel(a_ref, mu_ref, even_ref, odd_ref, g_ref, fz_ref, fy_ref, after, a_out, g_out, c_ref):
    nx = a_ref.shape[0]
    even = is_even()
    place = lax.axis_index("gx")
    count = lax.axis_size("gx")
    keep_low = (place > 0).astype(F32)
    keep_high = (place < count - 1).astype(F32)
    low = [jnp.where(even, odd_ref[i], even_ref[i]) * keep_low for i in range(3)]
    high = [jnp.where(even, even_ref[i], odd_ref[i]) * keep_high for i in range(3)]
    starts = [low[0], low[1], a_ref[0], a_ref[1]]
    ends = [a_ref[nx - 2], a_ref[nx - 1], high[0], high[1]]
    values = starts[1:3] + ends[1:3]
    rates = [
        rate(starts[0], starts[1], starts[2], low[2]),
        rate(starts[1], starts[2], starts[3], mu_ref[0]),
        rate(ends[0], ends[1], ends[2], mu_ref[nx - 1]),
        rate(ends[1], ends[2], ends[3], high[2]),
    ]
    for i in range(4):
        a_out[i] = values[i]
        g_out[i] = rates[i]
    outer = [v + time_step * g for v, g in zip(values, rates)]
    rest = planes_of(chunks(nx)[0][-1][1:-1], -1)
    inner = [a_ref[p] + time_step * g_ref[i] for i, p in enumerate(rest)]
    c_ref[...] = analyse(by_pairs(outer[:2] + inner + outer[2:]), fz_ref, fy_ref)


def later_kernel(a_ref, mu_ref, ab_ref, gb_ref, low_ref, high_ref, rest_ref, fz_ref, fy_ref, acc_ref, c_ref):
    nx = a_ref.shape[0]
    first = chunks(nx)[0]
    rates = reader(
        (gb_ref, outer_planes(nx)), (low_ref, planes_of(first[0], -1)), (high_ref, planes_of(first[-1][1:-1], -1))
    )
    own = analyse([(ab_ref[0], ab_ref[1]), (ab_ref[2], ab_ref[3])], fz_ref, fy_ref)
    width = 2 * KZ
    c_ref[:, :width] = own[:, :width]
    c_ref[:, width : c_ref.shape[1] - width] = rest_ref[...]
    c_ref[:, c_ref.shape[1] - width :] = own[:, width:]
    for i, p in enumerate((0, 1, nx - 2, nx - 1)):
        acc_ref[i] = later_part(rates(p - 1), rates(p), rates(p + 1), a_ref[p], mu_ref[p])


def received(c, own):
    return jnp.where(lax.axis_index("tm") > 0, c - own, 0.0)


def second_kernel(stage, *refs):
    a_ref, ab_ref, mu_ref, acc_ref, accb_ref, c1_ref, own_ref, fz_ref, fy_ref, by_ref, bz_ref = refs[:11]
    earlier, (a1_ref, e_ref, c2_ref) = refs[11:-3], refs[-3:]
    nx, ny, nz = mu_ref.shape
    first, second = chunks(nx)
    before = reader((a_ref, range(nx)), (ab_ref, outer_planes(nx)))
    receives = lax.axis_index("tm") > 0

    @pl.when(receives)
    def _():
        change = synthesise(c1_ref[...] - own_ref[...], by_ref, bz_ref)
        for i, p in enumerate(planes_of(first[stage], -1)):
            a1_ref[i] = before(p) + change[i // 2][:, (i % 2) * nz : (i % 2 + 1) * nz]

    @pl.when(jnp.logical_not(receives))
    def _():
        for i, p in enumerate(planes_of(first[stage], -1)):
            a1_ref[i] = before(p)

    values = reader(*[(ref, planes_of(part, -1)) for ref, part in zip((*earlier, a1_ref), first)])
    parts = reader((acc_ref, range(2, nx - 2)), (accb_ref, (0, 1, nx - 2, nx - 1)))
    ends = []
    for i, p in enumerate(planes_of(second[stage], 0)):
        v = values(p)
        e = v + time_step * LAST_ROW[0] * rate(values(p - 1), v, values(p + 1), mu_ref[p]) + parts(p)
        e_ref[i] = e
        ends.append(e)
    c2_ref[...] = analyse(by_pairs(ends), fz_ref, fy_ref)


def last_kernel(stage, count, *refs):
    c2_ref, by_ref, bz_ref, a_ref = refs[:4]
    c1_refs, a1_refs = refs[4 : 4 + count], refs[4 + count : 4 + 2 * count]
    out_ref, buffer, sems = refs[-3:]
    nx, ny, nz = out_ref.shape[1:]
    first, second = chunks(nx)
    where = {}
    for ref, part in zip(c1_refs, first):
        for i, p in enumerate(planes_of(part, -1)):
            where[p] = (ref, i)

    def column(p):
        ref, i = where[p]
        return ref[:, i * KZ : (i + 1) * KZ]

    receives = lax.axis_index("tm") > 0

    @pl.when(receives)
    def _():
        values = reader(*[(ref, planes_of(part, -1)) for ref, part in zip(a1_refs, first)])
        planes = planes_of(second[stage], 0)
        before = jnp.concatenate([column(p) for p in planes], axis=1)
        change = synthesise(c2_ref[...] - before, by_ref, bz_ref)
        copies = []
        for i in range(0, len(planes), 2):
            for k in (0, 1):
                buffer[i + k] = values(planes[i + k]) + change[i // 2][:, k * nz : (k + 1) * nz]
            copy = pltpu.make_async_copy(
                buffer.at[pl.ds(i, 2)], out_ref.at[0, pl.ds(planes[i], 2)], sems.at[i // 2]
            )
            copy.start()
            copies.append(copy)
        for copy in copies:
            copy.wait()

    if stage == 0:

        @pl.when(jnp.logical_not(receives))
        def _():
            half = nx // 2
            copies = [
                pltpu.make_async_copy(a_ref.at[pl.ds(i * half, half)], out_ref.at[0, pl.ds(i * half, half)], sems.at[i])
                for i in range(2)
            ]
            for copy in copies:
                copy.start()
            for copy in copies:
                copy.wait()


def join_kernel(*refs):
    parts, out_ref, sems = refs[:-2], refs[-2], refs[-1]
    copies = []
    for ref, part in zip(parts, chunks(out_ref.shape[1])[1]):
        for i, p in enumerate(planes_of(part, 0)[::2]):
            copies.append(
                pltpu.make_async_copy(ref.at[pl.ds(2 * i, 2)], out_ref.at[0, pl.ds(p, 2)], sems.at[len(copies)])
            )
    for copy in copies:
        copy.start()
    for copy in copies:
        copy.wait()


def body(start_states, mobility):
    nx, ny, nz = mobility.shape
    slices, slabs = lax.axis_size("tm"), lax.axis_size("gx")
    a, mu = start_states[0], mobility
    fz, fy, by, bz = map(jnp.asarray, tables(ny, nz))
    first, second = chunks(nx)
    count = len(first)

    def grid(planes):
        return jax.ShapeDtypeStruct((planes, ny, nz), F32)

    def modes(pairs):
        return jax.ShapeDtypeStruct((KY, len(pairs) * 2 * KZ), F32)

    even_pairs = [(s * slabs + g, s * slabs + (g ^ 1)) for s in range(slices) for g in range(slabs)]
    odd_pairs = []
    for s in range(slices):
        for g in range(slabs):
            other = g + 1 if g % 2 else g - 1
            if 0 <= other < slabs:
                odd_pairs.append((s * slabs + g, s * slabs + other))
            else:
                odd_pairs.append((s * slabs + g, (s ^ 2) * slabs + g))
    ring = [(s, (s + 1) % slices) for s in range(slices)]

    def onward(c):
        return lax.ppermute(c, "tm", ring)

    to_odd = call(pack_kernel, grid(3), "pack", scratch=[pltpu.SemaphoreType.DMA((2,))], specs=[ANY] * 2)(
        *[pltpu.with_memory_space_constraint(x, pltpu.HBM) for x in (a, mu)]
    )
    from_odd = lax.ppermute(to_odd, ("tm", "gx"), odd_pairs)
    g, c1 = [], []
    for stage, part in enumerate(first[:-1]):
        rates, c, *to_even = call(
            functools.partial(inner_kernel, stage),
            [grid(2 * len(part)), modes(part)] + [grid(3)] * (stage == 0),
            "inner",
            specs=[VMEM] * 4 + [ANY],
        )(a, mu, fz, fy, to_odd)
        g.append(rates)
        c1.append(onward(c))
        if stage == 0:
            from_even = lax.ppermute(to_even[0], ("tm", "gx"), even_pairs)
    rest = first[-1][1:-1]
    g_rest, acc, *own, own_rest = call(
        middle_kernel,
        [grid(2 * len(rest)), grid(nx - 4), *[modes(part) for part in first[:-1]], modes(rest)],
        "middle",
        cost=0,
    )(a, mu, fz, fy, *g)
    mark = call(mark_kernel, jax.ShapeDtypeStruct((8, 128), F32), "mark", specs=[ANY, ANY])(from_odd, acc)
    ab, gb, c = call(outer_kernel, [grid(4), grid(4), modes(first[-1])], "outer", specs=[VMEM] * 7 + [ANY])(
        a, mu, from_even, from_odd, g_rest, fz, fy, mark
    )
    c1.append(onward(c))
    accb, own_last = call(later_kernel, [grid(4), modes(first[-1])], "later")(
        a, mu, ab, gb, g[0], g_rest, own_rest, fz, fy
    )
    own.append(own_last)
    a1, e, c2 = [], [], []
    for stage in range(count):
        values, end, c = call(
            functools.partial(second_kernel, stage),
            [grid(2 * len(first[stage])), grid(2 * len(second[stage])), modes(second[stage])],
            "second",
        )(a, ab, mu, acc, accb, c1[stage], own[stage], fz, fy, by, bz, *a1)
        a1.append(values)
        e.append(end)
        c2.append(onward(c))
    whole = jax.ShapeDtypeStruct((1, nx, ny, nz), F32)
    end_state = call(
        join_kernel,
        whole,
        "join",
        scratch=[pltpu.SemaphoreType.DMA((nx // 2,))],
        specs=[ANY] * count,
        out_specs=ANY,
    )(*e)
    result = []
    for stage, part in enumerate(second):
        result = [
            call(
                functools.partial(last_kernel, stage, count),
                whole,
                "last",
                scratch=[pltpu.VMEM((2 * len(part), ny, nz), F32), pltpu.SemaphoreType.DMA((len(part),))],
                specs=[VMEM] * (4 + 2 * count) + [ANY] * len(result),
                out_specs=ANY,
                aliases={4 + 2 * count: 0} if result else {},
            )(c2[stage], by, bz, a, *c1, *a1, *result)
        ]
    return end_state, result[0]


def solution(mesh):
    placed = (P("tm", "gx", None, None), P("gx", None, None))
    return jax.shard_map(
        body,
        mesh=mesh,
        in_specs=placed,
        out_specs=(P("tm", "gx", None, None), P("tm", "gx", None, None)),
        check_vma=False,
    )
```

```python
import functools
import math

import jax
import jax.numpy as jnp
import numpy as np
from jax import lax
from jax.experimental import pallas as pl
from jax.experimental.pallas import tpu as pltpu
from jax.sharding import PartitionSpec as P

KY = 64
KZ = 64
time_step = 0.05
F32 = jnp.float32
BF16 = jnp.bfloat16
VMEM_LIMIT = 24 * 2**20
COST = 10**8
ANY = pl.BlockSpec(memory_space=pl.ANY)
VMEM = pl.BlockSpec(memory_space=pltpu.VMEM)


def basis_value(node_times, source, point):
    total = 1.0
    for other in range(5):
        if other != source:
            total = total * (point - node_times[other]) / (node_times[source] - node_times[other])
    return total


def lobatto():
    root = math.sqrt(3.0 / 7.0)
    node_times = [0.0, (1.0 - root) / 2.0, 0.5, (1.0 + root) / 2.0, 1.0]
    gauss_points = [-math.sqrt(0.6), 0.0, math.sqrt(0.6)]
    gauss_weights = [5.0 / 9.0, 8.0 / 9.0, 5.0 / 9.0]
    last_row = []
    for source in range(5):
        integral = 0.0
        for point, weight in zip(gauss_points, gauss_weights):
            integral += 0.5 * weight * basis_value(node_times, source, 0.5 * (1.0 + point))
        last_row.append(integral)
    return node_times, last_row


NODE_TIMES, LAST_ROW = lobatto()
W = [sum(LAST_ROW[j] * NODE_TIMES[j] ** k for j in range(1, 5)) for k in range(4)]


def dct_rows(count, kept):
    freq = np.arange(kept, dtype=np.float64)[:, None]
    place = np.arange(count, dtype=np.float64)[None, :]
    matrix = np.cos(np.pi * (place + 0.5) * freq / count) * np.sqrt(2.0 / count)
    return np.where(freq == 0, matrix * np.sqrt(0.5), matrix)


def halves(matrix):
    high = matrix.astype(jnp.bfloat16)
    low = (matrix - high.astype(np.float64)).astype(jnp.bfloat16)
    return high, low


def tables(ny, nz):
    cy = dct_rows(ny, KY)
    cz = dct_rows(nz, KZ)
    twice = np.zeros((2 * nz, 2 * KZ))
    twice[:nz, :KZ] = cz.T
    twice[nz:, KZ:] = cz.T
    zh, zl = halves(twice)
    fz = np.concatenate([zh, zl], axis=1)
    yh, yl = halves(cy)
    fy = np.block([[yh, yh], [yl, np.zeros_like(yl)]])
    by = np.concatenate([yh.T, yh.T, yl.T], axis=1)
    bz = np.concatenate([zh.T, zh.T, zl.T], axis=0)
    return fz, fy, by, bz


def split(x):
    high = x.astype(BF16)
    return high, (x - high.astype(F32)).astype(BF16)


def dot(a, b):
    return jnp.dot(a, b, preferred_element_type=F32)


def neighbours(v):
    ny, nz = v.shape
    rows = lax.broadcasted_iota(jnp.int32, (8, nz), 0)
    lanes = lax.broadcasted_iota(jnp.int32, v.shape, 1)
    low = pltpu.roll(v, 1, 0)
    high = pltpu.roll(v, ny - 1, 0)
    low = jnp.concatenate([jnp.where(rows == 0, 0.0, low[:8]), low[8:]], axis=0)
    high = jnp.concatenate([high[: ny - 8], jnp.where(rows == 7, 0.0, high[ny - 8 :])], axis=0)
    left = jnp.where(lanes == 0, 0.0, pltpu.roll(v, 1, 1))
    right = jnp.where(lanes == nz - 1, 0.0, pltpu.roll(v, nz - 1, 1))
    return (low + high) + (left + right)


def rate(below, v, above, mobility):
    return mobility * (neighbours(v) + (below + above) - v * (5.0 + v * v))


def analyse_small(pairs, fz_ref, fy_ref):
    ny = pairs[0][0].shape[0]
    width = 2 * KZ
    rows = [jnp.concatenate([first.astype(BF16), second.astype(BF16)], axis=1) for first, second in pairs]
    half = dot(jnp.concatenate(rows, axis=0), fz_ref[...])
    half = (half[:, :width] + half[:, width:]).astype(BF16)
    columns = [half[i * ny : (i + 1) * ny] for i in range(len(pairs))]
    coeffs = dot(fy_ref[:, :ny], jnp.concatenate(columns, axis=1))
    return coeffs[:KY] + coeffs[KY:]


def analyse(pairs, fz_ref, fy_ref):
    rows = []
    for first, second in pairs:
        first_high, first_low = split(first)
        second_high, second_low = split(second)
        rows.append(jnp.concatenate([first_high, second_high, first_low, second_low], axis=1))
    rows = jnp.concatenate(rows, axis=0)
    width, nz = 2 * KZ, pairs[0][0].shape[1]
    half = dot(rows[:, : 2 * nz], fz_ref[...])
    half = half[:, :width] + half[:, width:] + dot(rows[:, 2 * nz :], fz_ref[:, :width])
    ny = pairs[0][0].shape[0]
    columns = []
    for i in range(len(pairs)):
        columns.append(jnp.concatenate(split(half[i * ny : (i + 1) * ny]), axis=0))
    coeffs = dot(fy_ref[...], jnp.concatenate(columns, axis=1))
    return coeffs[:KY] + coeffs[KY:]


def synthesise(coeffs, by_ref, bz_ref):
    high, low = split(coeffs)
    half = dot(by_ref[...], jnp.concatenate([high, low, high], axis=0))
    width = 2 * KZ
    count = coeffs.shape[1] // width
    rows = []
    for i in range(count):
        high, low = split(half[:, i * width : (i + 1) * width])
        rows.append(jnp.concatenate([high, low, high], axis=1))
    planes = dot(jnp.concatenate(rows, axis=0), bz_ref[...])
    ny = half.shape[0]
    return [planes[i * ny : (i + 1) * ny] for i in range(count)]


def call(kernel, outs, name, scratch=(), specs=None, out_specs=None, aliases={}, cost=COST):
    def run(*args):
        return pl.pallas_call(
            kernel,
            out_shape=outs,
            in_specs=specs or [VMEM] * len(args),
            out_specs=out_specs or jax.tree.map(lambda _: VMEM, outs),
            scratch_shapes=scratch,
            input_output_aliases=aliases,
            compiler_params=pltpu.CompilerParams(vmem_limit_bytes=VMEM_LIMIT),
            cost_estimate=pl.CostEstimate(flops=100 * cost, bytes_accessed=10 * cost, transcendentals=0),
            name=name,
        )(*args)

    return run


def chunks(nx):
    last = nx // 2
    early, soon = last - 3, last - 4
    first = [list(range(1, early + 1)), [0, *range(early + 1, last + 1)]]
    second = [list(range(1, soon + 1)), [0, *range(soon + 1, last)]]
    return first, second


def planes_of(pairs, shift):
    return [2 * t + shift + k for t in pairs for k in (0, 1)]


def outer_planes(nx):
    return [-1, 0, nx - 1, nx]


def reader(*parts):
    where = {}
    for ref, planes in parts:
        for i, p in enumerate(planes):
            where[p] = (ref, i)

    def read(p):
        ref, i = where[p]
        return ref[i]

    return read


def by_pairs(planes):
    return list(zip(planes[::2], planes[1::2]))


def is_even():
    return lax.rem(lax.axis_index("gx"), 2) == 0


def pack_kernel(a_ref, mu_ref, odd_ref, sems):
    nx = a_ref.shape[0]
    even = is_even()
    copies = [
        pltpu.make_async_copy(a_ref.at[pl.ds(jnp.where(even, 0, nx - 2), 2)], odd_ref.at[pl.ds(0, 2)], sems.at[0]),
        pltpu.make_async_copy(mu_ref.at[pl.ds(jnp.where(even, 0, nx - 1), 1)], odd_ref.at[pl.ds(2, 1)], sems.at[1]),
    ]
    for copy in copies:
        copy.start()
    for copy in copies:
        copy.wait()


def inner_kernel(stage, a_ref, mu_ref, fz_ref, fy_ref, after, g_ref, c_ref, *even_ref):
    ends = []
    for i, p in enumerate(planes_of(chunks(a_ref.shape[0])[0][stage], -1)):
        g = rate(a_ref[p - 1], a_ref[p], a_ref[p + 1], mu_ref[p])
        g_ref[i] = g
        ends.append(a_ref[p] + time_step * g)
    c_ref[...] = analyse(by_pairs(ends), fz_ref, fy_ref)
    if stage == 0:
        nx = a_ref.shape[0]
        even = is_even()
        even_ref[0][0] = jnp.where(even, a_ref[nx - 2], a_ref[0])
        even_ref[0][1] = jnp.where(even, a_ref[nx - 1], a_ref[1])
        even_ref[0][2] = jnp.where(even, mu_ref[nx - 1], mu_ref[0])


def later_part(below, g, above, a, mobility):
    h = time_step
    laplace = neighbours(g) + (below + above) - 5.0 * g
    hg = h * g
    cube = hg * (3.0 * W[1] * a * a + hg * (3.0 * W[2] * a + W[3] * hg))
    return h * (W[0] * g + mobility * (h * W[1] * laplace - cube))


def middle_kernel(a_ref, mu_ref, fz_ref, fy_ref, after, g_ref, c_ref, *own_refs):
    nx = a_ref.shape[0]
    first = chunks(nx)[0]
    ends = []
    for i, p in enumerate(planes_of(first[-1][1:-1], -1)):
        g = rate(a_ref[p - 1], a_ref[p], a_ref[p + 1], mu_ref[p])
        g_ref[i] = g
        ends.append(a_ref[p] + time_step * g)
    inner = sum(first[:-1], []) + first[-1][1:-1]
    coeffs = analyse(by_pairs(ends) + [(a_ref[p - 1], a_ref[p]) for p in planes_of(inner, -1)[1::2]], fz_ref, fy_ref)
    start = 0
    for ref in (c_ref, *own_refs):
        ref[...] = coeffs[:, start : start + ref.shape[1]]
        start += ref.shape[1]


def ends_between(c_ref, outer, rest_ref):
    width = 2 * KZ
    c_ref[:, :width] = outer[:, :width]
    c_ref[:, width : c_ref.shape[1] - width] = rest_ref[...]
    c_ref[:, c_ref.shape[1] - width :] = outer[:, width:]


def mark_kernel(from_odd, after, out_ref):
    out_ref[...] = jnp.zeros_like(out_ref)


def outer_kernel(a_ref, mu_ref, even_ref, odd_ref, rest_ref, fz_ref, fy_ref, after, a_out, g_out, c_ref):
    nx = a_ref.shape[0]
    even = is_even()
    place = lax.axis_index("gx")
    count = lax.axis_size("gx")
    keep_low = (place > 0).astype(F32)
    keep_high = (place < count - 1).astype(F32)
    low = [jnp.where(even, odd_ref[i], even_ref[i]) * keep_low for i in range(3)]
    high = [jnp.where(even, even_ref[i], odd_ref[i]) * keep_high for i in range(3)]
    starts = [low[0], low[1], a_ref[0], a_ref[1]]
    ends = [a_ref[nx - 2], a_ref[nx - 1], high[0], high[1]]
    values = starts[1:3] + ends[1:3]
    rates = [
        rate(starts[0], starts[1], starts[2], low[2]),
        rate(starts[1], starts[2], starts[3], mu_ref[0]),
        rate(ends[0], ends[1], ends[2], mu_ref[nx - 1]),
        rate(ends[1], ends[2], ends[3], high[2]),
    ]
    for i in range(4):
        a_out[i] = values[i]
        g_out[i] = rates[i]
    outer = [v + time_step * g for v, g in zip(values, rates)]
    ends_between(c_ref, analyse(by_pairs(outer), fz_ref, fy_ref), rest_ref)


def later_kernel(a_ref, mu_ref, ab_ref, gb_ref, rest_ref, fz_ref, fy_ref, *refs):
    g_refs, (acc_ref, c_ref, cacc_ref) = refs[:-3], refs[-3:]
    nx = a_ref.shape[0]
    first = chunks(nx)[0]
    inner = [planes_of(part, -1) for part in (*first[:-1], first[-1][1:-1])]
    rates = reader((gb_ref, outer_planes(nx)), *zip(g_refs, inner))
    ends_between(c_ref, analyse([(ab_ref[0], ab_ref[1]), (ab_ref[2], ab_ref[3])], fz_ref, fy_ref), rest_ref)
    for p in range(nx):
        acc_ref[p] = later_part(rates(p - 1), rates(p), rates(p + 1), a_ref[p], mu_ref[p])
    planes = planes_of(chunks(nx)[1][-1], 0)
    cacc_ref[...] = analyse(by_pairs([acc_ref[p] for p in planes]), fz_ref, fy_ref)


def received(c, own):
    return jnp.where(lax.axis_index("tm") > 0, c - own, 0.0)


def second_kernel(stage, *refs):
    a_ref, ab_ref, mu_ref, acc_ref, c1_ref, own_ref, fz_ref, fy_ref, by_ref, bz_ref = refs[:10]
    earlier, (a1_ref, e_ref, c2_ref) = refs[10:-3], refs[-3:]
    if stage == 1:
        earlier, (cacc_ref, c1_first_ref, own_first_ref) = earlier[:1], earlier[1:]
    nx, ny, nz = mu_ref.shape
    first, second = chunks(nx)
    before = reader((a_ref, range(nx)), (ab_ref, outer_planes(nx)))
    receives = lax.axis_index("tm") > 0

    @pl.when(receives)
    def _():
        change = synthesise(c1_ref[...] - own_ref[...], by_ref, bz_ref)
        for i, p in enumerate(planes_of(first[stage], -1)):
            a1_ref[i] = before(p) + change[i // 2][:, (i % 2) * nz : (i % 2 + 1) * nz]

    @pl.when(jnp.logical_not(receives))
    def _():
        for i, p in enumerate(planes_of(first[stage], -1)):
            a1_ref[i] = before(p)

    values = reader(*[(ref, planes_of(part, -1)) for ref, part in zip((*earlier, a1_ref), first)])
    planes = planes_of(second[stage], 0)
    fresh = [rate(values(p - 1), values(p), values(p + 1), mu_ref[p]) for p in planes]
    weight = time_step * LAST_ROW[0]
    ends = [values(p) + weight * f + acc_ref[p] for p, f in zip(planes, fresh)]
    for i, e in enumerate(ends):
        e_ref[i] = e
    if stage == 0:
        c2_ref[...] = analyse(by_pairs(ends), fz_ref, fy_ref)
        return
    where = {}
    for c, own, part in ((c1_first_ref, own_first_ref, first[0]), (c1_ref, own_ref, first[1])):
        own_start = jnp.where(receives, c[...], own[...])
        for i, p in enumerate(planes_of(part, -1)):
            where[p] = own_start[:, i * KZ : (i + 1) * KZ]
    known = jnp.concatenate([where[p] for p in planes], axis=1) + cacc_ref[...]
    c2_ref[...] = known + weight * analyse_small(by_pairs(fresh), fz_ref, fy_ref)


def last_kernel(stage, count, *refs):
    c2_ref, by_ref, bz_ref, a_ref = refs[:4]
    c1_refs, a1_refs = refs[4 : 4 + count], refs[4 + count : 4 + 2 * count]
    out_ref, buffer, sems = refs[-3:]
    nx, ny, nz = out_ref.shape[1:]
    first, second = chunks(nx)
    where = {}
    for ref, part in zip(c1_refs, first):
        for i, p in enumerate(planes_of(part, -1)):
            where[p] = (ref, i)

    def column(p):
        ref, i = where[p]
        return ref[:, i * KZ : (i + 1) * KZ]

    receives = lax.axis_index("tm") > 0

    @pl.when(receives)
    def _():
        values = reader(*[(ref, planes_of(part, -1)) for ref, part in zip(a1_refs, first)])
        planes = planes_of(second[stage], 0)
        before = jnp.concatenate([column(p) for p in planes], axis=1)
        change = synthesise(c2_ref[...] - before, by_ref, bz_ref)
        copies = []
        for i in range(0, len(planes), 2):
            for k in (0, 1):
                buffer[i + k] = values(planes[i + k]) + change[i // 2][:, k * nz : (k + 1) * nz]
            copy = pltpu.make_async_copy(
                buffer.at[pl.ds(i, 2)], out_ref.at[0, pl.ds(planes[i], 2)], sems.at[i // 2]
            )
            copy.start()
            copies.append(copy)
        for copy in copies:
            copy.wait()

    if stage == 0:

        @pl.when(jnp.logical_not(receives))
        def _():
            half = nx // 2
            copies = [
                pltpu.make_async_copy(a_ref.at[pl.ds(i * half, half)], out_ref.at[0, pl.ds(i * half, half)], sems.at[i])
                for i in range(2)
            ]
            for copy in copies:
                copy.start()
            for copy in copies:
                copy.wait()


def join_kernel(*refs):
    parts, out_ref, sems = refs[:-2], refs[-2], refs[-1]
    copies = []
    for ref, part in zip(parts, chunks(out_ref.shape[1])[1]):
        for i, p in enumerate(planes_of(part, 0)[::2]):
            copies.append(
                pltpu.make_async_copy(ref.at[pl.ds(2 * i, 2)], out_ref.at[0, pl.ds(p, 2)], sems.at[len(copies)])
            )
    for copy in copies:
        copy.start()
    for copy in copies:
        copy.wait()


def body(start_states, mobility):
    nx, ny, nz = mobility.shape
    slices, slabs = lax.axis_size("tm"), lax.axis_size("gx")
    a, mu = start_states[0], mobility
    fz, fy, by, bz = map(jnp.asarray, tables(ny, nz))
    first, second = chunks(nx)
    count = len(first)

    def grid(planes):
        return jax.ShapeDtypeStruct((planes, ny, nz), F32)

    def modes(pairs):
        return jax.ShapeDtypeStruct((KY, len(pairs) * 2 * KZ), F32)

    even_pairs = [(s * slabs + g, s * slabs + (g ^ 1)) for s in range(slices) for g in range(slabs)]
    odd_pairs = []
    for s in range(slices):
        for g in range(slabs):
            other = g + 1 if g % 2 else g - 1
            if 0 <= other < slabs:
                odd_pairs.append((s * slabs + g, s * slabs + other))
            else:
                odd_pairs.append((s * slabs + g, (s ^ (1 if g else 2)) * slabs + g))
    ring = [(s, (s + 1) % slices) for s in range(slices)]

    def onward(c):
        return lax.ppermute(c, "tm", ring)

    to_odd = call(pack_kernel, grid(3), "pack", scratch=[pltpu.SemaphoreType.DMA((2,))], specs=[ANY] * 2)(
        *[pltpu.with_memory_space_constraint(x, pltpu.HBM) for x in (a, mu)]
    )
    from_odd = lax.ppermute(to_odd, ("tm", "gx"), odd_pairs)
    g, c1 = [], []
    for stage, part in enumerate(first[:-1]):
        rates, c, *to_even = call(
            functools.partial(inner_kernel, stage),
            [grid(2 * len(part)), modes(part)] + [grid(3)] * (stage == 0),
            "inner",
            specs=[VMEM] * 4 + [ANY],
        )(a, mu, fz, fy, to_odd)
        g.append(rates)
        c1.append(onward(c))
        if stage == 0:
            from_even = lax.ppermute(to_even[0], ("tm", "gx"), even_pairs)
    rest = first[-1][1:-1]
    g_rest, c_rest, *own, own_rest = call(
        middle_kernel,
        [grid(2 * len(rest)), modes(rest), *[modes(part) for part in first[:-1]], modes(rest)],
        "middle",
        specs=[VMEM] * 4 + [ANY],
        cost=0,
    )(a, mu, fz, fy, g[-1])
    mark = call(mark_kernel, jax.ShapeDtypeStruct((8, 128), F32), "mark", specs=[ANY, ANY])(from_odd, own_rest)
    ab, gb, c = call(outer_kernel, [grid(4), grid(4), modes(first[-1])], "outer", specs=[VMEM] * 7 + [ANY])(
        a, mu, from_even, from_odd, c_rest, fz, fy, mark
    )
    c1.append(onward(c))
    acc, own_last, cacc = call(later_kernel, [grid(nx), modes(first[-1]), modes(second[-1])], "later")(
        a, mu, ab, gb, own_rest, fz, fy, *g, g_rest
    )
    own.append(own_last)
    a1, e, c2 = [], [], []
    for stage in range(count):
        values, end, c = call(
            functools.partial(second_kernel, stage),
            [grid(2 * len(first[stage])), grid(2 * len(second[stage])), modes(second[stage])],
            "second",
        )(a, ab, mu, acc, c1[stage], own[stage], fz, fy, by, bz, *a1, *([cacc, c1[0], own[0]] if stage else []))
        a1.append(values)
        e.append(end)
        c2.append(onward(c))
    whole = jax.ShapeDtypeStruct((1, nx, ny, nz), F32)
    end_state = call(
        join_kernel,
        whole,
        "join",
        scratch=[pltpu.SemaphoreType.DMA((nx // 2,))],
        specs=[ANY] * count,
        out_specs=ANY,
    )(*e)
    result = []
    for stage, part in enumerate(second):
        result = [
            call(
                functools.partial(last_kernel, stage, count),
                whole,
                "last",
                scratch=[pltpu.VMEM((2 * len(part), ny, nz), F32), pltpu.SemaphoreType.DMA((len(part),))],
                specs=[VMEM] * (4 + 2 * count) + [ANY] * len(result),
                out_specs=ANY,
                aliases={4 + 2 * count: 0} if result else {},
            )(c2[stage], by, bz, a, *c1, *a1, *result)
        ]
    return end_state, result[0]


def solution(mesh):
    placed = (P("tm", "gx", None, None), P("gx", None, None))
    return jax.shard_map(
        body,
        mesh=mesh,
        in_specs=placed,
        out_specs=(P("tm", "gx", None, None), P("tm", "gx", None, None)),
        check_vma=False,
    )
```

```python
import functools
import math

import jax
import jax.numpy as jnp
import numpy as np
from jax import lax
from jax.experimental import pallas as pl
from jax.experimental.pallas import tpu as pltpu
from jax.sharding import PartitionSpec as P

KY = 64
KZ = 64
time_step = 0.05
F32 = jnp.float32
BF16 = jnp.bfloat16
VMEM_LIMIT = 24 * 2**20
COST = 10**8
ANY = pl.BlockSpec(memory_space=pl.ANY)
VMEM = pl.BlockSpec(memory_space=pltpu.VMEM)


def basis_value(node_times, source, point):
    total = 1.0
    for other in range(5):
        if other != source:
            total = total * (point - node_times[other]) / (node_times[source] - node_times[other])
    return total


def lobatto():
    root = math.sqrt(3.0 / 7.0)
    node_times = [0.0, (1.0 - root) / 2.0, 0.5, (1.0 + root) / 2.0, 1.0]
    gauss_points = [-math.sqrt(0.6), 0.0, math.sqrt(0.6)]
    gauss_weights = [5.0 / 9.0, 8.0 / 9.0, 5.0 / 9.0]
    last_row = []
    for source in range(5):
        integral = 0.0
        for point, weight in zip(gauss_points, gauss_weights):
            integral += 0.5 * weight * basis_value(node_times, source, 0.5 * (1.0 + point))
        last_row.append(integral)
    return node_times, last_row


NODE_TIMES, LAST_ROW = lobatto()
W = [sum(LAST_ROW[j] * NODE_TIMES[j] ** k for j in range(1, 5)) for k in range(4)]


def dct_rows(count, kept):
    freq = np.arange(kept, dtype=np.float64)[:, None]
    place = np.arange(count, dtype=np.float64)[None, :]
    matrix = np.cos(np.pi * (place + 0.5) * freq / count) * np.sqrt(2.0 / count)
    return np.where(freq == 0, matrix * np.sqrt(0.5), matrix)


def halves(matrix):
    high = matrix.astype(jnp.bfloat16)
    low = (matrix - high.astype(np.float64)).astype(jnp.bfloat16)
    return high, low


def tables(ny, nz):
    cy = dct_rows(ny, KY)
    cz = dct_rows(nz, KZ)
    twice = np.zeros((2 * nz, 2 * KZ))
    twice[:nz, :KZ] = cz.T
    twice[nz:, KZ:] = cz.T
    zh, zl = halves(twice)
    fz = np.concatenate([zh, zl], axis=1)
    yh, yl = halves(cy)
    fy = np.block([[yh, yh], [yl, np.zeros_like(yl)]])
    by = np.concatenate([yh.T, yh.T, yl.T], axis=1)
    bz = np.concatenate([zh.T, zh.T, zl.T], axis=0)
    return fz, fy, by, bz


def split(x):
    high = x.astype(BF16)
    return high, (x - high.astype(F32)).astype(BF16)


def dot(a, b):
    return jnp.dot(a, b, preferred_element_type=F32)


def neighbours(v):
    ny, nz = v.shape
    rows = lax.broadcasted_iota(jnp.int32, (8, nz), 0)
    lanes = lax.broadcasted_iota(jnp.int32, v.shape, 1)
    low = pltpu.roll(v, 1, 0)
    high = pltpu.roll(v, ny - 1, 0)
    low = jnp.concatenate([jnp.where(rows == 0, 0.0, low[:8]), low[8:]], axis=0)
    high = jnp.concatenate([high[: ny - 8], jnp.where(rows == 7, 0.0, high[ny - 8 :])], axis=0)
    left = jnp.where(lanes == 0, 0.0, pltpu.roll(v, 1, 1))
    right = jnp.where(lanes == nz - 1, 0.0, pltpu.roll(v, nz - 1, 1))
    return (low + high) + (left + right)


def rate(below, v, above, mobility):
    return mobility * (neighbours(v) + (below + above) - v * (5.0 + v * v))


def analyse(pairs, fz_ref, fy_ref):
    rows = []
    for first, second in pairs:
        first_high, first_low = split(first)
        second_high, second_low = split(second)
        rows.append(jnp.concatenate([first_high, second_high, first_low, second_low], axis=1))
    rows = jnp.concatenate(rows, axis=0)
    width, nz = 2 * KZ, pairs[0][0].shape[1]
    half = dot(rows[:, : 2 * nz], fz_ref[...])
    half = half[:, :width] + half[:, width:] + dot(rows[:, 2 * nz :], fz_ref[:, :width])
    ny = pairs[0][0].shape[0]
    columns = []
    for i in range(len(pairs)):
        columns.append(jnp.concatenate(split(half[i * ny : (i + 1) * ny]), axis=0))
    coeffs = dot(fy_ref[...], jnp.concatenate(columns, axis=1))
    return coeffs[:KY] + coeffs[KY:]


def synthesise(coeffs, by_ref, bz_ref):
    high, low = split(coeffs)
    half = dot(by_ref[...], jnp.concatenate([high, low, high], axis=0))
    width = 2 * KZ
    count = coeffs.shape[1] // width
    rows = []
    for i in range(count):
        high, low = split(half[:, i * width : (i + 1) * width])
        rows.append(jnp.concatenate([high, low, high], axis=1))
    planes = dot(jnp.concatenate(rows, axis=0), bz_ref[...])
    ny = half.shape[0]
    return [planes[i * ny : (i + 1) * ny] for i in range(count)]


def call(kernel, outs, name, scratch=(), specs=None, out_specs=None, aliases={}, cost=COST):
    def run(*args):
        return pl.pallas_call(
            kernel,
            out_shape=outs,
            in_specs=specs or [VMEM] * len(args),
            out_specs=out_specs or jax.tree.map(lambda _: VMEM, outs),
            scratch_shapes=scratch,
            input_output_aliases=aliases,
            compiler_params=pltpu.CompilerParams(vmem_limit_bytes=VMEM_LIMIT),
            cost_estimate=pl.CostEstimate(flops=100 * cost, bytes_accessed=10 * cost, transcendentals=0),
            name=name,
        )(*args)

    return run


def chunks(nx):
    last = nx // 2
    early, soon = last - 3, last - 4
    first = [list(range(1, early + 1)), [0, *range(early + 1, last + 1)]]
    second = [list(range(1, soon + 1)), [0, *range(soon + 1, last)]]
    return first, second


def planes_of(pairs, shift):
    return [2 * t + shift + k for t in pairs for k in (0, 1)]


def outer_planes(nx):
    return [-1, 0, nx - 1, nx]


def reader(*parts):
    where = {}
    for ref, planes in parts:
        for i, p in enumerate(planes):
            where[p] = (ref, i)

    def read(p):
        ref, i = where[p]
        return ref[i]

    return read


def by_pairs(planes):
    return list(zip(planes[::2], planes[1::2]))


def is_even():
    return lax.rem(lax.axis_index("gx"), 2) == 0


def pack_kernel(a_ref, mu_ref, odd_ref, sems):
    nx = a_ref.shape[0]
    even = is_even()
    copies = [
        pltpu.make_async_copy(a_ref.at[pl.ds(jnp.where(even, 0, nx - 2), 2)], odd_ref.at[pl.ds(0, 2)], sems.at[0]),
        pltpu.make_async_copy(mu_ref.at[pl.ds(jnp.where(even, 0, nx - 1), 1)], odd_ref.at[pl.ds(2, 1)], sems.at[1]),
    ]
    for copy in copies:
        copy.start()
    for copy in copies:
        copy.wait()


def inner_kernel(stage, a_ref, mu_ref, fz_ref, fy_ref, after, g_ref, c_ref, *even_ref):
    ends = []
    for i, p in enumerate(planes_of(chunks(a_ref.shape[0])[0][stage], -1)):
        g = rate(a_ref[p - 1], a_ref[p], a_ref[p + 1], mu_ref[p])
        g_ref[i] = g
        ends.append(a_ref[p] + time_step * g)
    c_ref[...] = analyse(by_pairs(ends), fz_ref, fy_ref)
    if stage == 0:
        nx = a_ref.shape[0]
        even = is_even()
        even_ref[0][0] = jnp.where(even, a_ref[nx - 2], a_ref[0])
        even_ref[0][1] = jnp.where(even, a_ref[nx - 1], a_ref[1])
        even_ref[0][2] = jnp.where(even, mu_ref[nx - 1], mu_ref[0])


def later_part(below, g, above, a, mobility):
    h = time_step
    laplace = neighbours(g) + (below + above) - 5.0 * g
    hg = h * g
    cube = hg * (3.0 * W[1] * a * a + hg * (3.0 * W[2] * a + W[3] * hg))
    return h * (W[0] * g + mobility * (h * W[1] * laplace - cube))


def middle_kernel(a_ref, mu_ref, fz_ref, fy_ref, *refs):
    nx = a_ref.shape[0]
    first = chunks(nx)[0]
    early = [planes_of(part, -1) for part in first[:-1]]
    g_refs, (g_ref, acc_ref), own_refs = refs[: len(early)], refs[len(early) : len(early) + 2], refs[len(early) + 2 :]
    rest = planes_of(first[-1][1:-1], -1)
    for i, p in enumerate(rest):
        g_ref[i] = rate(a_ref[p - 1], a_ref[p], a_ref[p + 1], mu_ref[p])
    rates = reader(*zip(g_refs, early), (g_ref, rest))
    inner = sum(first[:-1], []) + first[-1][1:-1]
    coeffs = analyse([(a_ref[p - 1], a_ref[p]) for p in planes_of(inner, -1)[1::2]], fz_ref, fy_ref)
    start = 0
    for ref in own_refs:
        ref[...] = coeffs[:, start : start + ref.shape[1]]
        start += ref.shape[1]
    for p in range(2, nx - 2):
        acc_ref[p - 2] = later_part(rates(p - 1), rates(p), rates(p + 1), a_ref[p], mu_ref[p])


def mark_kernel(from_odd, after, out_ref):
    out_ref[...] = jnp.zeros_like(out_ref)


def outer_kernel(a_ref, mu_ref, even_ref, odd_ref, g_ref, fz_ref, fy_ref, after, a_out, g_out, c_ref):
    nx = a_ref.shape[0]
    even = is_even()
    place = lax.axis_index("gx")
    count = lax.axis_size("gx")
    keep_low = (place > 0).astype(F32)
    keep_high = (place < count - 1).astype(F32)
    low = [jnp.where(even, odd_ref[i], even_ref[i]) * keep_low for i in range(3)]
    high = [jnp.where(even, even_ref[i], odd_ref[i]) * keep_high for i in range(3)]
    starts = [low[0], low[1], a_ref[0], a_ref[1]]
    ends = [a_ref[nx - 2], a_ref[nx - 1], high[0], high[1]]
    values = starts[1:3] + ends[1:3]
    rates = [
        rate(starts[0], starts[1], starts[2], low[2]),
        rate(starts[1], starts[2], starts[3], mu_ref[0]),
        rate(ends[0], ends[1], ends[2], mu_ref[nx - 1]),
        rate(ends[1], ends[2], ends[3], high[2]),
    ]
    for i in range(4):
        a_out[i] = values[i]
        g_out[i] = rates[i]
    outer = [v + time_step * g for v, g in zip(values, rates)]
    rest = planes_of(chunks(nx)[0][-1][1:-1], -1)
    inner = [a_ref[p] + time_step * g_ref[i] for i, p in enumerate(rest)]
    c_ref[...] = analyse(by_pairs(outer[:2] + inner + outer[2:]), fz_ref, fy_ref)


def later_kernel(a_ref, mu_ref, ab_ref, gb_ref, low_ref, high_ref, rest_ref, fz_ref, fy_ref, acc_ref, c_ref):
    nx = a_ref.shape[0]
    first = chunks(nx)[0]
    rates = reader(
        (gb_ref, outer_planes(nx)), (low_ref, planes_of(first[0], -1)), (high_ref, planes_of(first[-1][1:-1], -1))
    )
    own = analyse([(ab_ref[0], ab_ref[1]), (ab_ref[2], ab_ref[3])], fz_ref, fy_ref)
    width = 2 * KZ
    c_ref[:, :width] = own[:, :width]
    c_ref[:, width : c_ref.shape[1] - width] = rest_ref[...]
    c_ref[:, c_ref.shape[1] - width :] = own[:, width:]
    for i, p in enumerate((0, 1, nx - 2, nx - 1)):
        acc_ref[i] = later_part(rates(p - 1), rates(p), rates(p + 1), a_ref[p], mu_ref[p])


def received(c, own):
    return jnp.where(lax.axis_index("tm") > 0, c - own, 0.0)


def second_kernel(stage, *refs):
    a_ref, ab_ref, mu_ref, acc_ref, accb_ref, c1_ref, own_ref, fz_ref, fy_ref, by_ref, bz_ref = refs[:11]
    earlier, (a1_ref, e_ref, c2_ref) = refs[11:-3], refs[-3:]
    nx, ny, nz = mu_ref.shape
    first, second = chunks(nx)
    before = reader((a_ref, range(nx)), (ab_ref, outer_planes(nx)))
    receives = lax.axis_index("tm") > 0

    @pl.when(receives)
    def _():
        change = synthesise(c1_ref[...] - own_ref[...], by_ref, bz_ref)
        for i, p in enumerate(planes_of(first[stage], -1)):
            a1_ref[i] = before(p) + change[i // 2][:, (i % 2) * nz : (i % 2 + 1) * nz]

    @pl.when(jnp.logical_not(receives))
    def _():
        for i, p in enumerate(planes_of(first[stage], -1)):
            a1_ref[i] = before(p)

    values = reader(*[(ref, planes_of(part, -1)) for ref, part in zip((*earlier, a1_ref), first)])
    parts = reader((acc_ref, range(2, nx - 2)), (accb_ref, (0, 1, nx - 2, nx - 1)))
    ends = []
    for i, p in enumerate(planes_of(second[stage], 0)):
        v = values(p)
        e = v + time_step * LAST_ROW[0] * rate(values(p - 1), v, values(p + 1), mu_ref[p]) + parts(p)
        e_ref[i] = e
        ends.append(e)
    c2_ref[...] = analyse(by_pairs(ends), fz_ref, fy_ref)


def last_kernel(stage, count, *refs):
    c2_ref, by_ref, bz_ref, a_ref = refs[:4]
    before_ref, a1_refs = refs[4], refs[5 : 5 + count]
    out_ref, buffer, sems = refs[-3:]
    nx, ny, nz = out_ref.shape[1:]
    first, second = chunks(nx)
    receives = lax.axis_index("tm") > 0

    @pl.when(receives)
    def _():
        values = reader(*[(ref, planes_of(part, -1)) for ref, part in zip(a1_refs, first)])
        planes = planes_of(second[stage], 0)
        change = synthesise(c2_ref[...] - before_ref[...], by_ref, bz_ref)
        copies = []
        for i in range(0, len(planes), 2):
            for k in (0, 1):
                buffer[i + k] = values(planes[i + k]) + change[i // 2][:, k * nz : (k + 1) * nz]
            copy = pltpu.make_async_copy(
                buffer.at[pl.ds(i, 2)], out_ref.at[0, pl.ds(planes[i], 2)], sems.at[i // 2]
            )
            copy.start()
            copies.append(copy)
        for copy in copies:
            copy.wait()

    if stage == 0:

        @pl.when(jnp.logical_not(receives))
        def _():
            half = nx // 2
            copies = [
                pltpu.make_async_copy(a_ref.at[pl.ds(i * half, half)], out_ref.at[0, pl.ds(i * half, half)], sems.at[i])
                for i in range(2)
            ]
            for copy in copies:
                copy.start()
            for copy in copies:
                copy.wait()


def join_kernel(count, *refs):
    parts, c1_refs = refs[:count], refs[count : 2 * count]
    out_ref, before_refs, sems = refs[2 * count], refs[2 * count + 1 : -1], refs[-1]
    first, second = chunks(out_ref.shape[1])
    copies = []
    for ref, part in zip(parts, second):
        for i, p in enumerate(planes_of(part, 0)[::2]):
            copies.append(
                pltpu.make_async_copy(ref.at[pl.ds(2 * i, 2)], out_ref.at[0, pl.ds(p, 2)], sems.at[len(copies)])
            )
    for copy in copies:
        copy.start()
    columns = {}
    for ref, part in zip(c1_refs, first):
        for i, p in enumerate(planes_of(part, -1)):
            columns[p] = ref[:, i * KZ : (i + 1) * KZ]
    for ref, part in zip(before_refs, second):
        ref[...] = jnp.concatenate([columns[p] for p in planes_of(part, 0)], axis=1)
    for copy in copies:
        copy.wait()


def body(start_states, mobility):
    nx, ny, nz = mobility.shape
    slices, slabs = lax.axis_size("tm"), lax.axis_size("gx")
    a, mu = start_states[0], mobility
    fz, fy, by, bz = map(jnp.asarray, tables(ny, nz))
    first, second = chunks(nx)
    count = len(first)

    def grid(planes):
        return jax.ShapeDtypeStruct((planes, ny, nz), F32)

    def modes(pairs):
        return jax.ShapeDtypeStruct((KY, len(pairs) * 2 * KZ), F32)

    even_pairs = [(s * slabs + g, s * slabs + (g ^ 1)) for s in range(slices) for g in range(slabs)]
    odd_pairs = []
    for s in range(slices):
        for g in range(slabs):
            other = g + 1 if g % 2 else g - 1
            if 0 <= other < slabs:
                odd_pairs.append((s * slabs + g, s * slabs + other))
            else:
                odd_pairs.append((s * slabs + g, (s ^ 2) * slabs + g))
    ring = [(s, (s + 1) % slices) for s in range(slices)]

    def onward(c):
        return lax.ppermute(c, "tm", ring)

    to_odd = call(pack_kernel, grid(3), "pack", scratch=[pltpu.SemaphoreType.DMA((2,))], specs=[ANY] * 2)(
        *[pltpu.with_memory_space_constraint(x, pltpu.HBM) for x in (a, mu)]
    )
    from_odd = lax.ppermute(to_odd, ("tm", "gx"), odd_pairs)
    g, c1 = [], []
    for stage, part in enumerate(first[:-1]):
        rates, c, *to_even = call(
            functools.partial(inner_kernel, stage),
            [grid(2 * len(part)), modes(part)] + [grid(3)] * (stage == 0),
            "inner",
            specs=[VMEM] * 4 + [ANY],
        )(a, mu, fz, fy, to_odd)
        g.append(rates)
        c1.append(onward(c))
        if stage == 0:
            from_even = lax.ppermute(to_even[0], ("tm", "gx"), even_pairs)
    rest = first[-1][1:-1]
    g_rest, acc, *own, own_rest = call(
        middle_kernel,
        [grid(2 * len(rest)), grid(nx - 4), *[modes(part) for part in first[:-1]], modes(rest)],
        "middle",
        cost=0,
    )(a, mu, fz, fy, *g)
    mark = call(mark_kernel, jax.ShapeDtypeStruct((8, 128), F32), "mark", specs=[ANY, ANY])(from_odd, acc)
    ab, gb, c = call(outer_kernel, [grid(4), grid(4), modes(first[-1])], "outer", specs=[VMEM] * 7 + [ANY])(
        a, mu, from_even, from_odd, g_rest, fz, fy, mark
    )
    c1.append(onward(c))
    accb, own_last = call(later_kernel, [grid(4), modes(first[-1])], "later")(
        a, mu, ab, gb, g[0], g_rest, own_rest, fz, fy
    )
    own.append(own_last)
    a1, e, c2 = [], [], []
    for stage in range(count):
        values, end, c = call(
            functools.partial(second_kernel, stage),
            [grid(2 * len(first[stage])), grid(2 * len(second[stage])), modes(second[stage])],
            "second",
        )(a, ab, mu, acc, accb, c1[stage], own[stage], fz, fy, by, bz, *a1)
        a1.append(values)
        e.append(end)
        c2.append(onward(c))
    whole = jax.ShapeDtypeStruct((1, nx, ny, nz), F32)
    end_state, *before = call(
        functools.partial(join_kernel, count),
        [whole, *[modes(part) for part in second]],
        "join",
        scratch=[pltpu.SemaphoreType.DMA((nx // 2,))],
        specs=[ANY] * count + [VMEM] * count,
        out_specs=[ANY] + [VMEM] * count,
    )(*e, *c1)
    result = []
    for stage, part in enumerate(second):
        result = [
            call(
                functools.partial(last_kernel, stage, count),
                whole,
                "last",
                scratch=[pltpu.VMEM((2 * len(part), ny, nz), F32), pltpu.SemaphoreType.DMA((len(part),))],
                specs=[VMEM] * (5 + count) + [ANY] * len(result),
                out_specs=ANY,
                aliases={5 + count: 0} if result else {},
            )(c2[stage], by, bz, a, before[stage], *a1, *result)
        ]
    return end_state, result[0]


def solution(mesh):
    placed = (P("tm", "gx", None, None), P("gx", None, None))
    return jax.shard_map(
        body,
        mesh=mesh,
        in_specs=placed,
        out_specs=(P("tm", "gx", None, None), P("tm", "gx", None, None)),
        check_vma=False,
    )
```

```python
import functools
import math

import jax
import jax.numpy as jnp
import numpy as np
from jax import lax
from jax.experimental import pallas as pl
from jax.experimental.pallas import tpu as pltpu
from jax.sharding import PartitionSpec as P

KY = 64
KZ = 64
time_step = 0.05
F32 = jnp.float32
BF16 = jnp.bfloat16
VMEM_LIMIT = 24 * 2**20
COST = 10**8
ANY = pl.BlockSpec(memory_space=pl.ANY)
VMEM = pl.BlockSpec(memory_space=pltpu.VMEM)


def basis_value(node_times, source, point):
    total = 1.0
    for other in range(5):
        if other != source:
            total = total * (point - node_times[other]) / (node_times[source] - node_times[other])
    return total


def lobatto():
    root = math.sqrt(3.0 / 7.0)
    node_times = [0.0, (1.0 - root) / 2.0, 0.5, (1.0 + root) / 2.0, 1.0]
    gauss_points = [-math.sqrt(0.6), 0.0, math.sqrt(0.6)]
    gauss_weights = [5.0 / 9.0, 8.0 / 9.0, 5.0 / 9.0]
    last_row = []
    for source in range(5):
        integral = 0.0
        for point, weight in zip(gauss_points, gauss_weights):
            integral += 0.5 * weight * basis_value(node_times, source, 0.5 * (1.0 + point))
        last_row.append(integral)
    return node_times, last_row


NODE_TIMES, LAST_ROW = lobatto()
W = [sum(LAST_ROW[j] * NODE_TIMES[j] ** k for j in range(1, 5)) for k in range(4)]


def dct_rows(count, kept):
    freq = np.arange(kept, dtype=np.float64)[:, None]
    place = np.arange(count, dtype=np.float64)[None, :]
    matrix = np.cos(np.pi * (place + 0.5) * freq / count) * np.sqrt(2.0 / count)
    return np.where(freq == 0, matrix * np.sqrt(0.5), matrix)


def halves(matrix):
    high = matrix.astype(jnp.bfloat16)
    low = (matrix - high.astype(np.float64)).astype(jnp.bfloat16)
    return high, low


def tables(ny, nz):
    cy = dct_rows(ny, KY)
    cz = dct_rows(nz, KZ)
    twice = np.zeros((2 * nz, 2 * KZ))
    twice[:nz, :KZ] = cz.T
    twice[nz:, KZ:] = cz.T
    zh, zl = halves(twice)
    fz = np.concatenate([zh, zl], axis=1)
    yh, yl = halves(cy)
    fy = np.block([[yh, yh], [yl, np.zeros_like(yl)]])
    by = np.concatenate([yh.T, yh.T, yl.T], axis=1)
    bz = np.concatenate([zh.T, zh.T, zl.T], axis=0)
    return fz, fy, by, bz


def split(x):
    high = x.astype(BF16)
    return high, (x - high.astype(F32)).astype(BF16)


def dot(a, b):
    return jnp.dot(a, b, preferred_element_type=F32)


def neighbours(v):
    ny, nz = v.shape
    rows = lax.broadcasted_iota(jnp.int32, (8, nz), 0)
    lanes = lax.broadcasted_iota(jnp.int32, v.shape, 1)
    low = pltpu.roll(v, 1, 0)
    high = pltpu.roll(v, ny - 1, 0)
    low = jnp.concatenate([jnp.where(rows == 0, 0.0, low[:8]), low[8:]], axis=0)
    high = jnp.concatenate([high[: ny - 8], jnp.where(rows == 7, 0.0, high[ny - 8 :])], axis=0)
    left = jnp.where(lanes == 0, 0.0, pltpu.roll(v, 1, 1))
    right = jnp.where(lanes == nz - 1, 0.0, pltpu.roll(v, nz - 1, 1))
    return (low + high) + (left + right)


def rate(below, v, above, mobility):
    return mobility * (neighbours(v) + (below + above) - v * (5.0 + v * v))


def analyse_small(pairs, fz_ref, fy_ref):
    ny = pairs[0][0].shape[0]
    width = 2 * KZ
    rows = [jnp.concatenate([first.astype(BF16), second.astype(BF16)], axis=1) for first, second in pairs]
    half = dot(jnp.concatenate(rows, axis=0), fz_ref[...])
    half = (half[:, :width] + half[:, width:]).astype(BF16)
    columns = [half[i * ny : (i + 1) * ny] for i in range(len(pairs))]
    coeffs = dot(fy_ref[:, :ny], jnp.concatenate(columns, axis=1))
    return coeffs[:KY] + coeffs[KY:]


def analyse(pairs, fz_ref, fy_ref):
    rows = []
    for first, second in pairs:
        first_high, first_low = split(first)
        second_high, second_low = split(second)
        rows.append(jnp.concatenate([first_high, second_high, first_low, second_low], axis=1))
    rows = jnp.concatenate(rows, axis=0)
    width, nz = 2 * KZ, pairs[0][0].shape[1]
    half = dot(rows[:, : 2 * nz], fz_ref[...])
    half = half[:, :width] + half[:, width:] + dot(rows[:, 2 * nz :], fz_ref[:, :width])
    ny = pairs[0][0].shape[0]
    columns = []
    for i in range(len(pairs)):
        columns.append(jnp.concatenate(split(half[i * ny : (i + 1) * ny]), axis=0))
    coeffs = dot(fy_ref[...], jnp.concatenate(columns, axis=1))
    return coeffs[:KY] + coeffs[KY:]


def synthesise(coeffs, by_ref, bz_ref):
    high, low = split(coeffs)
    half = dot(by_ref[...], jnp.concatenate([high, low, high], axis=0))
    width = 2 * KZ
    count = coeffs.shape[1] // width
    rows = []
    for i in range(count):
        high, low = split(half[:, i * width : (i + 1) * width])
        rows.append(jnp.concatenate([high, low, high], axis=1))
    planes = dot(jnp.concatenate(rows, axis=0), bz_ref[...])
    ny = half.shape[0]
    return [planes[i * ny : (i + 1) * ny] for i in range(count)]


def call(kernel, outs, name, scratch=(), specs=None, out_specs=None, aliases={}, cost=COST):
    def run(*args):
        return pl.pallas_call(
            kernel,
            out_shape=outs,
            in_specs=specs or [VMEM] * len(args),
            out_specs=out_specs or jax.tree.map(lambda _: VMEM, outs),
            scratch_shapes=scratch,
            input_output_aliases=aliases,
            compiler_params=pltpu.CompilerParams(vmem_limit_bytes=VMEM_LIMIT),
            cost_estimate=pl.CostEstimate(flops=100 * cost, bytes_accessed=10 * cost, transcendentals=0),
            name=name,
        )(*args)

    return run


def chunks(nx):
    last = nx // 2
    early, soon = last - 3, last - 4
    first = [list(range(1, early + 1)), [0, *range(early + 1, last + 1)]]
    second = [list(range(1, soon + 1)), [0, *range(soon + 1, last)]]
    return first, second


def planes_of(pairs, shift):
    return [2 * t + shift + k for t in pairs for k in (0, 1)]


def outer_planes(nx):
    return [-1, 0, nx - 1, nx]


def reader(*parts):
    where = {}
    for ref, planes in parts:
        for i, p in enumerate(planes):
            where[p] = (ref, i)

    def read(p):
        ref, i = where[p]
        return ref[i]

    return read


def by_pairs(planes):
    return list(zip(planes[::2], planes[1::2]))


def is_even():
    return lax.rem(lax.axis_index("gx"), 2) == 0


def pack_kernel(a_ref, mu_ref, odd_ref, sems):
    nx = a_ref.shape[0]
    even = is_even()
    copies = [
        pltpu.make_async_copy(a_ref.at[pl.ds(jnp.where(even, 0, nx - 2), 2)], odd_ref.at[pl.ds(0, 2)], sems.at[0]),
        pltpu.make_async_copy(mu_ref.at[pl.ds(jnp.where(even, 0, nx - 1), 1)], odd_ref.at[pl.ds(2, 1)], sems.at[1]),
    ]
    for copy in copies:
        copy.start()
    for copy in copies:
        copy.wait()


def inner_kernel(stage, a_ref, mu_ref, fz_ref, fy_ref, after, g_ref, c_ref, *even_ref):
    ends = []
    for i, p in enumerate(planes_of(chunks(a_ref.shape[0])[0][stage], -1)):
        g = rate(a_ref[p - 1], a_ref[p], a_ref[p + 1], mu_ref[p])
        g_ref[i] = g
        ends.append(a_ref[p] + time_step * g)
    c_ref[...] = analyse(by_pairs(ends), fz_ref, fy_ref)
    if stage == 0:
        nx = a_ref.shape[0]
        even = is_even()
        even_ref[0][0] = jnp.where(even, a_ref[nx - 2], a_ref[0])
        even_ref[0][1] = jnp.where(even, a_ref[nx - 1], a_ref[1])
        even_ref[0][2] = jnp.where(even, mu_ref[nx - 1], mu_ref[0])


def later_part(below, g, above, a, mobility):
    h = time_step
    laplace = neighbours(g) + (below + above) - 5.0 * g
    hg = h * g
    cube = hg * (3.0 * W[1] * a * a + hg * (3.0 * W[2] * a + W[3] * hg))
    return h * (W[0] * g + mobility * (h * W[1] * laplace - cube))


def middle_kernel(a_ref, mu_ref, fz_ref, fy_ref, after, g_ref, c_ref, *own_refs):
    nx = a_ref.shape[0]
    first = chunks(nx)[0]
    ends = []
    for i, p in enumerate(planes_of(first[-1][1:-1], -1)):
        g = rate(a_ref[p - 1], a_ref[p], a_ref[p + 1], mu_ref[p])
        g_ref[i] = g
        ends.append(a_ref[p] + time_step * g)
    inner = sum(first[:-1], []) + first[-1][1:-1]
    coeffs = analyse(by_pairs(ends) + [(a_ref[p - 1], a_ref[p]) for p in planes_of(inner, -1)[1::2]], fz_ref, fy_ref)
    start = 0
    for ref in (c_ref, *own_refs):
        ref[...] = coeffs[:, start : start + ref.shape[1]]
        start += ref.shape[1]


def ends_between(c_ref, outer, rest_ref):
    width = 2 * KZ
    c_ref[:, :width] = outer[:, :width]
    c_ref[:, width : c_ref.shape[1] - width] = rest_ref[...]
    c_ref[:, c_ref.shape[1] - width :] = outer[:, width:]


def mark_kernel(from_odd, after, out_ref):
    out_ref[...] = jnp.zeros_like(out_ref)


def outer_kernel(a_ref, mu_ref, even_ref, odd_ref, rest_ref, fz_ref, fy_ref, after, a_out, g_out, c_ref):
    nx = a_ref.shape[0]
    even = is_even()
    place = lax.axis_index("gx")
    count = lax.axis_size("gx")
    keep_low = (place > 0).astype(F32)
    keep_high = (place < count - 1).astype(F32)
    low = [jnp.where(even, odd_ref[i], even_ref[i]) * keep_low for i in range(3)]
    high = [jnp.where(even, even_ref[i], odd_ref[i]) * keep_high for i in range(3)]
    starts = [low[0], low[1], a_ref[0], a_ref[1]]
    ends = [a_ref[nx - 2], a_ref[nx - 1], high[0], high[1]]
    values = starts[1:3] + ends[1:3]
    rates = [
        rate(starts[0], starts[1], starts[2], low[2]),
        rate(starts[1], starts[2], starts[3], mu_ref[0]),
        rate(ends[0], ends[1], ends[2], mu_ref[nx - 1]),
        rate(ends[1], ends[2], ends[3], high[2]),
    ]
    for i in range(4):
        a_out[i] = values[i]
        g_out[i] = rates[i]
    outer = [v + time_step * g for v, g in zip(values, rates)]
    ends_between(c_ref, analyse(by_pairs(outer), fz_ref, fy_ref), rest_ref)


def later_kernel(a_ref, mu_ref, ab_ref, gb_ref, rest_ref, fz_ref, fy_ref, *refs):
    g_refs, (acc_ref, c_ref, cacc_ref) = refs[:-3], refs[-3:]
    nx = a_ref.shape[0]
    first = chunks(nx)[0]
    inner = [planes_of(part, -1) for part in (*first[:-1], first[-1][1:-1])]
    rates = reader((gb_ref, outer_planes(nx)), *zip(g_refs, inner))
    ends_between(c_ref, analyse([(ab_ref[0], ab_ref[1]), (ab_ref[2], ab_ref[3])], fz_ref, fy_ref), rest_ref)
    for p in range(nx):
        acc_ref[p] = later_part(rates(p - 1), rates(p), rates(p + 1), a_ref[p], mu_ref[p])
    planes = planes_of(chunks(nx)[1][-1], 0)
    cacc_ref[...] = analyse(by_pairs([acc_ref[p] for p in planes]), fz_ref, fy_ref)


def received(c, own):
    return jnp.where(lax.axis_index("tm") > 0, c - own, 0.0)


def second_kernel(stage, *refs):
    a_ref, ab_ref, mu_ref, acc_ref, c1_ref, own_ref, fz_ref, fy_ref, by_ref, bz_ref = refs[:10]
    earlier, (a1_ref, e_ref, c2_ref) = refs[10:-3], refs[-3:]
    if stage == 1:
        earlier, (cacc_ref, c1_first_ref, own_first_ref) = earlier[:1], earlier[1:]
    nx, ny, nz = mu_ref.shape
    first, second = chunks(nx)
    before = reader((a_ref, range(nx)), (ab_ref, outer_planes(nx)))
    receives = lax.axis_index("tm") > 0

    @pl.when(receives)
    def _():
        change = synthesise(c1_ref[...] - own_ref[...], by_ref, bz_ref)
        for i, p in enumerate(planes_of(first[stage], -1)):
            a1_ref[i] = before(p) + change[i // 2][:, (i % 2) * nz : (i % 2 + 1) * nz]

    @pl.when(jnp.logical_not(receives))
    def _():
        for i, p in enumerate(planes_of(first[stage], -1)):
            a1_ref[i] = before(p)

    values = reader(*[(ref, planes_of(part, -1)) for ref, part in zip((*earlier, a1_ref), first)])
    planes = planes_of(second[stage], 0)
    fresh = [rate(values(p - 1), values(p), values(p + 1), mu_ref[p]) for p in planes]
    weight = time_step * LAST_ROW[0]
    ends = [values(p) + weight * f + acc_ref[p] for p, f in zip(planes, fresh)]
    for i, e in enumerate(ends):
        e_ref[i] = e
    if stage == 0:
        c2_ref[...] = analyse(by_pairs(ends), fz_ref, fy_ref)
        return
    where = {}
    for c, own, part in ((c1_first_ref, own_first_ref, first[0]), (c1_ref, own_ref, first[1])):
        own_start = jnp.where(receives, c[...], own[...])
        for i, p in enumerate(planes_of(part, -1)):
            where[p] = own_start[:, i * KZ : (i + 1) * KZ]
    known = jnp.concatenate([where[p] for p in planes], axis=1) + cacc_ref[...]
    c2_ref[...] = known + weight * analyse_small(by_pairs(fresh), fz_ref, fy_ref)


def last_kernel(stage, count, *refs):
    c2_ref, by_ref, bz_ref, a_ref = refs[:4]
    before_ref, a1_refs = refs[4], refs[5 : 5 + count]
    out_ref, buffer, sems = refs[-3:]
    nx, ny, nz = out_ref.shape[1:]
    first, second = chunks(nx)
    receives = lax.axis_index("tm") > 0

    @pl.when(receives)
    def _():
        values = reader(*[(ref, planes_of(part, -1)) for ref, part in zip(a1_refs, first)])
        planes = planes_of(second[stage], 0)
        change = synthesise(c2_ref[...] - before_ref[...], by_ref, bz_ref)
        copies = []
        for i in range(0, len(planes), 2):
            for k in (0, 1):
                buffer[i + k] = values(planes[i + k]) + change[i // 2][:, k * nz : (k + 1) * nz]
            copy = pltpu.make_async_copy(
                buffer.at[pl.ds(i, 2)], out_ref.at[0, pl.ds(planes[i], 2)], sems.at[i // 2]
            )
            copy.start()
            copies.append(copy)
        for copy in copies:
            copy.wait()

    if stage == 0:

        @pl.when(jnp.logical_not(receives))
        def _():
            half = nx // 2
            copies = [
                pltpu.make_async_copy(a_ref.at[pl.ds(i * half, half)], out_ref.at[0, pl.ds(i * half, half)], sems.at[i])
                for i in range(2)
            ]
            for copy in copies:
                copy.start()
            for copy in copies:
                copy.wait()


def join_kernel(count, *refs):
    parts, c1_refs = refs[:count], refs[count : 2 * count]
    out_ref, before_refs, sems = refs[2 * count], refs[2 * count + 1 : -1], refs[-1]
    first, second = chunks(out_ref.shape[1])
    copies = []
    for ref, part in zip(parts, second):
        for i, p in enumerate(planes_of(part, 0)[::2]):
            copies.append(
                pltpu.make_async_copy(ref.at[pl.ds(2 * i, 2)], out_ref.at[0, pl.ds(p, 2)], sems.at[len(copies)])
            )
    for copy in copies:
        copy.start()
    columns = {}
    for ref, part in zip(c1_refs, first):
        for i, p in enumerate(planes_of(part, -1)):
            columns[p] = ref[:, i * KZ : (i + 1) * KZ]
    for ref, part in zip(before_refs, second):
        ref[...] = jnp.concatenate([columns[p] for p in planes_of(part, 0)], axis=1)
    for copy in copies:
        copy.wait()


def body(start_states, mobility):
    nx, ny, nz = mobility.shape
    slices, slabs = lax.axis_size("tm"), lax.axis_size("gx")
    a, mu = start_states[0], mobility
    fz, fy, by, bz = map(jnp.asarray, tables(ny, nz))
    first, second = chunks(nx)
    count = len(first)

    def grid(planes):
        return jax.ShapeDtypeStruct((planes, ny, nz), F32)

    def modes(pairs):
        return jax.ShapeDtypeStruct((KY, len(pairs) * 2 * KZ), F32)

    even_pairs = [(s * slabs + g, s * slabs + (g ^ 1)) for s in range(slices) for g in range(slabs)]
    odd_pairs = []
    for s in range(slices):
        for g in range(slabs):
            other = g + 1 if g % 2 else g - 1
            if 0 <= other < slabs:
                odd_pairs.append((s * slabs + g, s * slabs + other))
            else:
                odd_pairs.append((s * slabs + g, (s ^ (1 if g else 2)) * slabs + g))
    ring = [(s, (s + 1) % slices) for s in range(slices)]

    def onward(c):
        return lax.ppermute(c, "tm", ring)

    to_odd = call(pack_kernel, grid(3), "pack", scratch=[pltpu.SemaphoreType.DMA((2,))], specs=[ANY] * 2)(
        *[pltpu.with_memory_space_constraint(x, pltpu.HBM) for x in (a, mu)]
    )
    from_odd = lax.ppermute(to_odd, ("tm", "gx"), odd_pairs)
    g, c1 = [], []
    for stage, part in enumerate(first[:-1]):
        rates, c, *to_even = call(
            functools.partial(inner_kernel, stage),
            [grid(2 * len(part)), modes(part)] + [grid(3)] * (stage == 0),
            "inner",
            specs=[VMEM] * 4 + [ANY],
        )(a, mu, fz, fy, to_odd)
        g.append(rates)
        c1.append(onward(c))
        if stage == 0:
            from_even = lax.ppermute(to_even[0], ("tm", "gx"), even_pairs)
    rest = first[-1][1:-1]
    g_rest, c_rest, *own, own_rest = call(
        middle_kernel,
        [grid(2 * len(rest)), modes(rest), *[modes(part) for part in first[:-1]], modes(rest)],
        "middle",
        specs=[VMEM] * 4 + [ANY],
        cost=0,
    )(a, mu, fz, fy, g[-1])
    mark = call(mark_kernel, jax.ShapeDtypeStruct((8, 128), F32), "mark", specs=[ANY, ANY])(from_odd, own_rest)
    ab, gb, c = call(outer_kernel, [grid(4), grid(4), modes(first[-1])], "outer", specs=[VMEM] * 7 + [ANY])(
        a, mu, from_even, from_odd, c_rest, fz, fy, mark
    )
    c1.append(onward(c))
    acc, own_last, cacc = call(later_kernel, [grid(nx), modes(first[-1]), modes(second[-1])], "later")(
        a, mu, ab, gb, own_rest, fz, fy, *g, g_rest
    )
    own.append(own_last)
    a1, e, c2 = [], [], []
    for stage in range(count):
        values, end, c = call(
            functools.partial(second_kernel, stage),
            [grid(2 * len(first[stage])), grid(2 * len(second[stage])), modes(second[stage])],
            "second",
        )(a, ab, mu, acc, c1[stage], own[stage], fz, fy, by, bz, *a1, *([cacc, c1[0], own[0]] if stage else []))
        a1.append(values)
        e.append(end)
        c2.append(onward(c))
    whole = jax.ShapeDtypeStruct((1, nx, ny, nz), F32)
    end_state, *before = call(
        functools.partial(join_kernel, count),
        [whole, *[modes(part) for part in second]],
        "join",
        scratch=[pltpu.SemaphoreType.DMA((nx // 2,))],
        specs=[ANY] * count + [VMEM] * count,
        out_specs=[ANY] + [VMEM] * count,
    )(*e, *c1)
    result = []
    for stage, part in enumerate(second):
        result = [
            call(
                functools.partial(last_kernel, stage, count),
                whole,
                "last",
                scratch=[pltpu.VMEM((2 * len(part), ny, nz), F32), pltpu.SemaphoreType.DMA((len(part),))],
                specs=[VMEM] * (5 + count) + [ANY] * len(result),
                out_specs=ANY,
                aliases={5 + count: 0} if result else {},
            )(c2[stage], by, bz, a, before[stage], *a1, *result)
        ]
    return end_state, result[0]


def solution(mesh):
    placed = (P("tm", "gx", None, None), P("gx", None, None))
    return jax.shard_map(
        body,
        mesh=mesh,
        in_specs=placed,
        out_specs=(P("tm", "gx", None, None), P("tm", "gx", None, None)),
        check_vma=False,
    )
```

```python
import functools
import math

import jax
import jax.numpy as jnp
import numpy as np
from jax import lax
from jax.experimental import pallas as pl
from jax.experimental.pallas import tpu as pltpu
from jax.sharding import PartitionSpec as P

KY = 64
KZ = 64
time_step = 0.05
F32 = jnp.float32
BF16 = jnp.bfloat16
VMEM_LIMIT = 24 * 2**20
COST = 10**8
ANY = pl.BlockSpec(memory_space=pl.ANY)
VMEM = pl.BlockSpec(memory_space=pltpu.VMEM)


def basis_value(node_times, source, point):
    total = 1.0
    for other in range(5):
        if other != source:
            total = total * (point - node_times[other]) / (node_times[source] - node_times[other])
    return total


def lobatto():
    root = math.sqrt(3.0 / 7.0)
    node_times = [0.0, (1.0 - root) / 2.0, 0.5, (1.0 + root) / 2.0, 1.0]
    gauss_points = [-math.sqrt(0.6), 0.0, math.sqrt(0.6)]
    gauss_weights = [5.0 / 9.0, 8.0 / 9.0, 5.0 / 9.0]
    last_row = []
    for source in range(5):
        integral = 0.0
        for point, weight in zip(gauss_points, gauss_weights):
            integral += 0.5 * weight * basis_value(node_times, source, 0.5 * (1.0 + point))
        last_row.append(integral)
    return node_times, last_row


NODE_TIMES, LAST_ROW = lobatto()
W = [sum(LAST_ROW[j] * NODE_TIMES[j] ** k for j in range(1, 5)) for k in range(4)]


def dct_rows(count, kept):
    freq = np.arange(kept, dtype=np.float64)[:, None]
    place = np.arange(count, dtype=np.float64)[None, :]
    matrix = np.cos(np.pi * (place + 0.5) * freq / count) * np.sqrt(2.0 / count)
    return np.where(freq == 0, matrix * np.sqrt(0.5), matrix)


def halves(matrix):
    high = matrix.astype(jnp.bfloat16)
    low = (matrix - high.astype(np.float64)).astype(jnp.bfloat16)
    return high, low


def tables(ny, nz):
    cy = dct_rows(ny, KY)
    cz = dct_rows(nz, KZ)
    twice = np.zeros((2 * nz, 2 * KZ))
    twice[:nz, :KZ] = cz.T
    twice[nz:, KZ:] = cz.T
    zh, zl = halves(twice)
    fz = np.concatenate([zh, zl], axis=1)
    yh, yl = halves(cy)
    fy = np.block([[yh, yh], [yl, np.zeros_like(yl)]])
    by = np.concatenate([yh.T, yh.T, yl.T], axis=1)
    bz = np.concatenate([zh.T, zh.T, zl.T], axis=0)
    return fz, fy, by, bz


def split(x):
    high = x.astype(BF16)
    return high, (x - high.astype(F32)).astype(BF16)


def dot(a, b):
    return jnp.dot(a, b, preferred_element_type=F32)


def neighbours(v):
    ny, nz = v.shape
    rows = lax.broadcasted_iota(jnp.int32, (8, nz), 0)
    lanes = lax.broadcasted_iota(jnp.int32, v.shape, 1)
    low = pltpu.roll(v, 1, 0)
    high = pltpu.roll(v, ny - 1, 0)
    low = jnp.concatenate([jnp.where(rows == 0, 0.0, low[:8]), low[8:]], axis=0)
    high = jnp.concatenate([high[: ny - 8], jnp.where(rows == 7, 0.0, high[ny - 8 :])], axis=0)
    left = jnp.where(lanes == 0, 0.0, pltpu.roll(v, 1, 1))
    right = jnp.where(lanes == nz - 1, 0.0, pltpu.roll(v, nz - 1, 1))
    return (low + high) + (left + right)


def rate(below, v, above, mobility):
    return mobility * (neighbours(v) + (below + above) - v * (5.0 + v * v))


def analyse_small(pairs, fz_ref, fy_ref):
    ny = pairs[0][0].shape[0]
    width = 2 * KZ
    rows = [jnp.concatenate([first.astype(BF16), second.astype(BF16)], axis=1) for first, second in pairs]
    half = dot(jnp.concatenate(rows, axis=0), fz_ref[...])
    half = (half[:, :width] + half[:, width:]).astype(BF16)
    columns = [half[i * ny : (i + 1) * ny] for i in range(len(pairs))]
    coeffs = dot(fy_ref[:, :ny], jnp.concatenate(columns, axis=1))
    return coeffs[:KY] + coeffs[KY:]


def analyse(pairs, fz_ref, fy_ref):
    rows = []
    for first, second in pairs:
        first_high, first_low = split(first)
        second_high, second_low = split(second)
        rows.append(jnp.concatenate([first_high, second_high, first_low, second_low], axis=1))
    rows = jnp.concatenate(rows, axis=0)
    width, nz = 2 * KZ, pairs[0][0].shape[1]
    half = dot(rows[:, : 2 * nz], fz_ref[...])
    half = half[:, :width] + half[:, width:] + dot(rows[:, 2 * nz :], fz_ref[:, :width])
    ny = pairs[0][0].shape[0]
    columns = []
    for i in range(len(pairs)):
        columns.append(jnp.concatenate(split(half[i * ny : (i + 1) * ny]), axis=0))
    coeffs = dot(fy_ref[...], jnp.concatenate(columns, axis=1))
    return coeffs[:KY] + coeffs[KY:]


def synthesise(coeffs, by_ref, bz_ref):
    high, low = split(coeffs)
    half = dot(by_ref[...], jnp.concatenate([high, low, high], axis=0))
    width = 2 * KZ
    count = coeffs.shape[1] // width
    rows = []
    for i in range(count):
        high, low = split(half[:, i * width : (i + 1) * width])
        rows.append(jnp.concatenate([high, low, high], axis=1))
    planes = dot(jnp.concatenate(rows, axis=0), bz_ref[...])
    ny = half.shape[0]
    return [planes[i * ny : (i + 1) * ny] for i in range(count)]


def call(kernel, outs, name, scratch=(), specs=None, out_specs=None, aliases={}, cost=COST):
    def run(*args):
        return pl.pallas_call(
            kernel,
            out_shape=outs,
            in_specs=specs or [VMEM] * len(args),
            out_specs=out_specs or jax.tree.map(lambda _: VMEM, outs),
            scratch_shapes=scratch,
            input_output_aliases=aliases,
            compiler_params=pltpu.CompilerParams(vmem_limit_bytes=VMEM_LIMIT),
            cost_estimate=pl.CostEstimate(flops=100 * cost, bytes_accessed=10 * cost, transcendentals=0),
            name=name,
        )(*args)

    return run


def chunks(nx):
    last = nx // 2
    early, soon = last - 3, last - 4
    first = [list(range(1, early + 1)), [0, *range(early + 1, last + 1)]]
    second = [list(range(1, soon + 1)), [0, *range(soon + 1, last)]]
    return first, second


def planes_of(pairs, shift):
    return [2 * t + shift + k for t in pairs for k in (0, 1)]


def outer_planes(nx):
    return [-1, 0, nx - 1, nx]


def reader(*parts):
    where = {}
    for ref, planes in parts:
        for i, p in enumerate(planes):
            where[p] = (ref, i)

    def read(p):
        ref, i = where[p]
        return ref[i]

    return read


def by_pairs(planes):
    return list(zip(planes[::2], planes[1::2]))


def is_even():
    return lax.rem(lax.axis_index("gx"), 2) == 0


def pack_kernel(a_ref, mu_ref, odd_ref, sems):
    nx = a_ref.shape[0]
    even = is_even()
    copies = [
        pltpu.make_async_copy(a_ref.at[pl.ds(jnp.where(even, 0, nx - 2), 2)], odd_ref.at[pl.ds(0, 2)], sems.at[0]),
        pltpu.make_async_copy(mu_ref.at[pl.ds(jnp.where(even, 0, nx - 1), 1)], odd_ref.at[pl.ds(2, 1)], sems.at[1]),
    ]
    for copy in copies:
        copy.start()
    for copy in copies:
        copy.wait()


def inner_kernel(stage, a_ref, mu_ref, fz_ref, fy_ref, after, g_ref, c_ref, *even_ref):
    ends = []
    for i, p in enumerate(planes_of(chunks(a_ref.shape[0])[0][stage], -1)):
        g = rate(a_ref[p - 1], a_ref[p], a_ref[p + 1], mu_ref[p])
        g_ref[i] = g
        ends.append(a_ref[p] + time_step * g)
    c_ref[...] = analyse(by_pairs(ends), fz_ref, fy_ref)
    if stage == 0:
        nx = a_ref.shape[0]
        even = is_even()
        even_ref[0][0] = jnp.where(even, a_ref[nx - 2], a_ref[0])
        even_ref[0][1] = jnp.where(even, a_ref[nx - 1], a_ref[1])
        even_ref[0][2] = jnp.where(even, mu_ref[nx - 1], mu_ref[0])


def later_part(below, g, above, a, mobility):
    h = time_step
    laplace = neighbours(g) + (below + above) - 5.0 * g
    hg = h * g
    cube = hg * (3.0 * W[1] * a * a + hg * (3.0 * W[2] * a + W[3] * hg))
    return h * (W[0] * g + mobility * (h * W[1] * laplace - cube))


def middle_kernel(a_ref, mu_ref, fz_ref, fy_ref, after, g_ref, c_ref, *own_refs):
    nx = a_ref.shape[0]
    first = chunks(nx)[0]
    ends = []
    for i, p in enumerate(planes_of(first[-1][1:-1], -1)):
        g = rate(a_ref[p - 1], a_ref[p], a_ref[p + 1], mu_ref[p])
        g_ref[i] = g
        ends.append(a_ref[p] + time_step * g)
    inner = sum(first[:-1], []) + first[-1][1:-1]
    coeffs = analyse(by_pairs(ends) + [(a_ref[p - 1], a_ref[p]) for p in planes_of(inner, -1)[1::2]], fz_ref, fy_ref)
    start = 0
    for ref in (c_ref, *own_refs):
        ref[...] = coeffs[:, start : start + ref.shape[1]]
        start += ref.shape[1]


def ends_between(c_ref, outer, rest_ref):
    width = 2 * KZ
    c_ref[:, :width] = outer[:, :width]
    c_ref[:, width : c_ref.shape[1] - width] = rest_ref[...]
    c_ref[:, c_ref.shape[1] - width :] = outer[:, width:]


def mark_kernel(from_odd, after, out_ref):
    out_ref[...] = jnp.zeros_like(out_ref)


def outer_kernel(a_ref, mu_ref, even_ref, odd_ref, rest_ref, fz_ref, fy_ref, after, a_out, g_out, c_ref):
    nx = a_ref.shape[0]
    even = is_even()
    place = lax.axis_index("gx")
    count = lax.axis_size("gx")
    keep_low = (place > 0).astype(F32)
    keep_high = (place < count - 1).astype(F32)
    low = [jnp.where(even, odd_ref[i], even_ref[i]) * keep_low for i in range(3)]
    high = [jnp.where(even, even_ref[i], odd_ref[i]) * keep_high for i in range(3)]
    starts = [low[0], low[1], a_ref[0], a_ref[1]]
    ends = [a_ref[nx - 2], a_ref[nx - 1], high[0], high[1]]
    values = starts[1:3] + ends[1:3]
    rates = [
        rate(starts[0], starts[1], starts[2], low[2]),
        rate(starts[1], starts[2], starts[3], mu_ref[0]),
        rate(ends[0], ends[1], ends[2], mu_ref[nx - 1]),
        rate(ends[1], ends[2], ends[3], high[2]),
    ]
    for i in range(4):
        a_out[i] = values[i]
        g_out[i] = rates[i]
    outer = [v + time_step * g for v, g in zip(values, rates)]
    ends_between(c_ref, analyse(by_pairs(outer), fz_ref, fy_ref), rest_ref)


def later_kernel(a_ref, mu_ref, ab_ref, gb_ref, rest_ref, fz_ref, fy_ref, *refs):
    g_refs, (acc_ref, c_ref, cacc_ref) = refs[:-3], refs[-3:]
    nx = a_ref.shape[0]
    first = chunks(nx)[0]
    inner = [planes_of(part, -1) for part in (*first[:-1], first[-1][1:-1])]
    rates = reader((gb_ref, outer_planes(nx)), *zip(g_refs, inner))
    ends_between(c_ref, analyse([(ab_ref[0], ab_ref[1]), (ab_ref[2], ab_ref[3])], fz_ref, fy_ref), rest_ref)
    for p in range(nx):
        acc_ref[p] = later_part(rates(p - 1), rates(p), rates(p + 1), a_ref[p], mu_ref[p])
    planes = planes_of(chunks(nx)[1][-1], 0)
    cacc_ref[...] = analyse(by_pairs([acc_ref[p] for p in planes]), fz_ref, fy_ref)


def received(c, own):
    return jnp.where(lax.axis_index("tm") > 0, c - own, 0.0)


def second_kernel(stage, *refs):
    a_ref, ab_ref, mu_ref, acc_ref, c1_ref, own_ref, fz_ref, fy_ref, by_ref, bz_ref = refs[:10]
    earlier, (a1_ref, e_ref, c2_ref) = refs[10:-3], refs[-3:]
    if stage == 1:
        earlier, (cacc_ref, c1_first_ref, own_first_ref) = earlier[:1], earlier[1:]
    nx, ny, nz = mu_ref.shape
    first, second = chunks(nx)
    before = reader((a_ref, range(nx)), (ab_ref, outer_planes(nx)))
    receives = lax.axis_index("tm") > 0

    @pl.when(receives)
    def _():
        change = synthesise(c1_ref[...] - own_ref[...], by_ref, bz_ref)
        for i, p in enumerate(planes_of(first[stage], -1)):
            a1_ref[i] = before(p) + change[i // 2][:, (i % 2) * nz : (i % 2 + 1) * nz]

    @pl.when(jnp.logical_not(receives))
    def _():
        for i, p in enumerate(planes_of(first[stage], -1)):
            a1_ref[i] = before(p)

    values = reader(*[(ref, planes_of(part, -1)) for ref, part in zip((*earlier, a1_ref), first)])
    planes = planes_of(second[stage], 0)
    fresh = [rate(values(p - 1), values(p), values(p + 1), mu_ref[p]) for p in planes]
    weight = time_step * LAST_ROW[0]
    ends = [values(p) + weight * f + acc_ref[p] for p, f in zip(planes, fresh)]
    for i, e in enumerate(ends):
        e_ref[i] = e
    if stage == 0:
        c2_ref[...] = analyse(by_pairs(ends), fz_ref, fy_ref)
        return
    where = {}
    for c, own, part in ((c1_first_ref, own_first_ref, first[0]), (c1_ref, own_ref, first[1])):
        own_start = jnp.where(receives, c[...], own[...])
        for i, p in enumerate(planes_of(part, -1)):
            where[p] = own_start[:, i * KZ : (i + 1) * KZ]
    known = jnp.concatenate([where[p] for p in planes], axis=1) + cacc_ref[...]
    c2_ref[...] = known + weight * analyse_small(by_pairs(fresh), fz_ref, fy_ref)


def last_kernel(stage, count, *refs):
    c2_ref, by_ref, bz_ref, a_ref = refs[:4]
    before_ref, a1_refs = refs[4], refs[5 : 5 + count]
    out_ref, buffer, sems = refs[-3:]
    nx, ny, nz = out_ref.shape[1:]
    first, second = chunks(nx)
    receives = lax.axis_index("tm") > 0

    @pl.when(receives)
    def _():
        values = reader(*[(ref, planes_of(part, -1)) for ref, part in zip(a1_refs, first)])
        planes = planes_of(second[stage], 0)
        change = synthesise(c2_ref[...] - before_ref[...], by_ref, bz_ref)
        copies = []
        for i in range(0, len(planes), 2):
            for k in (0, 1):
                buffer[i + k] = values(planes[i + k]) + change[i // 2][:, k * nz : (k + 1) * nz]
            copy = pltpu.make_async_copy(
                buffer.at[pl.ds(i, 2)], out_ref.at[0, pl.ds(planes[i], 2)], sems.at[i // 2]
            )
            copy.start()
            copies.append(copy)
        for copy in copies:
            copy.wait()

    if stage == 0:

        @pl.when(jnp.logical_not(receives))
        def _():
            half = nx // 2
            copies = [
                pltpu.make_async_copy(a_ref.at[pl.ds(i * half, half)], out_ref.at[0, pl.ds(i * half, half)], sems.at[i])
                for i in range(2)
            ]
            for copy in copies:
                copy.start()
            for copy in copies:
                copy.wait()


def join_kernel(count, *refs):
    parts, c1_refs = refs[:count], refs[count : 2 * count]
    out_ref, before_refs, sems = refs[2 * count], refs[2 * count + 1 : -1], refs[-1]
    first, second = chunks(out_ref.shape[1])
    copies = []
    for ref, part in zip(parts, second):
        for i, p in enumerate(planes_of(part, 0)[::2]):
            copies.append(
                pltpu.make_async_copy(ref.at[pl.ds(2 * i, 2)], out_ref.at[0, pl.ds(p, 2)], sems.at[len(copies)])
            )
    for copy in copies:
        copy.start()
    columns = {}
    for ref, part in zip(c1_refs, first):
        for i, p in enumerate(planes_of(part, -1)):
            columns[p] = ref[:, i * KZ : (i + 1) * KZ]
    for ref, part in zip(before_refs, second):
        ref[...] = jnp.concatenate([columns[p] for p in planes_of(part, 0)], axis=1)
    for copy in copies:
        copy.wait()


def body(start_states, mobility):
    nx, ny, nz = mobility.shape
    slices, slabs = lax.axis_size("tm"), lax.axis_size("gx")
    a, mu = start_states[0], mobility
    fz, fy, by, bz = map(jnp.asarray, tables(ny, nz))
    first, second = chunks(nx)
    count = len(first)

    def grid(planes):
        return jax.ShapeDtypeStruct((planes, ny, nz), F32)

    def modes(pairs):
        return jax.ShapeDtypeStruct((KY, len(pairs) * 2 * KZ), F32)

    even_pairs = [(s * slabs + g, s * slabs + (g ^ 1)) for s in range(slices) for g in range(slabs)]
    odd_pairs = []
    for s in range(slices):
        for g in range(slabs):
            other = g + 1 if g % 2 else g - 1
            if 0 <= other < slabs:
                odd_pairs.append((s * slabs + g, s * slabs + other))
            else:
                odd_pairs.append((s * slabs + g, (s ^ 2) * slabs + g))
    ring = [(s, (s + 1) % slices) for s in range(slices)]

    def onward(c):
        return lax.ppermute(c, "tm", ring)

    to_odd = call(pack_kernel, grid(3), "pack", scratch=[pltpu.SemaphoreType.DMA((2,))], specs=[ANY] * 2)(
        *[pltpu.with_memory_space_constraint(x, pltpu.HBM) for x in (a, mu)]
    )
    from_odd = lax.ppermute(to_odd, ("tm", "gx"), odd_pairs)
    g, c1 = [], []
    for stage, part in enumerate(first[:-1]):
        rates, c, *to_even = call(
            functools.partial(inner_kernel, stage),
            [grid(2 * len(part)), modes(part)] + [grid(3)] * (stage == 0),
            "inner",
            specs=[VMEM] * 4 + [ANY],
        )(a, mu, fz, fy, to_odd)
        g.append(rates)
        c1.append(onward(c))
        if stage == 0:
            from_even = lax.ppermute(to_even[0], ("tm", "gx"), even_pairs)
    rest = first[-1][1:-1]
    g_rest, c_rest, *own, own_rest = call(
        middle_kernel,
        [grid(2 * len(rest)), modes(rest), *[modes(part) for part in first[:-1]], modes(rest)],
        "middle",
        specs=[VMEM] * 4 + [ANY],
        cost=0,
    )(a, mu, fz, fy, g[-1])
    mark = call(mark_kernel, jax.ShapeDtypeStruct((8, 128), F32), "mark", specs=[ANY, ANY])(from_odd, own_rest)
    ab, gb, c = call(outer_kernel, [grid(4), grid(4), modes(first[-1])], "outer", specs=[VMEM] * 7 + [ANY])(
        a, mu, from_even, from_odd, c_rest, fz, fy, mark
    )
    c1.append(onward(c))
    acc, own_last, cacc = call(later_kernel, [grid(nx), modes(first[-1]), modes(second[-1])], "later")(
        a, mu, ab, gb, own_rest, fz, fy, *g, g_rest
    )
    own.append(own_last)
    a1, e, c2 = [], [], []
    for stage in range(count):
        values, end, c = call(
            functools.partial(second_kernel, stage),
            [grid(2 * len(first[stage])), grid(2 * len(second[stage])), modes(second[stage])],
            "second",
        )(a, ab, mu, acc, c1[stage], own[stage], fz, fy, by, bz, *a1, *([cacc, c1[0], own[0]] if stage else []))
        a1.append(values)
        e.append(end)
        c2.append(onward(c))
    whole = jax.ShapeDtypeStruct((1, nx, ny, nz), F32)
    end_state, *before = call(
        functools.partial(join_kernel, count),
        [whole, *[modes(part) for part in second]],
        "join",
        scratch=[pltpu.SemaphoreType.DMA((nx // 2,))],
        specs=[ANY] * count + [VMEM] * count,
        out_specs=[ANY] + [VMEM] * count,
    )(*e, *c1)
    result = []
    for stage, part in enumerate(second):
        result = [
            call(
                functools.partial(last_kernel, stage, count),
                whole,
                "last",
                scratch=[pltpu.VMEM((2 * len(part), ny, nz), F32), pltpu.SemaphoreType.DMA((len(part),))],
                specs=[VMEM] * (5 + count) + [ANY] * len(result),
                out_specs=ANY,
                aliases={5 + count: 0} if result else {},
            )(c2[stage], by, bz, a, before[stage], *a1, *result)
        ]
    return end_state, result[0]


def solution(mesh):
    placed = (P("tm", "gx", None, None), P("gx", None, None))
    return jax.shard_map(
        body,
        mesh=mesh,
        in_specs=placed,
        out_specs=(P("tm", "gx", None, None), P("tm", "gx", None, None)),
        check_vma=False,
    )
```
